32 devices in a mesh: sp: 4 (over y, x), fsdp: 8 (over z, core).
Axes of the slice: x: 2, y: 2, z: 4, core: 2. Of those that a mesh axis runs over, the one named last changes fastest.
Arguments:
- tokens: bfloat16 [8, 1536, 2560], P('fsdp', 'sp'), may hold values from -6 to 6
- cotangent: bfloat16 [8, 1536, 2560], P('fsdp', 'sp'), may hold values from -6 to 6
- attn_gain: bfloat16 [2560], P('fsdp'), may hold values from 0.099609375 to 1.8984375
- w_query: bfloat16 [2560, 2560], P('fsdp'), may hold values from -0.25 to 0.25
- key_weight: bfloat16 [2560, 640], P('fsdp'), may hold values from -0.125 to 0.125
- value_weight: bfloat16 [2560, 640], P('fsdp'), may hold values from -0.125 to 0.125
- w_out: bfloat16 [2560, 2560], P('fsdp'), may hold values from -0.5 to 0.5
- mlp_gain: bfloat16 [2560], P('fsdp'), may hold values from 0.099609375 to 1.8984375
- w_gate: bfloat16 [2560, 7168], P('fsdp'), may hold values from -0.125 to 0.125
- w_up: bfloat16 [2560, 7168], P('fsdp'), may hold values from -0.125 to 0.125
- w_down: bfloat16 [7168, 2560], P('fsdp'), may hold values from -0.09375 to 0.09375
- positions: int32 [8, 1536], P('fsdp', 'sp'), may hold values from 0 to 32767
- lengths: int32 [8, 3], P('fsdp'), may hold values from 1 to 1344, 1536 in all within a row
- deal_slots: int32 [8, 4, 8], replicated, may hold values from 0 to 63, as said below
Outputs:
- layer_out: bfloat16 [8, 1536, 2560], P('fsdp', 'sp')
- input_grad: bfloat16 [8, 1536, 2560], P('fsdp', 'sp')
- grad_attn_gain: float32 [2560], P('fsdp')
- grad_query: float32 [2560, 2560], P('fsdp')
- grad_key: float32 [2560, 640], P('fsdp')
- grad_value: float32 [2560, 640], P('fsdp')
- grad_out: float32 [2560, 2560], P('fsdp')
- grad_mlp_gain: float32 [2560], P('fsdp')
- grad_gate: float32 [2560, 7168], P('fsdp')
- grad_up: float32 [2560, 7168], P('fsdp')
- grad_down: float32 [7168, 2560], P('fsdp')
The draws below stay inside these ranges and needn't reach their ends.
Inputs may be any that keep to these rules, and one draw needn't show every extreme that they name: In each group the 3 lengths sum to 1536, and the largest is 1344. For each f and s, deal_slots[f, s, j] // 8 names every group once over j; for each s all 64 entries are different.
All inputs are finite; a program needn't handle non-finite values.
Results may differ from the reference program's by a relative error of at most 0.024.
Values may be sent and summed in bfloat16 or wider, within the bound.
No kernel may reach another device: no remote copies, remote signals or barrier semaphores. Data moves between devices by JAX's collectives and lax.ppermute only.
A program may use at most 768 MiB of HBM per device.

```python
import math
import jax
import jax.numpy as jnp
import numpy as np
from jax import lax

D = 2560
QUERY_HEADS = 32
KEY_VALUE_HEADS = 8
HEAD_SIZE = 80
FF = 7168
SEQ_GRP = 3
POSMAX = 32768
QC = 2560
KC = 640
SEQUENCE_GROUPS = 8
GROUP_TOKENS = 1536
BLK = 48
MOST = 1344
N_SP = 4


def shuffled_rows(key, token_count, width):
    row_keys = jax.random.split(key, token_count)

    def one_row(row_key):
        return jax.random.permutation(row_key, width)
    return jax.vmap(one_row)(row_keys)


def draw_deal_slots(key, part):
    key = jax.random.fold_in(key, 7)
    target = shuffled_rows(jax.random.fold_in(key, 1), SEQUENCE_GROUPS * N_SP, SEQUENCE_GROUPS).reshape(SEQUENCE_GROUPS, N_SP, SEQUENCE_GROUPS)
    slot = shuffled_rows(jax.random.fold_in(key, 2), SEQUENCE_GROUPS * N_SP, SEQUENCE_GROUPS).reshape(SEQUENCE_GROUPS, N_SP, SEQUENCE_GROUPS)
    source = jnp.arange(SEQUENCE_GROUPS)[:, None, None] + jnp.zeros_like(target)
    lane = jnp.arange(N_SP)[None, :, None] + jnp.zeros_like(target)
    place = slot[target, lane, source]
    return (target * SEQUENCE_GROUPS + place).astype(jnp.int32)


def place_ends(values, own_key, low, high):
    longest = values.shape.index(max(values.shape))
    spots = []
    for shift in (0, 1):
        where = [jax.random.randint(jax.random.fold_in(own_key, axis), (), 0, length) for axis, length in enumerate(values.shape)]
        where[longest] = (where[longest] + shift) % values.shape[longest]
        spots.append(tuple(where))
    return values.at[spots[0]].set(low).at[spots[1]].set(high)


def level_of(key, shape, pieces, least, top_value):
    level, own = 1.0, jax.random.fold_in(key, 6)
    for axis_at, blocks in pieces:
        steps = jnp.exp(jax.random.uniform(jax.random.fold_in(own, axis_at), (blocks,), jnp.float32, least / len(pieces), top_value / len(pieces)))
        level = level * jnp.repeat(steps, shape[axis_at] // blocks).reshape([-1 if axis == axis_at else 1 for axis in range(len(shape))])
    return level


def length_profile(count, total, most, slope):
    weights = [(1 << 20) // math.isqrt(rank ** slope) + 1 for rank in range(2, count + 1)]
    spare, given = total - most - (count - 1), [1] * (count - 1)
    while spare > 0:
        free = [i for i in range(count - 1) if given[i] < most]
        mass, budget = sum([weights[i] for i in free]), spare
        for i in free:
            more = min(most - given[i], max(1, budget * weights[i] // mass), spare)
            given[i] = given[i] + more
            spare = spare - more
    return np.array([most] + given)


def uneven(key, amount, total, reach, skew):
    if amount == 2:
        one = jax.random.randint(key, (), max(1, total - reach), min(reach, total - 1) + 1)
        return jnp.stack([one, total - one])
    sizes = jnp.asarray(length_profile(amount, total, reach, skew), jnp.int32)
    couples = (amount - 1) // 2
    source_of, sink = sizes[1:1 + 2 * couples:2], sizes[2:2 + 2 * couples:2]
    slack = jnp.minimum(source_of - 1, reach - sink)
    shifted = jax.random.randint(jax.random.fold_in(key, 1), (couples,), 0, 1 << 20) % (slack + 1)
    sizes = sizes.at[1:1 + 2 * couples:2].set(source_of - shifted).at[2:2 + 2 * couples:2].set(sink + shifted)
    return sizes[jax.random.permutation(jax.random.fold_in(key, 2), amount)]


def normal_values(stream_key, shape, deviation, limit, cuts=(), held_as=jnp.bfloat16):
    drawn = deviation * jax.random.normal(stream_key, shape, jnp.float32)
    if cuts:
        drawn = drawn * level_of(stream_key, shape, cuts, -0.22, 0.18)
    return jnp.clip(drawn, -limit, limit).astype(held_as)


def setup_inputs(seed: int = 0) -> dict:
    streams_of = jax.random.split(jax.random.key(seed), 15)
    return {
        "tokens": normal_values(streams_of[0], (SEQUENCE_GROUPS, GROUP_TOKENS, D), 1.0, 6.0, ((0, 8), (1, 4))),
        "cotangent": normal_values(streams_of[1], (SEQUENCE_GROUPS, GROUP_TOKENS, D), 1.0, 6.0, ((0, 8), (1, 4))),
        "attn_gain": jnp.clip(1.0 + 0.18 * jax.random.normal(streams_of[2], (D,), jnp.float32), 0.099609375, 1.8984375).astype(jnp.bfloat16),
        "w_query": normal_values(streams_of[3], (D, QC), (D // 4) ** -0.5, 0.25, ((0, 8),)),
        "key_weight": normal_values(streams_of[4], (D, KC), D ** -0.5, 0.125, ((0, 8),)),
        "value_weight": normal_values(streams_of[5], (D, KC), D ** -0.5, 0.125, ((0, 8),)),
        "w_out": normal_values(streams_of[6], (QC, D), (QC // 16) ** -0.5, 0.5, ((0, 8),)),
        "mlp_gain": jnp.clip(1.0 + 0.18 * jax.random.normal(streams_of[7], (D,), jnp.float32), 0.099609375, 1.8984375).astype(jnp.bfloat16),
        "w_gate": normal_values(streams_of[8], (D, FF), D ** -0.5, 0.125, ((0, 8),)),
        "w_up": normal_values(streams_of[9], (D, FF), D ** -0.5, 0.125, ((0, 8),)),
        "w_down": normal_values(streams_of[10], (FF, D), (FF // 2) ** -0.5, 0.09375, ((0, 8),)),
        "positions": place_ends(jax.random.randint(streams_of[11], (SEQUENCE_GROUPS, GROUP_TOKENS), 0, POSMAX), jax.random.fold_in(streams_of[11], 1), 0, POSMAX - 1).astype(jnp.int32),
        "lengths": jax.vmap(lambda own: uneven(own, SEQ_GRP, GROUP_TOKENS, MOST, 2))(jax.random.split(streams_of[12], SEQUENCE_GROUPS)).reshape((SEQUENCE_GROUPS, SEQ_GRP)).astype(jnp.int32),
        "deal_slots": draw_deal_slots(jax.random.fold_in(streams_of[14], 71), 0),
    }


eps = 1e-05
theta = 1000000.0
masked_score = -1e+30

@jax.custom_vjp
def reduced_precision(v):
    return lax.optimization_barrier(v.astype(jnp.bfloat16)).astype(jnp.float32)

@jax.custom_vjp
def reduced_precision_back(v):
    return v

def low_keep(v):
    return (reduced_precision(v), None)

def low_pass(kept, grad):
    return (grad,)

def back_keep(v):
    return (v, None)

def back_low(kept, grad):
    return (reduced_precision(grad),)
reduced_precision.defvjp(low_keep, low_pass)
reduced_precision_back.defvjp(back_keep, back_low)

def matrix_product(left, right):
    return jnp.dot(left, right, precision=lax.Precision.HIGHEST)

def rms_scale(value_matrix, gains):
    return value_matrix * lax.rsqrt(lax.optimization_barrier(jnp.mean(value_matrix * value_matrix, axis=-1, keepdims=True)) + eps) * gains

def rotary_tables(positions, head):
    halves = head // 2
    frequency = theta ** (-(2.0 * jnp.arange(halves, dtype=jnp.float32)) / head)
    angles = positions.astype(jnp.float32)[:, None] * frequency[None, :]
    cosine = jnp.concatenate([jnp.cos(angles), jnp.cos(angles)], axis=1)
    sine = jnp.concatenate([jnp.sin(angles), jnp.sin(angles)], axis=1)
    return (cosine, sine)

def rotate(value_matrix, cosine, sine):
    halves = value_matrix.shape[-1] // 2
    turned = jnp.concatenate([-value_matrix[..., halves:], value_matrix[..., :halves]], axis=-1)
    return value_matrix * cosine[:, None, :] + turned * sine[:, None, :]

def attention_per_group(parts):
    query_matrix, key_matrix, value_matrix, lengths = parts
    total_tokens = query_matrix.shape[0]
    ends = jnp.cumsum(lengths).astype(jnp.int32)
    places = jnp.arange(total_tokens, dtype=jnp.int32)
    segment = lax.optimization_barrier(jnp.sum((places[:, None] >= ends[None, :]).astype(jnp.int32), axis=1)).astype(jnp.int32)
    allowed = (segment[:, None] == segment[None, :]) & (places[None, :] <= places[:, None])
    grouped_rows = query_matrix.reshape(total_tokens, KEY_VALUE_HEADS, QUERY_HEADS // KEY_VALUE_HEADS, HEAD_SIZE)
    scores = jnp.einsum('qkgd,skd->kgqs', grouped_rows, key_matrix, precision=lax.Precision.HIGHEST) * HEAD_SIZE ** (-0.5)
    scores = reduced_precision_back(scores)
    scores = jnp.where(allowed[None, None], scores, masked_score)
    top = lax.optimization_barrier(jnp.max(scores, axis=-1, keepdims=True))
    weights = jnp.exp(scores - top)
    probs = weights / lax.optimization_barrier(jnp.sum(weights, axis=-1, keepdims=True))
    mixed_heads = jnp.einsum('kgqs,skd->qkgd', reduced_precision(probs), value_matrix, precision=lax.Precision.HIGHEST)
    return mixed_heads.reshape(total_tokens, QUERY_HEADS * HEAD_SIZE)

def layer(inputs, attn_gain, w_query, key_weight, value_weight, w_out, mlp_gain, w_gate, w_up, w_down, positions, lengths):
    token_count = inputs.shape[0]
    normed_input = reduced_precision(rms_scale(inputs, attn_gain))
    cosine, sine = rotary_tables(positions.reshape(-1), HEAD_SIZE)
    query_matrix = reduced_precision_back(matrix_product(normed_input, w_query)).reshape(token_count, QUERY_HEADS, HEAD_SIZE)
    query_matrix = reduced_precision(reduced_precision_back(rotate(query_matrix, cosine, sine)))
    key_matrix = reduced_precision_back(matrix_product(normed_input, key_weight)).reshape(token_count, KEY_VALUE_HEADS, HEAD_SIZE)
    key_matrix = reduced_precision(reduced_precision_back(rotate(key_matrix, cosine, sine)))
    value_matrix = reduced_precision(reduced_precision_back(matrix_product(normed_input, value_weight))).reshape(token_count, KEY_VALUE_HEADS, HEAD_SIZE)
    mixed_heads = lax.map(jax.checkpoint(attention_per_group), (query_matrix.reshape(SEQUENCE_GROUPS, GROUP_TOKENS, QUERY_HEADS, HEAD_SIZE), key_matrix.reshape(SEQUENCE_GROUPS, GROUP_TOKENS, KEY_VALUE_HEADS, HEAD_SIZE), value_matrix.reshape(SEQUENCE_GROUPS, GROUP_TOKENS, KEY_VALUE_HEADS, HEAD_SIZE), lengths))
    mixed_heads = reduced_precision(reduced_precision_back(mixed_heads.reshape(token_count, QUERY_HEADS * HEAD_SIZE)))
    hidden_one = inputs + reduced_precision_back(matrix_product(mixed_heads, w_out))
    normed_two = reduced_precision(rms_scale(hidden_one, mlp_gain))
    gate = reduced_precision_back(matrix_product(normed_two, w_gate))
    upward = reduced_precision_back(matrix_product(normed_two, w_up))
    active = reduced_precision(jax.nn.silu(gate) * upward)
    return hidden_one + reduced_precision_back(matrix_product(active, w_down))

def owner_places(deal_slots):
    target = deal_slots // SEQUENCE_GROUPS
    slot = deal_slots % SEQUENCE_GROUPS
    lane = jnp.arange(N_SP, dtype=jnp.int32)[None, :, None]
    return ((target * N_SP + lane) * SEQUENCE_GROUPS + slot).reshape(-1).astype(jnp.int32)

def to_owner(given, places):
    blocks = given.reshape(-1, BLK, D)
    owner = jnp.zeros_like(blocks).at[places].set(blocks)
    return owner.reshape(-1, D)

def to_given(owner, places):
    return owner.reshape(-1, BLK, D)[places].reshape(SEQUENCE_GROUPS, GROUP_TOKENS, D)

def reference(tokens, cotangent, attn_gain, w_query, key_weight, value_weight, w_out, mlp_gain, w_gate, w_up, w_down, positions, lengths, deal_slots):
    places = owner_places(deal_slots)
    inputs = to_owner(tokens.astype(jnp.float32), places)
    incoming = to_owner(cotangent.astype(jnp.float32), places)

    def forward(value_matrix, gain_one, query_w, key_w, value_w, out_w, gain_two, gate_w, up_w, down_w):
        return layer(value_matrix, gain_one, query_w, key_w, value_w, out_w, gain_two, gate_w, up_w, down_w, positions, lengths)
    result, pullback = jax.vjp(forward, inputs, attn_gain.astype(jnp.float32), w_query.astype(jnp.float32), key_weight.astype(jnp.float32), value_weight.astype(jnp.float32), w_out.astype(jnp.float32), mlp_gain.astype(jnp.float32), w_gate.astype(jnp.float32), w_up.astype(jnp.float32), w_down.astype(jnp.float32))
    grads = pullback(incoming)
    layer_out = to_given(result, places).astype(jnp.bfloat16)
    input_grad = to_given(grads[0], places).astype(jnp.bfloat16)
    return (layer_out, input_grad, grads[1], grads[2], grads[3], grads[4], grads[5], grads[6], grads[7], grads[8], grads[9])
```

```python
import jax
import jax.numpy as jnp
from jax import lax
from jax.experimental.layout import Layout, with_layout_constraint
from jax.sharding import PartitionSpec as P

QUERY_HEADS = 32
KEY_VALUE_HEADS = 8
HEAD_SIZE = 80


eps = 1e-05
theta = 1000000.0
masked_score = -1e30
block_rows = 512


def swap(value, bit):
    size = lax.axis_size("sp")
    return lax.ppermute(value, "sp", [(i, i ^ bit) for i in range(size)])


def row_major(value):
    return with_layout_constraint(value, Layout(major_to_minor=tuple(range(value.ndim))))


def gather_sp(value):
    size = lax.axis_size("sp")
    if size != 4:
        return lax.all_gather(value, "sp", axis=0, tiled=False)
    place = lax.axis_index("sp")
    half = value.shape[0] // 2
    first, second = value[:half], value[half:]
    x_first, y_second = swap(first, 1), swap(second, 2)
    x_second, y_first = swap(second, 1), swap(first, 2)
    far_first, far_second = swap(x_first, 2), swap(y_second, 1)
    out = jnp.zeros((size,) + value.shape, value.dtype)
    zeros = (0,) * (value.ndim - 1)
    for turn, low, high in (
        (0, first, second),
        (1, x_first, x_second),
        (2, y_first, y_second),
        (3, far_first, far_second),
    ):
        out = lax.dynamic_update_slice(out, low[None], (place ^ turn, 0) + zeros)
        out = lax.dynamic_update_slice(out, high[None], (place ^ turn, half) + zeros)
    return row_major(out)


def scatter_sp(parts):
    size = lax.axis_size("sp")
    if size != 4:
        return lax.psum_scatter(
            parts, "sp", scatter_dimension=0, tiled=False
        ).astype(jnp.float32)
    place = lax.axis_index("sp")
    half = parts.shape[1] // 2
    parts = row_major(parts)

    def block(turn, lower):
        start = (place ^ turn, 0 if lower else half) + (0,) * (parts.ndim - 2)
        return lax.dynamic_slice(parts, start, (1, half) + parts.shape[2:])[0]

    wide = jnp.float32
    low = parts.dtype
    from_x, from_y = swap(block(3, True), 1), swap(block(3, False), 2)
    x_first, y_second = swap(block(1, True), 1), swap(block(2, False), 2)
    y_first = swap((block(2, True).astype(wide) + from_x.astype(wide)).astype(low), 2)
    x_second = swap((block(1, False).astype(wide) + from_y.astype(wide)).astype(low), 1)
    first = block(0, True).astype(wide) + x_first.astype(wide) + y_first.astype(wide)
    second = block(0, False).astype(wide) + x_second.astype(wide) + y_second.astype(wide)
    return jnp.concatenate([first, second], axis=0)


def rotary_tables(positions, head):
    halves = head // 2
    frequency = theta ** (-(2.0 * jnp.arange(halves, dtype=jnp.float32)) / head)
    angles = positions.astype(jnp.float32)[:, None] * frequency[None, :]
    cosine = jnp.concatenate([jnp.cos(angles), jnp.cos(angles)], axis=1)
    sine = jnp.concatenate([jnp.sin(angles), jnp.sin(angles)], axis=1)
    return (cosine, sine)


def rotate(value_matrix, cosine, sine):
    halves = value_matrix.shape[-1] // 2
    turned = jnp.concatenate([-value_matrix[..., halves:], value_matrix[..., :halves]], axis=-1)
    return value_matrix * cosine[:, None, :] + turned * sine[:, None, :]


def rotate_back(grads, cosine, sine):
    halves = grads.shape[-1] // 2
    scaled = grads * sine[:, None, :]
    turned = jnp.concatenate([scaled[..., halves:], -scaled[..., :halves]], axis=-1)
    return grads * cosine[:, None, :] + turned


def gated(gate, upward):
    return jax.nn.silu(gate) * upward


def allowed_mask(segment, row_first, token_count, row_stop):
    query_segment = segment[row_first : row_first + token_count]
    places = jnp.arange(row_stop, dtype=jnp.int32)
    own_places = places[row_first : row_first + token_count]
    return (query_segment[:, None] == segment[None, :row_stop]) & (
        places[None, :] <= own_places[:, None]
    )


def block_scores(query_rows, key_rows, allowed):
    scores = jnp.einsum(
        "qkgd,skd->kgqs", query_rows, key_rows, preferred_element_type=jnp.float32
    ) * HEAD_SIZE ** (-0.5)
    return jnp.where(allowed[None, None], scores, masked_score)


def attention(query_low, key_low, value_low, segment):
    total_tokens = query_low.shape[0]
    kv_heads = key_low.shape[1] // HEAD_SIZE
    grouped_query = query_low.reshape(total_tokens, kv_heads, -1, HEAD_SIZE)
    grouped_key = key_low.reshape(total_tokens, kv_heads, HEAD_SIZE)
    grouped_value = value_low.reshape(total_tokens, kv_heads, HEAD_SIZE)
    span = min(block_rows, total_tokens)
    pieces = []
    totals = []
    for block_index in range(total_tokens // span):
        row_first = block_index * span
        row_stop = row_first + span
        allowed = allowed_mask(segment, row_first, span, row_stop)
        scores = block_scores(grouped_query[row_first:row_stop], grouped_key[:row_stop], allowed)
        top = jnp.max(scores, axis=-1, keepdims=True)
        weights = jnp.exp(scores - top)
        summed = jnp.sum(weights, axis=-1, keepdims=True)
        probs = (weights / summed).astype(jnp.bfloat16)
        mixed_heads = jnp.einsum(
            "kgqs,skd->qkgd", probs, grouped_value[:row_stop], preferred_element_type=jnp.float32
        )
        pieces.append(mixed_heads.reshape(span, -1))
        totals.append(top + jnp.log(summed))
    return jnp.concatenate(pieces, axis=0).astype(jnp.bfloat16), totals


def attention_back(query_low, key_low, value_low, segment, totals, d_mixed):
    total_tokens = query_low.shape[0]
    kv_heads = key_low.shape[1] // HEAD_SIZE
    grouped_query = query_low.reshape(total_tokens, kv_heads, -1, HEAD_SIZE)
    grouped_key = key_low.reshape(total_tokens, kv_heads, HEAD_SIZE)
    grouped_value = value_low.reshape(total_tokens, kv_heads, HEAD_SIZE)
    grouped_grad = d_mixed.reshape(total_tokens, kv_heads, -1, HEAD_SIZE)
    span = min(block_rows, total_tokens)
    query_grads = []
    key_grad = jnp.zeros((total_tokens, kv_heads, HEAD_SIZE), jnp.float32)
    value_grad = jnp.zeros((total_tokens, kv_heads, HEAD_SIZE), jnp.float32)
    for block_index in range(total_tokens // span):
        row_first = block_index * span
        row_stop = row_first + span
        allowed = allowed_mask(segment, row_first, span, row_stop)
        scores = block_scores(grouped_query[row_first:row_stop], grouped_key[:row_stop], allowed)
        probs = jnp.exp(scores - totals[block_index])
        grad_rows = grouped_grad[row_first:row_stop]
        value_grad = value_grad.at[:row_stop].add(
            jnp.einsum(
                "kgqs,qkgd->skd",
                probs.astype(jnp.bfloat16),
                grad_rows,
                preferred_element_type=jnp.float32,
            )
        )
        d_probs = jnp.einsum(
            "qkgd,skd->kgqs",
            grad_rows,
            grouped_value[:row_stop],
            preferred_element_type=jnp.float32,
        )
        delta = jnp.sum(probs * d_probs, axis=-1, keepdims=True)
        d_scores = (probs * (d_probs - delta)).astype(jnp.bfloat16)
        query_part = jnp.einsum(
            "kgqs,skd->qkgd", d_scores, grouped_key[:row_stop], preferred_element_type=jnp.float32
        )
        query_grads.append((query_part * HEAD_SIZE ** (-0.5)).reshape(span, -1))
        key_part = jnp.einsum(
            "kgqs,qkgd->skd",
            d_scores,
            grouped_query[row_first:row_stop],
            preferred_element_type=jnp.float32,
        )
        key_grad = key_grad.at[:row_stop].add(key_part * HEAD_SIZE ** (-0.5))
    return (
        jnp.concatenate(query_grads, axis=0).astype(jnp.bfloat16),
        key_grad.reshape(total_tokens, -1).astype(jnp.bfloat16),
        value_grad.reshape(total_tokens, -1).astype(jnp.bfloat16),
    )


def dot(left, right):
    return jnp.dot(left, right, preferred_element_type=jnp.float32)


def dot_rows(left, right):
    return lax.dot_general(left, right, (((0,), (0,)), ((), ())), preferred_element_type=jnp.float32)


def dot_cols(left, right):
    return lax.dot_general(left, right, (((1,), (1,)), ((), ())), preferred_element_type=jnp.float32)


def local(
    tokens,
    cotangent,
    attn_gain,
    w_query,
    key_weight,
    value_weight,
    w_out,
    mlp_gain,
    w_gate,
    w_up,
    w_down,
    positions,
    lengths,
    deal_slots,
):
    groups = lax.axis_size("fsdp")
    parts = lax.axis_size("sp")
    width = tokens.shape[-1]
    rows = tokens.shape[1]
    fsdp_place = lax.axis_index("fsdp")
    sp_place = lax.axis_index("sp")
    low = jnp.bfloat16
    wide = jnp.float32

    lanes = jnp.arange(groups, dtype=jnp.int32)
    own_row = deal_slots[fsdp_place, sp_place]
    target = own_row // groups
    pick_send = jnp.sum(jnp.where(target[None, :] == lanes[:, None], lanes[None, :], 0), axis=1)
    column = deal_slots[:, sp_place, :]
    arrived_slot = jnp.sum(jnp.where(column // groups == fsdp_place, column % groups, 0), axis=1)
    pick_place = jnp.sum(
        jnp.where(arrived_slot[None, :] == lanes[:, None], lanes[None, :], 0), axis=1
    )

    def to_owner(given):
        blocks = jnp.take(given.reshape(groups, -1, width), pick_send, axis=0)
        came = lax.all_to_all(blocks, "fsdp", split_axis=0, concat_axis=0, tiled=True)
        return jnp.take(came, pick_place, axis=0).reshape(rows, width)

    def to_given(owned):
        blocks = jnp.take(owned.reshape(groups, -1, width), arrived_slot, axis=0)
        gone = lax.all_to_all(blocks, "fsdp", split_axis=0, concat_axis=0, tiled=True)
        return jnp.take(gone, target, axis=0).reshape(tokens.shape)

    def column_share(weight):
        share = weight.shape[1] // parts
        return lax.dynamic_slice_in_dim(weight, sp_place * share, share, axis=1)

    def gather_fsdp(shard):
        return lax.all_gather(shard, "fsdp", axis=0, tiled=True)

    ff_rows = w_down.shape[0]
    ff_share = ff_rows // parts

    def hidden_share(weight):
        def pick(place):
            starts = [i * ff_rows + place * ff_share for i in range(groups)]
            return lambda: jnp.concatenate([weight[:, i : i + ff_share] for i in starts], axis=1)

        return lax.switch(sp_place, [pick(place) for place in range(parts)])

    query_cols = w_query.shape[1] // parts
    key_cols = key_weight.shape[1] // parts
    qkv_cols = query_cols + 2 * key_cols
    extra = -qkv_cols % 128
    extra = extra if extra else 128
    gains = jnp.pad(jnp.stack([attn_gain, mlp_gain], axis=1), ((0, 0), (0, extra - 2)))
    qkv_shard = jnp.concatenate(
        [column_share(w_query), column_share(key_weight), column_share(value_weight), gains], axis=1
    )
    qkv_all = gather_fsdp(qkv_shard)
    out_all = gather_fsdp(column_share(w_out))
    gate_all = gather_fsdp(hidden_share(w_gate))
    up_all = gather_fsdp(hidden_share(w_up))
    down_all = gather_fsdp(lax.dynamic_slice_in_dim(w_down, sp_place * ff_share, ff_share, axis=0))
    qkv_weight = qkv_all[:, :qkv_cols]
    gain_one = qkv_all[:, qkv_cols].astype(wide)[None, :]
    gain_two = qkv_all[:, qkv_cols + 1].astype(wide)[None, :]

    group_inputs = gather_sp(to_owner(tokens)).reshape(-1, width)
    group_incoming = gather_sp(to_owner(cotangent)).reshape(-1, width)
    group_positions = gather_sp(positions.reshape(-1, 1)).reshape(-1)
    total = group_inputs.shape[0]

    inputs = group_inputs.astype(wide)
    rms_one = lax.rsqrt(jnp.mean(inputs * inputs, axis=-1, keepdims=True) + eps)
    normed = (inputs * rms_one * gain_one).astype(low)
    cosine, sine = rotary_tables(group_positions, HEAD_SIZE)
    qkv_rows = dot(normed, qkv_weight)

    def turn(matrix):
        return rotate(matrix.reshape(total, -1, HEAD_SIZE), cosine, sine).reshape(total, -1).astype(low)

    query_low = turn(qkv_rows[:, :query_cols])
    key_low = turn(qkv_rows[:, query_cols : query_cols + key_cols])
    value_low = qkv_rows[:, query_cols + key_cols :].astype(low)
    ends = jnp.cumsum(lengths.reshape(-1))
    places = jnp.arange(total, dtype=jnp.int32)
    segment = jnp.sum((places[:, None] >= ends[None, :]).astype(jnp.int32), axis=1)
    own_mixed, totals = attention(query_low, key_low, value_low, segment)

    def side_by_side(stacked):
        return jnp.concatenate([stacked[i] for i in range(parts)], axis=1)

    def by_columns(matrix):
        share = matrix.shape[1] // parts
        return jnp.stack([matrix[:, i * share : (i + 1) * share] for i in range(parts)], axis=0)

    share = width // parts

    def own_columns(matrix):
        return lax.dynamic_slice_in_dim(matrix, sp_place * share, share, axis=1)

    mixed = side_by_side(gather_sp(own_mixed))
    own_hidden = own_columns(group_inputs).astype(wide) + dot(mixed, out_all)
    hidden_low = side_by_side(gather_sp(own_hidden.astype(low)))

    hidden = hidden_low.astype(wide)
    rms_two = lax.rsqrt(jnp.mean(hidden * hidden, axis=-1, keepdims=True) + eps)
    normed_two = (hidden * rms_two * gain_two).astype(low)
    gate = dot(normed_two, gate_all)
    upward = dot(normed_two, up_all)
    active, active_back = jax.vjp(gated, gate, upward)
    active_low = active.astype(low)
    grad_down = dot_rows(active_low, group_incoming)
    d_active = dot_cols(group_incoming, down_all)
    d_gate, d_up = active_back(d_active)
    d_gate, d_up = d_gate.astype(low), d_up.astype(low)
    grad_gate = dot_rows(normed_two, d_gate).astype(low)
    grad_up = dot_rows(normed_two, d_up).astype(low)
    grad_down = grad_down.astype(low)
    d_gate, d_up, grad_gate, grad_up, grad_down = lax.optimization_barrier(
        (d_gate, d_up, grad_gate, grad_up, grad_down)
    )
    d_normed_two = dot_cols(d_gate, gate_all) + dot_cols(d_up, up_all)
    result_part = dot(active_low, down_all).astype(low)
    own_hidden_rows = lax.dynamic_slice_in_dim(hidden_low, sp_place * rows, rows, axis=0)
    result = own_hidden_rows.astype(wide) + scatter_sp(result_part.reshape(parts, rows, width))
    layer_out = to_given(result.astype(low))

    grad_gain_two = jnp.sum(d_normed_two * hidden * rms_two, axis=0)
    scaled = gain_two * d_normed_two
    back_two = rms_two * scaled - hidden * rms_two**3 * jnp.mean(scaled * hidden, axis=-1, keepdims=True)
    own_d_hidden = own_columns(group_incoming).astype(wide) + scatter_sp(by_columns(back_two.astype(low)))
    d_branch = own_d_hidden.astype(low)
    grad_out = dot_rows(mixed, d_branch)
    d_mixed = scatter_sp(by_columns(dot_cols(d_branch, out_all).astype(low))).astype(low)
    d_query, d_key, d_value = attention_back(query_low, key_low, value_low, segment, totals, d_mixed)

    def turn_back(matrix):
        return (
            rotate_back(matrix.astype(wide).reshape(total, -1, HEAD_SIZE), cosine, sine)
            .reshape(total, -1)
            .astype(low)
        )

    d_qkv = jnp.concatenate([turn_back(d_query), turn_back(d_key), d_value], axis=1)
    grad_qkv = dot_rows(normed, d_qkv)
    d_normed = dot_cols(d_qkv, qkv_weight)
    grad_gain_one = jnp.sum(d_normed * inputs * rms_one, axis=0)
    scaled_one = gain_one * d_normed
    back_one = rms_one * scaled_one - inputs * rms_one**3 * jnp.mean(
        scaled_one * inputs, axis=-1, keepdims=True
    )
    own_place = (jnp.arange(width, dtype=jnp.int32) // share == sp_place)[None, :]
    spread = jnp.concatenate([own_d_hidden] * parts, axis=1)
    back_one = back_one + jnp.where(own_place, spread, 0.0)
    d_inputs = scatter_sp(back_one.astype(low).reshape(parts, rows, width))
    input_grad = to_given(d_inputs.astype(low))

    def scatter_fsdp(matrix):
        return lax.psum_scatter(matrix.astype(low), "fsdp", scatter_dimension=0, tiled=True)

    def all_sp(shard, axis):
        return lax.all_gather(shard, "sp", axis=axis, tiled=True)

    down_shard = all_sp(scatter_fsdp(grad_down), 0).astype(wide)

    def hidden_whole(shard):
        gathered = lax.all_gather(shard, "sp", axis=0, tiled=False)
        return jnp.concatenate(
            [
                gathered[i, :, j * ff_share : (j + 1) * ff_share]
                for j in range(groups)
                for i in range(parts)
            ],
            axis=1,
        ).astype(wide)

    gate_shard = hidden_whole(scatter_fsdp(grad_gate))
    up_shard = hidden_whole(scatter_fsdp(grad_up))
    out_shard = all_sp(scatter_fsdp(grad_out), 1).astype(wide)
    gain_grads = jnp.pad(
        jnp.stack([grad_gain_one, grad_gain_two], axis=1), ((0, 0), (0, extra - 2))
    )
    qkv_shards = lax.all_gather(
        scatter_fsdp(jnp.concatenate([grad_qkv, gain_grads], axis=1)), "sp", axis=0, tiled=False
    ).astype(wide)
    edges = (0, query_cols, query_cols + key_cols, qkv_cols)
    query_shard, key_shard, value_shard = (
        side_by_side(qkv_shards[:, :, edges[i] : edges[i + 1]]) for i in range(3)
    )
    gain_shards = jnp.sum(qkv_shards[:, :, qkv_cols : qkv_cols + 2], axis=0)
    return (
        layer_out,
        input_grad,
        gain_shards[:, 0],
        query_shard,
        key_shard,
        value_shard,
        out_shard,
        gain_shards[:, 1],
        gate_shard,
        up_shard,
        down_shard,
    )


def solution(mesh):
    placed = (
        P("fsdp", "sp", None),
        P("fsdp", "sp", None),
        P("fsdp"),
        P("fsdp", None),
        P("fsdp", None),
        P("fsdp", None),
        P("fsdp", None),
        P("fsdp"),
        P("fsdp", None),
        P("fsdp", None),
        P("fsdp", None),
        P("fsdp", "sp"),
        P("fsdp", None),
        P(),
    )
    return jax.shard_map(
        local,
        mesh=mesh,
        in_specs=placed,
        out_specs=(
            P("fsdp", "sp", None),
            P("fsdp", "sp", None),
            P("fsdp"),
            P("fsdp", None),
            P("fsdp", None),
            P("fsdp", None),
            P("fsdp", None),
            P("fsdp"),
            P("fsdp", None),
            P("fsdp", None),
            P("fsdp", None),
        ),
        check_vma=False,
    )
```

```python
import functools
import jax
import jax.numpy as jnp
from jax import lax
from jax.experimental import pallas as pl
from jax.experimental.pallas import tpu as pltpu
from jax.experimental.layout import Layout, with_layout_constraint
from jax.sharding import PartitionSpec as P

QUERY_HEADS = 32
KEY_VALUE_HEADS = 8
HEAD_SIZE = 80
LANES = 128


eps = 1e-05
theta = 1000000.0
log2e = 1.4426950408889634


def swap(value, bit):
    size = lax.axis_size("sp")
    return lax.ppermute(value, "sp", [(i, i ^ bit) for i in range(size)])


def row_major(value):
    return with_layout_constraint(value, Layout(major_to_minor=tuple(range(value.ndim))))


def gather_sp(value):
    size = lax.axis_size("sp")
    if size != 4:
        return lax.all_gather(value, "sp", axis=0, tiled=False)
    place = lax.axis_index("sp")
    half = value.shape[0] // 2
    first, second = value[:half], value[half:]
    x_first, y_second = swap(first, 1), swap(second, 2)
    x_second, y_first = swap(second, 1), swap(first, 2)
    far_first, far_second = swap(x_first, 2), swap(y_second, 1)
    out = jnp.zeros((size,) + value.shape, value.dtype)
    zeros = (0,) * (value.ndim - 1)
    for turn, low, high in (
        (0, first, second),
        (1, x_first, x_second),
        (2, y_first, y_second),
        (3, far_first, far_second),
    ):
        out = lax.dynamic_update_slice(out, low[None], (place ^ turn, 0) + zeros)
        out = lax.dynamic_update_slice(out, high[None], (place ^ turn, half) + zeros)
    return row_major(out)


def scatter_sp(parts):
    size = lax.axis_size("sp")
    if size != 4:
        return lax.psum_scatter(
            parts, "sp", scatter_dimension=0, tiled=False
        ).astype(jnp.float32)
    place = lax.axis_index("sp")
    half = parts.shape[1] // 2
    parts = row_major(parts)

    def block(turn, lower):
        start = (place ^ turn, 0 if lower else half) + (0,) * (parts.ndim - 2)
        return lax.dynamic_slice(parts, start, (1, half) + parts.shape[2:])[0]

    wide = jnp.float32
    low = parts.dtype
    from_x, from_y = swap(block(3, True), 1), swap(block(3, False), 2)
    x_first, y_second = swap(block(1, True), 1), swap(block(2, False), 2)
    y_first = swap((block(2, True).astype(wide) + from_x.astype(wide)).astype(low), 2)
    x_second = swap((block(1, False).astype(wide) + from_y.astype(wide)).astype(low), 1)
    first = block(0, True).astype(wide) + x_first.astype(wide) + y_first.astype(wide)
    second = block(0, False).astype(wide) + x_second.astype(wide) + y_second.astype(wide)
    return jnp.concatenate([first, second], axis=0)


def rotary_tables(positions):
    halves = HEAD_SIZE // 2
    frequency = theta ** (-(2.0 * jnp.arange(halves, dtype=jnp.float32)) / HEAD_SIZE)
    angles = positions.astype(jnp.float32)[:, None] * frequency[None, :]
    cosine, sine = jnp.cos(angles), jnp.sin(angles)
    rest = jnp.zeros((positions.shape[0], LANES - HEAD_SIZE), jnp.float32)
    return (
        jnp.concatenate([cosine, cosine, rest], axis=1),
        jnp.concatenate([-sine, sine, rest], axis=1),
    )


def gated(gate, upward):
    return jax.nn.silu(gate) * upward


def dot(left, right):
    return jnp.dot(left, right, preferred_element_type=jnp.float32)


def dot_rows(left, right):
    return lax.dot_general(left, right, (((0,), (0,)), ((), ())), preferred_element_type=jnp.float32)


def dot_cols(left, right):
    return lax.dot_general(left, right, (((1,), (1,)), ((), ())), preferred_element_type=jnp.float32)


def head_of(matrix, head):
    first = head * HEAD_SIZE
    if first + LANES <= matrix.shape[1]:
        return matrix[:, first : first + LANES]
    kept = matrix[:, first : first + HEAD_SIZE]
    return jnp.concatenate([kept, jnp.zeros((kept.shape[0], LANES - HEAD_SIZE), kept.dtype)], axis=1)


def half_turn(padded):
    lane = lax.broadcasted_iota(jnp.int32, padded.shape, 1)
    half = HEAD_SIZE // 2
    return jnp.where(lane < half, pltpu.roll(padded, LANES - half, 1), pltpu.roll(padded, half, 1))


def qkv_kernel(heads, keys, x_ref, gain_ref, weight_ref, cos_ref, sin_ref, normed_ref, q_ref, k_ref, v_ref):
    x = x_ref[...].astype(jnp.float32)
    scale = lax.rsqrt(jnp.mean(x * x, axis=1, keepdims=True) + eps)
    normed = (x * scale * gain_ref[...]).astype(jnp.bfloat16)
    normed_ref[...] = normed
    rows = jnp.dot(normed, weight_ref[...], preferred_element_type=jnp.float32)
    cosine, sine = cos_ref[...], sin_ref[...]
    inside = lax.broadcasted_iota(jnp.int32, cosine.shape, 1) < HEAD_SIZE
    for i in range(heads + keys):
        v = head_of(rows, i)
        turned = (v * cosine + half_turn(v) * sine).astype(jnp.bfloat16)
        if i < heads:
            q_ref[:, i * LANES : (i + 1) * LANES] = turned
        else:
            k_ref[:, (i - heads) * LANES : (i - heads + 1) * LANES] = turned
    for i in range(keys):
        v = head_of(rows, heads + keys + i)
        v_ref[:, i * LANES : (i + 1) * LANES] = jnp.where(inside, v, 0.0).astype(jnp.bfloat16)


def qkv_call(x, gain, weight, cosine, sine, heads, keys):
    total, width = x.shape
    block = 256
    bf = jnp.bfloat16
    row = lambda n: pl.BlockSpec((block, n), lambda i: (i, 0))
    whole = lambda a: pl.BlockSpec(a.shape, lambda i: (0, 0))
    return pl.pallas_call(
        functools.partial(qkv_kernel, heads, keys),
        grid=(total // block,),
        in_specs=[row(width), whole(gain), whole(weight), row(LANES), row(LANES)],
        out_specs=[row(width), row(heads * LANES), row(keys * LANES), row(keys * LANES)],
        out_shape=[
            jax.ShapeDtypeStruct((total, width), bf),
            jax.ShapeDtypeStruct((total, heads * LANES), bf),
            jax.ShapeDtypeStruct((total, keys * LANES), bf),
            jax.ShapeDtypeStruct((total, keys * LANES), bf),
        ],
        compiler_params=pltpu.CompilerParams(vmem_limit_bytes=48 * 2**20),
        cost_estimate=pl.CostEstimate(
            flops=2 * total * width * weight.shape[1], bytes_accessed=20 * 2**20, transcendentals=0
        ),
    )(x, gain, weight, cosine, sine)


def attend_kernel(heads, keys, block, q_ref, k_ref, v_ref, start_ref, mixed_ref, lse_ref, bias_ref):
    total = q_ref.shape[0]
    group = heads // keys
    factor = HEAD_SIZE**-0.5 * log2e
    for i in range(total // block):
        first, stop = i * block, (i + 1) * block
        column = lax.broadcasted_iota(jnp.int32, (block, stop), 1)
        row = lax.broadcasted_iota(jnp.int32, (block, stop), 0) + first
        good = (column >= start_ref[first:stop, :]) & (column <= row)
        bias_ref[:, :stop] = jnp.where(good, 0.0, -1e30)
        for head in range(heads):
            lanes = slice(head * LANES, (head + 1) * LANES)
            key = slice(head // group * LANES, (head // group + 1) * LANES)
            scores = dot_cols(q_ref[first:stop, lanes], k_ref[:stop, key]) * factor + bias_ref[:, :stop]
            top = jnp.max(scores, axis=1, keepdims=True)
            weights = jnp.exp2(scores - top)
            summed = jnp.sum(weights, axis=1, keepdims=True)
            mixed = jnp.dot(
                weights.astype(jnp.bfloat16), v_ref[:stop, key], preferred_element_type=jnp.float32
            ) / summed
            mixed_ref[first:stop, head * HEAD_SIZE : (head + 1) * HEAD_SIZE] = mixed[:, :HEAD_SIZE].astype(
                jnp.bfloat16
            )
            lse_ref[first:stop, head : head + 1] = top + jnp.log2(summed)


def attend_call(q, k, v, start, block=256):
    total = q.shape[0]
    heads, keys = q.shape[1] // LANES, k.shape[1] // LANES
    return pl.pallas_call(
        functools.partial(attend_kernel, heads, keys, block),
        out_shape=[
            jax.ShapeDtypeStruct((total, heads * HEAD_SIZE), jnp.bfloat16),
            jax.ShapeDtypeStruct((total, heads), jnp.float32),
        ],
        scratch_shapes=[pltpu.VMEM((block, total), jnp.float32)],
        compiler_params=pltpu.CompilerParams(vmem_limit_bytes=56 * 2**20),
        cost_estimate=pl.CostEstimate(
            flops=heads * total * total * 512, bytes_accessed=8 * 2**20, transcendentals=heads * total * total // 2
        ),
    )(q, k, v, start)


def attend_back_kernel(
    heads, keys, block, q_ref, k_ref, v_ref, grad_ref, lse_ref, start_ref, cos_ref, sin_ref, out_ref, bias_ref, dk_ref, dv_ref
):
    total = q_ref.shape[0]
    group = heads // keys
    scale = HEAD_SIZE**-0.5
    factor = scale * log2e
    low = jnp.bfloat16
    dk_ref[...] = jnp.zeros_like(dk_ref)
    dv_ref[...] = jnp.zeros_like(dv_ref)
    inside = lax.broadcasted_iota(jnp.int32, (block, LANES), 1) < HEAD_SIZE
    half = HEAD_SIZE // 2

    def turned_back(w, rows):
        w = w.astype(low).astype(jnp.float32)
        scaled = w * sin_ref[rows, :]
        lane = lax.broadcasted_iota(jnp.int32, w.shape, 1)
        moved = jnp.where(lane < half, pltpu.roll(scaled, LANES - half, 1), pltpu.roll(scaled, half, 1))
        return (w * cos_ref[rows, :] + moved).astype(low)

    for i in range(total // block):
        first, stop = i * block, (i + 1) * block
        rows = slice(first, stop)
        key_place = lax.broadcasted_iota(jnp.int32, (stop, block), 0)
        place = lax.broadcasted_iota(jnp.int32, (stop, block), 1) + first
        good = (key_place >= start_ref[:, rows]) & (key_place <= place)
        bias_ref[:stop, :] = jnp.where(good, 0.0, -1e30)
        grads = grad_ref[rows, :].astype(jnp.float32)
        for head in range(heads):
            lanes = slice(head * LANES, (head + 1) * LANES)
            key = slice(head // group * LANES, (head // group + 1) * LANES)
            query = q_ref[rows, lanes]
            grad = jnp.where(inside, head_of(grads, head), 0.0).astype(low)
            scores = dot_cols(k_ref[:stop, key], query) * factor + bias_ref[:stop, :]
            probs = jnp.exp2(scores - lse_ref[head : head + 1, rows])
            dv_ref[:stop, key] += jnp.dot(probs.astype(low), grad, preferred_element_type=jnp.float32)
            d_probs = dot_cols(v_ref[:stop, key], grad)
            delta = jnp.sum(probs * d_probs, axis=0, keepdims=True)
            d_scores = (probs * (d_probs - delta)).astype(low)
            dk_ref[:stop, key] += jnp.dot(d_scores, query, preferred_element_type=jnp.float32)
            d_query = dot_rows(d_scores, k_ref[:stop, key]) * scale
            out_ref[rows, head * HEAD_SIZE : (head + 1) * HEAD_SIZE] = turned_back(d_query, rows)[:, :HEAD_SIZE]
    for i in range(total // block):
        rows = slice(i * block, (i + 1) * block)
        for j in range(keys):
            lanes = slice(j * LANES, (j + 1) * LANES)
            at = (heads + j) * HEAD_SIZE
            out_ref[rows, at : at + HEAD_SIZE] = turned_back(dk_ref[rows, lanes] * scale, rows)[:, :HEAD_SIZE]
            at = (heads + keys + j) * HEAD_SIZE
            out_ref[rows, at : at + HEAD_SIZE] = dv_ref[rows, lanes][:, :HEAD_SIZE].astype(low)


def attend_back_call(q, k, v, grad, lse_rows, start_row, cosine, sine_back, block=256):
    total = q.shape[0]
    heads, keys = q.shape[1] // LANES, k.shape[1] // LANES
    return pl.pallas_call(
        functools.partial(attend_back_kernel, heads, keys, block),
        out_shape=jax.ShapeDtypeStruct((total, (heads + 2 * keys) * HEAD_SIZE), jnp.bfloat16),
        scratch_shapes=[
            pltpu.VMEM((total, block), jnp.float32),
            pltpu.VMEM((total, keys * LANES), jnp.float32),
            pltpu.VMEM((total, keys * LANES), jnp.float32),
        ],
        compiler_params=pltpu.CompilerParams(vmem_limit_bytes=56 * 2**20),
        cost_estimate=pl.CostEstimate(
            flops=heads * total * total * 1280, bytes_accessed=12 * 2**20, transcendentals=heads * total * total // 2
        ),
    )(q, k, v, grad, lse_rows, start_row, cosine, sine_back)

def spread_kernel(groups, parts_ref, out_ref):
    parts, _, columns = parts_ref.shape
    share = columns // groups
    for i in range(parts):
        for j in range(groups):
            at = (j * parts + i) * share
            out_ref[:, at : at + share] = parts_ref[i, :, j * share : (j + 1) * share].astype(jnp.float32)


def spread_call(gathered, groups):
    parts, rows, columns = gathered.shape
    block = rows // 5 if rows % 80 == 0 else rows
    return pl.pallas_call(
        functools.partial(spread_kernel, groups),
        grid=(rows // block,),
        in_specs=[pl.BlockSpec((parts, block, columns), lambda i: (0, i, 0))],
        out_specs=pl.BlockSpec((block, parts * columns), lambda i: (i, 0)),
        out_shape=jax.ShapeDtypeStruct((rows, parts * columns), jnp.float32),
        compiler_params=pltpu.CompilerParams(vmem_limit_bytes=32 * 2**20),
        cost_estimate=pl.CostEstimate(
            flops=0, bytes_accessed=6 * parts * rows * columns, transcendentals=0
        ),
    )(gathered)


def after(value, *others):
    return lax.optimization_barrier((value,) + others)[0]


def local(
    tokens,
    cotangent,
    attn_gain,
    w_query,
    key_weight,
    value_weight,
    w_out,
    mlp_gain,
    w_gate,
    w_up,
    w_down,
    positions,
    lengths,
    deal_slots,
):
    groups = lax.axis_size("fsdp")
    parts = lax.axis_size("sp")
    width = tokens.shape[-1]
    rows = tokens.shape[1]
    fsdp_place = lax.axis_index("fsdp")
    sp_place = lax.axis_index("sp")
    low = jnp.bfloat16
    wide = jnp.float32

    lanes = jnp.arange(groups, dtype=jnp.int32)
    own_row = deal_slots[fsdp_place, sp_place]
    target = own_row // groups
    pick_send = jnp.sum(jnp.where(target[None, :] == lanes[:, None], lanes[None, :], 0), axis=1)
    column = deal_slots[:, sp_place, :]
    arrived_slot = jnp.sum(jnp.where(column // groups == fsdp_place, column % groups, 0), axis=1)
    pick_place = jnp.sum(
        jnp.where(arrived_slot[None, :] == lanes[:, None], lanes[None, :], 0), axis=1
    )

    def deal(given):
        blocks = jnp.take(given.reshape(groups, -1, width), pick_send, axis=0)
        return lax.all_to_all(blocks, "fsdp", split_axis=0, concat_axis=0, tiled=True)

    def in_place(came):
        return jnp.take(came, pick_place, axis=0).reshape(rows, width)

    def to_given(owned):
        blocks = jnp.take(owned.reshape(groups, -1, width), arrived_slot, axis=0)
        gone = lax.all_to_all(blocks, "fsdp", split_axis=0, concat_axis=0, tiled=True)
        return jnp.take(gone, target, axis=0).reshape(tokens.shape)

    def column_share(weight):
        share = weight.shape[1] // parts
        return lax.dynamic_slice_in_dim(weight, sp_place * share, share, axis=1)

    def gather_fsdp(shard):
        return lax.all_gather(shard, "fsdp", axis=0, tiled=True)

    ff_rows = w_down.shape[0]
    ff_share = ff_rows // parts

    def hidden_share(weight):
        def pick(place):
            starts = [i * ff_rows + place * ff_share for i in range(groups)]
            return lambda: jnp.concatenate([weight[:, i : i + ff_share] for i in starts], axis=1)

        return lax.switch(sp_place, [pick(place) for place in range(parts)])

    query_cols = w_query.shape[1] // parts
    key_cols = key_weight.shape[1] // parts
    qkv_cols = query_cols + 2 * key_cols
    extra = -qkv_cols % 128
    extra = extra if extra else 128
    gains = jnp.pad(jnp.stack([attn_gain, mlp_gain], axis=1), ((0, 0), (0, extra - 2)))
    came_tokens = deal(tokens)
    w_query, w_out, w_gate, w_up, w_down = (
        after(w, came_tokens) for w in (w_query, w_out, w_gate, w_up, w_down)
    )
    qkv_shard = jnp.concatenate(
        [column_share(w_query), column_share(key_weight), column_share(value_weight), gains], axis=1
    )
    qkv_all = gather_fsdp(qkv_shard)
    out_all = gather_fsdp(column_share(w_out))
    gate_all = gather_fsdp(hidden_share(w_gate))
    up_all = gather_fsdp(hidden_share(w_up))
    down_all = gather_fsdp(lax.dynamic_slice_in_dim(w_down, sp_place * ff_share, ff_share, axis=0))
    qkv_weight = qkv_all[:, :qkv_cols]
    gain_one = qkv_all[:, qkv_cols].astype(wide)[None, :]
    gain_two = qkv_all[:, qkv_cols + 1].astype(wide)[None, :]

    group_inputs = gather_sp(in_place(came_tokens)).reshape(-1, width)
    group_incoming = gather_sp(in_place(deal(after(cotangent, qkv_all)))).reshape(-1, width)
    group_positions = gather_sp(positions.reshape(-1, 1)).reshape(-1)
    total = group_inputs.shape[0]

    cosine, sine = rotary_tables(group_positions)
    heads, keys = query_cols // HEAD_SIZE, key_cols // HEAD_SIZE
    normed, query_low, key_low, value_low = qkv_call(
        group_inputs, gain_one, qkv_all, cosine, sine, heads, keys
    )
    sizes = lengths.reshape(-1)
    ends = jnp.cumsum(sizes)
    places = jnp.arange(total, dtype=jnp.int32)
    start = jnp.sum(jnp.where(places[:, None] >= ends[None, :], sizes[None, :], 0), axis=1)
    own_mixed, logs = attend_call(query_low, key_low, value_low, start[:, None])

    def side_by_side(stacked):
        return jnp.concatenate([stacked[i] for i in range(parts)], axis=1)

    def by_columns(matrix):
        share = matrix.shape[1] // parts
        return jnp.stack([matrix[:, i * share : (i + 1) * share] for i in range(parts)], axis=0)

    share = width // parts

    def own_columns(matrix):
        return lax.dynamic_slice_in_dim(matrix, sp_place * share, share, axis=1)

    mixed = side_by_side(gather_sp(own_mixed))
    own_hidden = own_columns(group_inputs).astype(wide) + dot(mixed, out_all)
    hidden_low = side_by_side(gather_sp(own_hidden.astype(low)))

    hidden = hidden_low.astype(wide)
    rms_two = lax.rsqrt(jnp.mean(hidden * hidden, axis=-1, keepdims=True) + eps)
    normed_two = (hidden * rms_two * gain_two).astype(low)
    gate = dot(normed_two, gate_all)
    upward = dot(normed_two, up_all)
    active, active_back = jax.vjp(gated, gate, upward)
    active_low = active.astype(low)
    grad_down = dot_rows(active_low, group_incoming).astype(low)
    d_active = dot_cols(after(group_incoming, grad_down), down_all)
    d_gate, d_up = active_back(d_active)
    d_gate, d_up = d_gate.astype(low), d_up.astype(low)
    d_normed_two = dot_cols(d_gate, gate_all) + dot_cols(d_up, up_all)
    grad_gate = dot_rows(normed_two, d_gate).astype(low)
    grad_up = dot_rows(normed_two, d_up).astype(low)
    grad_gain_two = jnp.sum(d_normed_two * hidden * rms_two, axis=0)
    scaled = gain_two * d_normed_two
    back_two = rms_two * scaled - hidden * rms_two**3 * jnp.mean(scaled * hidden, axis=-1, keepdims=True)
    own_d_hidden = own_columns(group_incoming).astype(wide) + scatter_sp(by_columns(back_two.astype(low)))
    d_branch = own_d_hidden.astype(low)
    grad_out = dot_rows(mixed, d_branch)
    d_mixed = scatter_sp(by_columns(dot_cols(d_branch, out_all).astype(low))).astype(low)
    result_part = dot(after(active_low, d_mixed), down_all).astype(low)
    own_hidden_rows = lax.dynamic_slice_in_dim(hidden_low, sp_place * rows, rows, axis=0)
    result = own_hidden_rows.astype(wide) + scatter_sp(result_part.reshape(parts, rows, width))
    layer_out = to_given(result.astype(low))

    d_qkv = attend_back_call(
        query_low, key_low, value_low, d_mixed, logs.T, start[None, :], cosine, sine
    )
    grad_qkv = dot_rows(normed, d_qkv)
    d_normed = dot_cols(d_qkv, qkv_weight)
    inputs = group_inputs.astype(wide)
    rms_one = lax.rsqrt(jnp.mean(inputs * inputs, axis=-1, keepdims=True) + eps)
    grad_gain_one = jnp.sum(d_normed * inputs * rms_one, axis=0)
    scaled_one = gain_one * d_normed
    back_one = rms_one * scaled_one - inputs * rms_one**3 * jnp.mean(
        scaled_one * inputs, axis=-1, keepdims=True
    )
    own_place = (jnp.arange(width, dtype=jnp.int32) // share == sp_place)[None, :]
    spread = jnp.concatenate([own_d_hidden] * parts, axis=1)
    back_one = back_one + jnp.where(own_place, spread, 0.0)
    d_inputs = scatter_sp(back_one.astype(low).reshape(parts, rows, width))
    input_grad = to_given(d_inputs.astype(low))

    def scatter_fsdp(matrix):
        return lax.psum_scatter(matrix.astype(low), "fsdp", scatter_dimension=0, tiled=True)

    def all_sp(shard, axis):
        return lax.all_gather(shard, "sp", axis=axis, tiled=True)

    gain_grads = jnp.pad(
        jnp.stack([grad_gain_one, grad_gain_two], axis=1), ((0, 0), (0, extra - 2))
    )
    down_sum = scatter_fsdp(grad_down)
    gate_sum = scatter_fsdp(after(grad_gate, down_sum))
    up_sum = scatter_fsdp(after(grad_up, gate_sum))
    out_sum = scatter_fsdp(after(grad_out.astype(low), up_sum))
    qkv_sum = scatter_fsdp(after(jnp.concatenate([grad_qkv, gain_grads], axis=1).astype(low), out_sum))

    down_shard = all_sp(down_sum, 0).astype(wide)

    def hidden_whole(shard):
        return spread_call(lax.all_gather(shard, "sp", axis=0, tiled=False), groups)

    gate_shard = hidden_whole(gate_sum)
    up_shard = hidden_whole(up_sum)
    out_shard = side_by_side(gather_sp(out_sum)).astype(wide)
    qkv_shards = gather_sp(qkv_sum).astype(wide)
    edges = (0, query_cols, query_cols + key_cols, qkv_cols)
    query_shard, key_shard, value_shard = (
        side_by_side(qkv_shards[:, :, edges[i] : edges[i + 1]]) for i in range(3)
    )
    gain_shards = jnp.sum(qkv_shards[:, :, qkv_cols : qkv_cols + 2], axis=0)
    return (
        layer_out,
        input_grad,
        gain_shards[:, 0],
        query_shard,
        key_shard,
        value_shard,
        out_shard,
        gain_shards[:, 1],
        gate_shard,
        up_shard,
        down_shard,
    )


def solution(mesh):
    placed = (
        P("fsdp", "sp", None),
        P("fsdp", "sp", None),
        P("fsdp"),
        P("fsdp", None),
        P("fsdp", None),
        P("fsdp", None),
        P("fsdp", None),
        P("fsdp"),
        P("fsdp", None),
        P("fsdp", None),
        P("fsdp", None),
        P("fsdp", "sp"),
        P("fsdp", None),
        P(),
    )
    return jax.shard_map(
        local,
        mesh=mesh,
        in_specs=placed,
        out_specs=(
            P("fsdp", "sp", None),
            P("fsdp", "sp", None),
            P("fsdp"),
            P("fsdp", None),
            P("fsdp", None),
            P("fsdp", None),
            P("fsdp", None),
            P("fsdp"),
            P("fsdp", None),
            P("fsdp", None),
            P("fsdp", None),
        ),
        check_vma=False,
    )
```

```python
import functools
import jax
import jax.numpy as jnp
from jax import lax
from jax.experimental import pallas as pl
from jax.experimental.pallas import tpu as pltpu
from jax.experimental.layout import Layout, with_layout_constraint
from jax.sharding import PartitionSpec as P

QUERY_HEADS = 32
KEY_VALUE_HEADS = 8
HEAD_SIZE = 80
LANES = 128


eps = 1e-05
theta = 1000000.0
log2e = 1.4426950408889634


def swap(value, bit):
    size = lax.axis_size("sp")
    return lax.ppermute(value, "sp", [(i, i ^ bit) for i in range(size)])


def row_major(value):
    return with_layout_constraint(value, Layout(major_to_minor=tuple(range(value.ndim))))


def gather_sp(value):
    size = lax.axis_size("sp")
    if size != 4:
        return lax.all_gather(value, "sp", axis=0, tiled=False)
    place = lax.axis_index("sp")
    half = value.shape[0] // 2
    first, second = value[:half], value[half:]
    x_first, y_second = swap(first, 1), swap(second, 2)
    x_second, y_first = swap(second, 1), swap(first, 2)
    far_first, far_second = swap(x_first, 2), swap(y_second, 1)
    out = jnp.zeros((size,) + value.shape, value.dtype)
    zeros = (0,) * (value.ndim - 1)
    for turn, low, high in (
        (0, first, second),
        (1, x_first, x_second),
        (2, y_first, y_second),
        (3, far_first, far_second),
    ):
        out = lax.dynamic_update_slice(out, low[None], (place ^ turn, 0) + zeros)
        out = lax.dynamic_update_slice(out, high[None], (place ^ turn, half) + zeros)
    return row_major(out)


def gather_small(value):
    size = lax.axis_size("sp")
    if size != 4:
        return lax.all_gather(value, "sp", axis=0, tiled=False)
    place = lax.axis_index("sp")
    pieces = [value] + [swap(value, turn) for turn in range(1, size)]
    here = [
        sum(jnp.where(place ^ turn == i, pieces[turn], 0) for turn in range(size)) for i in range(size)
    ]
    return jnp.stack(here, axis=0)


def scatter_sp(parts):
    size = lax.axis_size("sp")
    if size != 4:
        return lax.psum_scatter(
            parts, "sp", scatter_dimension=0, tiled=False
        ).astype(jnp.float32)
    place = lax.axis_index("sp")
    half = parts.shape[1] // 2
    parts = row_major(parts)

    def block(turn, lower):
        start = (place ^ turn, 0 if lower else half) + (0,) * (parts.ndim - 2)
        return lax.dynamic_slice(parts, start, (1, half) + parts.shape[2:])[0]

    wide = jnp.float32
    low = parts.dtype
    from_x, from_y = swap(block(3, True), 1), swap(block(3, False), 2)
    x_first, y_second = swap(block(1, True), 1), swap(block(2, False), 2)
    y_first = swap((block(2, True).astype(wide) + from_x.astype(wide)).astype(low), 2)
    x_second = swap((block(1, False).astype(wide) + from_y.astype(wide)).astype(low), 1)
    first = block(0, True).astype(wide) + x_first.astype(wide) + y_first.astype(wide)
    second = block(0, False).astype(wide) + x_second.astype(wide) + y_second.astype(wide)
    return jnp.concatenate([first, second], axis=0)


def rotary_tables(positions):
    halves = HEAD_SIZE // 2
    frequency = theta ** (-(2.0 * jnp.arange(halves, dtype=jnp.float32)) / HEAD_SIZE)
    angles = positions.astype(jnp.float32)[:, None] * frequency[None, :]
    cosine, sine = jnp.cos(angles), jnp.sin(angles)
    rest = jnp.zeros((positions.shape[0], LANES - HEAD_SIZE), jnp.float32)
    return (
        jnp.concatenate([cosine, cosine, rest], axis=1),
        jnp.concatenate([-sine, sine, rest], axis=1),
    )


def gated(gate, upward):
    return jax.nn.silu(gate) * upward


def dot(left, right):
    return jnp.dot(left, right, preferred_element_type=jnp.float32)


def dot_rows(left, right):
    return lax.dot_general(left, right, (((0,), (0,)), ((), ())), preferred_element_type=jnp.float32)


def dot_cols(left, right):
    return lax.dot_general(left, right, (((1,), (1,)), ((), ())), preferred_element_type=jnp.float32)


def head_of(matrix, head):
    first = head * HEAD_SIZE
    if first + LANES <= matrix.shape[1]:
        return matrix[:, first : first + LANES]
    kept = matrix[:, first : first + HEAD_SIZE]
    return jnp.concatenate([kept, jnp.zeros((kept.shape[0], LANES - HEAD_SIZE), kept.dtype)], axis=1)


def half_turn(padded):
    lane = lax.broadcasted_iota(jnp.int32, padded.shape, 1)
    half = HEAD_SIZE // 2
    return jnp.where(lane < half, pltpu.roll(padded, LANES - half, 1), pltpu.roll(padded, half, 1))


def qkv_kernel(heads, keys, x_ref, gain_ref, weight_ref, cos_ref, sin_ref, normed_ref, q_ref, k_ref, v_ref):
    x = x_ref[...].astype(jnp.float32)
    scale = lax.rsqrt(jnp.mean(x * x, axis=1, keepdims=True) + eps)
    normed = (x * scale * gain_ref[...]).astype(jnp.bfloat16)
    normed_ref[...] = normed
    rows = jnp.dot(normed, weight_ref[...], preferred_element_type=jnp.float32)
    cosine, sine = cos_ref[...], sin_ref[...]
    inside = lax.broadcasted_iota(jnp.int32, cosine.shape, 1) < HEAD_SIZE
    for i in range(heads + keys):
        v = head_of(rows, i)
        turned = (v * cosine + half_turn(v) * sine).astype(jnp.bfloat16)
        if i < heads:
            q_ref[:, i * LANES : (i + 1) * LANES] = turned
        else:
            k_ref[:, (i - heads) * LANES : (i - heads + 1) * LANES] = turned
    for i in range(keys):
        v = head_of(rows, heads + keys + i)
        v_ref[:, i * LANES : (i + 1) * LANES] = jnp.where(inside, v, 0.0).astype(jnp.bfloat16)


def qkv_call(x, gain, weight, cosine, sine, heads, keys):
    total, width = x.shape
    block = 256
    bf = jnp.bfloat16
    row = lambda n: pl.BlockSpec((block, n), lambda i: (i, 0))
    whole = lambda a: pl.BlockSpec(a.shape, lambda i: (0, 0))
    return pl.pallas_call(
        functools.partial(qkv_kernel, heads, keys),
        grid=(total // block,),
        in_specs=[row(width), whole(gain), whole(weight), row(LANES), row(LANES)],
        out_specs=[row(width), row(heads * LANES), row(keys * LANES), row(keys * LANES)],
        out_shape=[
            jax.ShapeDtypeStruct((total, width), bf),
            jax.ShapeDtypeStruct((total, heads * LANES), bf),
            jax.ShapeDtypeStruct((total, keys * LANES), bf),
            jax.ShapeDtypeStruct((total, keys * LANES), bf),
        ],
        compiler_params=pltpu.CompilerParams(vmem_limit_bytes=48 * 2**20),
        cost_estimate=pl.CostEstimate(
            flops=2 * total * width * weight.shape[1], bytes_accessed=20 * 2**20, transcendentals=0
        ),
    )(x, gain, weight, cosine, sine)


def attend_kernel(heads, keys, block, q_ref, k_ref, v_ref, start_ref, mixed_ref, lse_ref, bias_ref):
    total = q_ref.shape[0]
    group = heads // keys
    factor = HEAD_SIZE**-0.5 * log2e
    for i in range(total // block):
        first, stop = i * block, (i + 1) * block
        column = lax.broadcasted_iota(jnp.int32, (block, stop), 1)
        row = lax.broadcasted_iota(jnp.int32, (block, stop), 0) + first
        good = (column >= start_ref[first:stop, :]) & (column <= row)
        bias_ref[:, :stop] = jnp.where(good, 0.0, -1e30)
        for head in range(heads):
            lanes = slice(head * LANES, (head + 1) * LANES)
            key = slice(head // group * LANES, (head // group + 1) * LANES)
            scores = dot_cols(q_ref[first:stop, lanes], k_ref[:stop, key]) * factor + bias_ref[:, :stop]
            top = jnp.max(scores, axis=1, keepdims=True)
            weights = jnp.exp2(scores - top)
            summed = jnp.sum(weights, axis=1, keepdims=True)
            mixed = jnp.dot(
                weights.astype(jnp.bfloat16), v_ref[:stop, key], preferred_element_type=jnp.float32
            ) / summed
            mixed_ref[first:stop, head * HEAD_SIZE : (head + 1) * HEAD_SIZE] = mixed[:, :HEAD_SIZE].astype(
                jnp.bfloat16
            )
            lse_ref[first:stop, head : head + 1] = top + jnp.log2(summed)


def attend_call(q, k, v, start, block=256):
    total = q.shape[0]
    heads, keys = q.shape[1] // LANES, k.shape[1] // LANES
    return pl.pallas_call(
        functools.partial(attend_kernel, heads, keys, block),
        out_shape=[
            jax.ShapeDtypeStruct((total, heads * HEAD_SIZE), jnp.bfloat16),
            jax.ShapeDtypeStruct((total, heads), jnp.float32),
        ],
        scratch_shapes=[pltpu.VMEM((block, total), jnp.float32)],
        compiler_params=pltpu.CompilerParams(vmem_limit_bytes=56 * 2**20),
        cost_estimate=pl.CostEstimate(
            flops=heads * total * total * 512, bytes_accessed=8 * 2**20, transcendentals=heads * total * total // 2
        ),
    )(q, k, v, start)


def attend_back_kernel(
    heads, keys, block, q_ref, k_ref, v_ref, grad_ref, lse_ref, start_ref, cos_ref, sin_ref, out_ref, bias_ref, dk_ref, dv_ref
):
    total = q_ref.shape[0]
    group = heads // keys
    scale = HEAD_SIZE**-0.5
    factor = scale * log2e
    low = jnp.bfloat16
    dk_ref[...] = jnp.zeros_like(dk_ref)
    dv_ref[...] = jnp.zeros_like(dv_ref)
    inside = lax.broadcasted_iota(jnp.int32, (block, LANES), 1) < HEAD_SIZE
    half = HEAD_SIZE // 2

    def turned_back(w, rows):
        w = w.astype(low).astype(jnp.float32)
        scaled = w * sin_ref[rows, :]
        lane = lax.broadcasted_iota(jnp.int32, w.shape, 1)
        moved = jnp.where(lane < half, pltpu.roll(scaled, LANES - half, 1), pltpu.roll(scaled, half, 1))
        return (w * cos_ref[rows, :] + moved).astype(low)

    for i in range(total // block):
        first, stop = i * block, (i + 1) * block
        rows = slice(first, stop)
        key_place = lax.broadcasted_iota(jnp.int32, (stop, block), 0)
        place = lax.broadcasted_iota(jnp.int32, (stop, block), 1) + first
        good = (key_place >= start_ref[:, rows]) & (key_place <= place)
        bias_ref[:stop, :] = jnp.where(good, 0.0, -1e30)
        grads = grad_ref[rows, :].astype(jnp.float32)
        for head in range(heads):
            lanes = slice(head * LANES, (head + 1) * LANES)
            key = slice(head // group * LANES, (head // group + 1) * LANES)
            query = q_ref[rows, lanes]
            grad = jnp.where(inside, head_of(grads, head), 0.0).astype(low)
            scores = dot_cols(k_ref[:stop, key], query) * factor + bias_ref[:stop, :]
            probs = jnp.exp2(scores - lse_ref[head : head + 1, rows])
            dv_ref[:stop, key] += jnp.dot(probs.astype(low), grad, preferred_element_type=jnp.float32)
            d_probs = dot_cols(v_ref[:stop, key], grad)
            delta = jnp.sum(probs * d_probs, axis=0, keepdims=True)
            d_scores = (probs * (d_probs - delta)).astype(low)
            dk_ref[:stop, key] += jnp.dot(d_scores, query, preferred_element_type=jnp.float32)
            d_query = dot_rows(d_scores, k_ref[:stop, key]) * scale
            out_ref[rows, head * HEAD_SIZE : (head + 1) * HEAD_SIZE] = turned_back(d_query, rows)[:, :HEAD_SIZE]
    for i in range(total // block):
        rows = slice(i * block, (i + 1) * block)
        for j in range(keys):
            lanes = slice(j * LANES, (j + 1) * LANES)
            at = (heads + j) * HEAD_SIZE
            out_ref[rows, at : at + HEAD_SIZE] = turned_back(dk_ref[rows, lanes] * scale, rows)[:, :HEAD_SIZE]
            at = (heads + keys + j) * HEAD_SIZE
            out_ref[rows, at : at + HEAD_SIZE] = dv_ref[rows, lanes][:, :HEAD_SIZE].astype(low)


def attend_back_call(q, k, v, grad, lse_rows, start_row, cosine, sine_back, block=256):
    total = q.shape[0]
    heads, keys = q.shape[1] // LANES, k.shape[1] // LANES
    return pl.pallas_call(
        functools.partial(attend_back_kernel, heads, keys, block),
        out_shape=jax.ShapeDtypeStruct((total, (heads + 2 * keys) * HEAD_SIZE), jnp.bfloat16),
        scratch_shapes=[
            pltpu.VMEM((total, block), jnp.float32),
            pltpu.VMEM((total, keys * LANES), jnp.float32),
            pltpu.VMEM((total, keys * LANES), jnp.float32),
        ],
        compiler_params=pltpu.CompilerParams(vmem_limit_bytes=56 * 2**20),
        cost_estimate=pl.CostEstimate(
            flops=heads * total * total * 1280, bytes_accessed=12 * 2**20, transcendentals=heads * total * total // 2
        ),
    )(q, k, v, grad, lse_rows, start_row, cosine, sine_back)

def spread_kernel(groups, parts_ref, out_ref):
    parts, _, columns = parts_ref.shape
    share = columns // groups
    for i in range(parts):
        for j in range(groups):
            at = (j * parts + i) * share
            out_ref[:, at : at + share] = parts_ref[i, :, j * share : (j + 1) * share].astype(jnp.float32)


def spread_call(gathered, groups):
    parts, rows, columns = gathered.shape
    block = rows // 5 if rows % 80 == 0 else rows
    return pl.pallas_call(
        functools.partial(spread_kernel, groups),
        grid=(rows // block,),
        in_specs=[pl.BlockSpec((parts, block, columns), lambda i: (0, i, 0))],
        out_specs=pl.BlockSpec((block, parts * columns), lambda i: (i, 0)),
        out_shape=jax.ShapeDtypeStruct((rows, parts * columns), jnp.float32),
        compiler_params=pltpu.CompilerParams(vmem_limit_bytes=32 * 2**20),
        cost_estimate=pl.CostEstimate(
            flops=0, bytes_accessed=6 * parts * rows * columns, transcendentals=0
        ),
    )(gathered)


def pass_kernel(*refs):
    pass


def after(value, *others):
    here = pl.BlockSpec(memory_space=pl.ANY)
    return pl.pallas_call(
        pass_kernel,
        in_specs=[here] * (1 + len(others)),
        out_specs=here,
        out_shape=jax.ShapeDtypeStruct(value.shape, value.dtype),
        input_output_aliases={0: 0},
        cost_estimate=pl.CostEstimate(flops=0, bytes_accessed=0, transcendentals=0),
    )(value, *others)


def pack_kernel(groups, parts, place_ref, gate_ref, up_ref, _, out_ref):
    rows, columns = gate_ref.shape
    share = columns // (groups * parts)
    for place in range(parts):

        @pl.when(place_ref[0] == place)
        def _():
            for i, ref in enumerate((gate_ref, up_ref)):
                for j in range(groups):
                    at = (i * groups + j) * share
                    begin = (j * parts + place) * share
                    out_ref[:, at : at + share] = ref[:, begin : begin + share]


def pack_call(place, gate, up, when, groups, parts):
    rows, columns = gate.shape
    block = rows // 5 if rows % 80 == 0 else rows
    spec = pl.BlockSpec((block, columns), lambda i: (i, 0))
    return pl.pallas_call(
        functools.partial(pack_kernel, groups, parts),
        grid=(rows // block,),
        in_specs=[
            pl.BlockSpec(memory_space=pltpu.SMEM),
            spec,
            spec,
            pl.BlockSpec(memory_space=pl.ANY),
        ],
        out_specs=pl.BlockSpec((block, 2 * columns // parts), lambda i: (i, 0)),
        out_shape=jax.ShapeDtypeStruct((rows, 2 * columns // parts), gate.dtype),
        compiler_params=pltpu.CompilerParams(vmem_limit_bytes=32 * 2**20),
        cost_estimate=pl.CostEstimate(flops=0, bytes_accessed=5 * rows * columns, transcendentals=0),
    )(place, gate, up, when)


def local(
    tokens,
    cotangent,
    attn_gain,
    w_query,
    key_weight,
    value_weight,
    w_out,
    mlp_gain,
    w_gate,
    w_up,
    w_down,
    positions,
    lengths,
    deal_slots,
):
    groups = lax.axis_size("fsdp")
    parts = lax.axis_size("sp")
    width = tokens.shape[-1]
    rows = tokens.shape[1]
    fsdp_place = lax.axis_index("fsdp")
    sp_place = lax.axis_index("sp")
    low = jnp.bfloat16
    wide = jnp.float32

    lanes = jnp.arange(groups, dtype=jnp.int32)
    own_row = deal_slots[fsdp_place, sp_place]
    target = own_row // groups
    pick_send = jnp.sum(jnp.where(target[None, :] == lanes[:, None], lanes[None, :], 0), axis=1)
    column = deal_slots[:, sp_place, :]
    arrived_slot = jnp.sum(jnp.where(column // groups == fsdp_place, column % groups, 0), axis=1)
    pick_place = jnp.sum(
        jnp.where(arrived_slot[None, :] == lanes[:, None], lanes[None, :], 0), axis=1
    )

    def picked(given):
        return jnp.take(given.reshape(groups, -1, width), pick_send, axis=0)

    def deal(blocks):
        return lax.all_to_all(blocks, "fsdp", split_axis=0, concat_axis=0, tiled=True)

    def in_place(came):
        return jnp.take(came, pick_place, axis=0).reshape(rows, width)

    def to_given(owned):
        blocks = jnp.take(owned.reshape(groups, -1, width), arrived_slot, axis=0)
        gone = lax.all_to_all(blocks, "fsdp", split_axis=0, concat_axis=0, tiled=True)
        return jnp.take(gone, target, axis=0).reshape(tokens.shape)

    def column_share(weight):
        share = weight.shape[1] // parts
        return lax.dynamic_slice_in_dim(weight, sp_place * share, share, axis=1)

    def gather_fsdp(shard):
        return lax.all_gather(shard, "fsdp", axis=0, tiled=True)

    ff_rows = w_down.shape[0]
    ff_share = ff_rows // parts

    query_cols = w_query.shape[1] // parts
    key_cols = key_weight.shape[1] // parts
    qkv_cols = query_cols + 2 * key_cols
    extra = -qkv_cols % 128
    extra = extra if extra else 128
    gains = jnp.pad(jnp.stack([attn_gain, mlp_gain], axis=1), ((0, 0), (0, extra - 2)))
    came_tokens = deal(picked(tokens))
    came_incoming = deal(after(picked(cotangent), came_tokens))
    gate_up_shard = pack_call(sp_place.reshape(1), w_gate, w_up, came_tokens, groups, parts)
    qkv_shard = jnp.concatenate(
        [column_share(w_query), column_share(key_weight), column_share(value_weight), gains], axis=1
    )
    qkv_all = gather_fsdp(qkv_shard)
    out_all = gather_fsdp(column_share(w_out))
    gate_up_all = gather_fsdp(gate_up_shard)
    hidden_units = gate_up_all.shape[1] // 2
    gate_all, up_all = gate_up_all[:, :hidden_units], gate_up_all[:, hidden_units:]
    down_all = gather_fsdp(lax.dynamic_slice_in_dim(w_down, sp_place * ff_share, ff_share, axis=0))
    qkv_weight = qkv_all[:, :qkv_cols]
    gain_one = qkv_all[:, qkv_cols].astype(wide)[None, :]
    gain_two = qkv_all[:, qkv_cols + 1].astype(wide)[None, :]

    group_inputs = gather_sp(in_place(came_tokens)).reshape(-1, width)
    group_incoming = gather_sp(after(in_place(came_incoming), group_inputs)).reshape(-1, width)
    group_positions = gather_small(positions.reshape(-1)).reshape(-1)
    total = group_inputs.shape[0]

    cosine, sine = rotary_tables(group_positions)
    heads, keys = query_cols // HEAD_SIZE, key_cols // HEAD_SIZE
    normed, query_low, key_low, value_low = qkv_call(
        group_inputs, gain_one, qkv_all, cosine, sine, heads, keys
    )
    sizes = lengths.reshape(-1)
    ends = jnp.cumsum(sizes)
    places = jnp.arange(total, dtype=jnp.int32)
    start = jnp.sum(jnp.where(places[:, None] >= ends[None, :], sizes[None, :], 0), axis=1)
    own_mixed, logs = attend_call(query_low, key_low, value_low, start[:, None])

    def side_by_side(stacked):
        return jnp.concatenate([stacked[i] for i in range(parts)], axis=1)

    def by_columns(matrix):
        share = matrix.shape[1] // parts
        return jnp.stack([matrix[:, i * share : (i + 1) * share] for i in range(parts)], axis=0)

    share = width // parts

    def own_columns(matrix):
        return lax.dynamic_slice_in_dim(matrix, sp_place * share, share, axis=1)

    mixed = side_by_side(gather_sp(own_mixed))
    own_hidden = own_columns(group_inputs).astype(wide) + dot(mixed, out_all)
    hidden_low = side_by_side(gather_sp(own_hidden.astype(low)))

    hidden = hidden_low.astype(wide)
    rms_two = lax.rsqrt(jnp.mean(hidden * hidden, axis=-1, keepdims=True) + eps)
    normed_two = (hidden * rms_two * gain_two).astype(low)
    gate = dot(normed_two, gate_all)
    upward = dot(normed_two, up_all)
    active, active_back = jax.vjp(gated, gate, upward)
    active_low = active.astype(low)
    grad_down = dot_rows(active_low, group_incoming).astype(low)
    down_all = after(down_all, grad_down)
    d_active = dot_cols(group_incoming, down_all)
    d_gate, d_up = active_back(d_active)
    d_gate, d_up = d_gate.astype(low), d_up.astype(low)
    d_hidden_units = jnp.concatenate([d_gate, d_up], axis=1)
    d_normed_two = dot_cols(d_hidden_units, gate_up_all)
    grad_gain_two = jnp.sum(d_normed_two * hidden * rms_two, axis=0)
    scaled = gain_two * d_normed_two
    back_two = rms_two * scaled - hidden * rms_two**3 * jnp.mean(scaled * hidden, axis=-1, keepdims=True)
    back_two = back_two.astype(low)
    d_hidden_units = after(d_hidden_units, back_two)
    grad_gate = dot_rows(normed_two, d_hidden_units[:, :hidden_units]).astype(low)
    grad_up = dot_rows(normed_two, d_hidden_units[:, hidden_units:]).astype(low)
    own_d_hidden = own_columns(group_incoming).astype(wide) + scatter_sp(by_columns(back_two))
    d_branch = own_d_hidden.astype(low)
    grad_out = dot_rows(mixed, d_branch)
    d_mixed = scatter_sp(by_columns(dot_cols(d_branch, out_all).astype(low))).astype(low)
    result_part = after(dot(after(active_low, d_branch, grad_down), down_all).astype(low), d_mixed)
    own_hidden_rows = lax.dynamic_slice_in_dim(hidden_low, sp_place * rows, rows, axis=0)
    result = own_hidden_rows.astype(wide) + scatter_sp(result_part.reshape(parts, rows, width))
    layer_out = to_given(result.astype(low))

    d_qkv = attend_back_call(
        query_low, key_low, value_low, d_mixed, logs.T, start[None, :], cosine, sine
    )
    grad_qkv = dot_rows(normed, d_qkv)
    d_normed = dot_cols(d_qkv, qkv_weight)
    inputs = group_inputs.astype(wide)
    rms_one = lax.rsqrt(jnp.mean(inputs * inputs, axis=-1, keepdims=True) + eps)
    grad_gain_one = jnp.sum(d_normed * inputs * rms_one, axis=0)
    scaled_one = gain_one * d_normed
    back_one = rms_one * scaled_one - inputs * rms_one**3 * jnp.mean(
        scaled_one * inputs, axis=-1, keepdims=True
    )
    own_place = (jnp.arange(width, dtype=jnp.int32) // share == sp_place)[None, :]
    spread = jnp.concatenate([own_d_hidden] * parts, axis=1)
    back_one = back_one + jnp.where(own_place, spread, 0.0)
    d_inputs = scatter_sp(back_one.astype(low).reshape(parts, rows, width))
    input_grad = to_given(d_inputs.astype(low))

    def scatter_fsdp(matrix):
        return lax.psum_scatter(matrix.astype(low), "fsdp", scatter_dimension=0, tiled=True)

    def all_sp(shard):
        return lax.all_gather(shard, "sp", axis=0, tiled=False)

    gain_grads = jnp.pad(
        jnp.stack([grad_gain_one, grad_gain_two], axis=1), ((0, 0), (0, extra - 2))
    )
    down_sum = scatter_fsdp(grad_down)
    gate_sum = scatter_fsdp(grad_gate)
    up_sum = scatter_fsdp(grad_up)
    out_sum = scatter_fsdp(grad_out)
    qkv_sum = scatter_fsdp(jnp.concatenate([grad_qkv, gain_grads], axis=1))

    down_parts = all_sp(down_sum)
    gate_parts = all_sp(after(gate_sum, down_parts))
    up_parts = all_sp(after(up_sum, gate_parts))
    out_sum = after(out_sum, up_parts)
    qkv_sum = after(qkv_sum, out_sum)
    down_shard = down_parts.reshape(-1, width).astype(wide)
    gate_shard = spread_call(gate_parts, groups)
    up_shard = spread_call(up_parts, groups)
    out_shard = side_by_side(gather_sp(out_sum)).astype(wide)
    qkv_shards = gather_sp(qkv_sum).astype(wide)
    edges = (0, query_cols, query_cols + key_cols, qkv_cols)
    query_shard, key_shard, value_shard = (
        side_by_side(qkv_shards[:, :, edges[i] : edges[i + 1]]) for i in range(3)
    )
    gain_shards = jnp.sum(qkv_shards[:, :, qkv_cols : qkv_cols + 2], axis=0)
    return (
        layer_out,
        input_grad,
        gain_shards[:, 0],
        query_shard,
        key_shard,
        value_shard,
        out_shard,
        gain_shards[:, 1],
        gate_shard,
        up_shard,
        down_shard,
    )


def solution(mesh):
    placed = (
        P("fsdp", "sp", None),
        P("fsdp", "sp", None),
        P("fsdp"),
        P("fsdp", None),
        P("fsdp", None),
        P("fsdp", None),
        P("fsdp", None),
        P("fsdp"),
        P("fsdp", None),
        P("fsdp", None),
        P("fsdp", None),
        P("fsdp", "sp"),
        P("fsdp", None),
        P(),
    )
    return jax.shard_map(
        local,
        mesh=mesh,
        in_specs=placed,
        out_specs=(
            P("fsdp", "sp", None),
            P("fsdp", "sp", None),
            P("fsdp"),
            P("fsdp", None),
            P("fsdp", None),
            P("fsdp", None),
            P("fsdp", None),
            P("fsdp"),
            P("fsdp", None),
            P("fsdp", None),
            P("fsdp", None),
        ),
        check_vma=False,
    )
```

```python
import functools
import jax
import jax.numpy as jnp
from jax import lax
from jax.experimental import pallas as pl
from jax.experimental.pallas import tpu as pltpu
from jax.experimental.layout import Layout, with_layout_constraint
from jax.sharding import PartitionSpec as P

QUERY_HEADS = 32
KEY_VALUE_HEADS = 8
HEAD_SIZE = 80
LANES = 128


eps = 1e-05
theta = 1000000.0
log2e = 1.4426950408889634


def swap(value, bit):
    size = lax.axis_size("sp")
    return lax.ppermute(value, "sp", [(i, i ^ bit) for i in range(size)])


def row_major(value):
    return with_layout_constraint(value, Layout(major_to_minor=tuple(range(value.ndim))))


def gather_sp(value):
    size = lax.axis_size("sp")
    if size != 4:
        return lax.all_gather(value, "sp", axis=0, tiled=False)
    place = lax.axis_index("sp")
    half = value.shape[0] // 2
    first, second = value[:half], value[half:]
    x_first, y_second = swap(first, 1), swap(second, 2)
    x_second, y_first = swap(second, 1), swap(first, 2)
    far_first, far_second = swap(x_first, 2), swap(y_second, 1)
    out = jnp.zeros((size,) + value.shape, value.dtype)
    zeros = (0,) * (value.ndim - 1)
    for turn, low, high in (
        (0, first, second),
        (1, x_first, x_second),
        (2, y_first, y_second),
        (3, far_first, far_second),
    ):
        out = lax.dynamic_update_slice(out, low[None], (place ^ turn, 0) + zeros)
        out = lax.dynamic_update_slice(out, high[None], (place ^ turn, half) + zeros)
    return row_major(out)


def gather_small(value):
    size = lax.axis_size("sp")
    if size != 4:
        return lax.all_gather(value, "sp", axis=0, tiled=False)
    place = lax.axis_index("sp")
    pieces = [value] + [swap(value, turn) for turn in range(1, size)]
    here = [
        sum(jnp.where(place ^ turn == i, pieces[turn], 0) for turn in range(size)) for i in range(size)
    ]
    return jnp.stack(here, axis=0)


def scatter_sp(parts):
    size = lax.axis_size("sp")
    if size != 4:
        summed = lax.psum_scatter(parts, "sp", scatter_dimension=0, tiled=False)
        return summed.astype(jnp.float32), ((summed,), (summed,))
    place = lax.axis_index("sp")
    half = parts.shape[1] // 2
    parts = row_major(parts)

    def block(turn, lower):
        start = (place ^ turn, 0 if lower else half) + (0,) * (parts.ndim - 2)
        return lax.dynamic_slice(parts, start, (1, half) + parts.shape[2:])[0]

    wide = jnp.float32
    low = parts.dtype
    from_x, from_y = swap(block(3, True), 1), swap(block(3, False), 2)
    x_first, y_second = swap(block(1, True), 1), swap(block(2, False), 2)
    y_sent = (block(2, True).astype(wide) + from_x.astype(wide)).astype(low)
    x_sent = (block(1, False).astype(wide) + from_y.astype(wide)).astype(low)
    y_first, x_second = swap(y_sent, 2), swap(x_sent, 1)
    first = block(0, True).astype(wide) + x_first.astype(wide) + y_first.astype(wide)
    second = block(0, False).astype(wide) + x_second.astype(wide) + y_second.astype(wide)
    return jnp.concatenate([first, second], axis=0), ((y_sent, x_sent), (x_first, y_second))


def rotary_tables(positions):
    halves = HEAD_SIZE // 2
    frequency = theta ** (-(2.0 * jnp.arange(halves, dtype=jnp.float32)) / HEAD_SIZE)
    angles = positions.astype(jnp.float32)[:, None] * frequency[None, :]
    cosine, sine = jnp.cos(angles), jnp.sin(angles)
    rest = jnp.zeros((positions.shape[0], LANES - HEAD_SIZE), jnp.float32)
    return (
        jnp.concatenate([cosine, cosine, rest], axis=1),
        jnp.concatenate([-sine, sine, rest], axis=1),
    )


def dot(left, right):
    return jnp.dot(left, right, preferred_element_type=jnp.float32)


def dot_rows(left, right):
    return lax.dot_general(left, right, (((0,), (0,)), ((), ())), preferred_element_type=jnp.float32)


def dot_cols(left, right):
    return lax.dot_general(left, right, (((1,), (1,)), ((), ())), preferred_element_type=jnp.float32)


def head_of(matrix, head):
    first = head * HEAD_SIZE
    if first + LANES <= matrix.shape[1]:
        return matrix[:, first : first + LANES]
    kept = matrix[:, first : first + HEAD_SIZE]
    return jnp.concatenate([kept, jnp.zeros((kept.shape[0], LANES - HEAD_SIZE), kept.dtype)], axis=1)


def half_turn(padded):
    lane = lax.broadcasted_iota(jnp.int32, padded.shape, 1)
    half = HEAD_SIZE // 2
    return jnp.where(lane < half, pltpu.roll(padded, LANES - half, 1), pltpu.roll(padded, half, 1))


def qkv_kernel(heads, keys, x_ref, gain_ref, weight_ref, cos_ref, sin_ref, normed_ref, q_ref, k_ref, v_ref):
    x = x_ref[...].astype(jnp.float32)
    scale = lax.rsqrt(jnp.mean(x * x, axis=1, keepdims=True) + eps)
    normed = (x * scale * gain_ref[...]).astype(jnp.bfloat16)
    normed_ref[...] = normed
    rows = jnp.dot(normed, weight_ref[...], preferred_element_type=jnp.float32)
    cosine, sine = cos_ref[...], sin_ref[...]
    inside = lax.broadcasted_iota(jnp.int32, cosine.shape, 1) < HEAD_SIZE
    for i in range(heads + keys):
        v = head_of(rows, i)
        turned = (v * cosine + half_turn(v) * sine).astype(jnp.bfloat16)
        if i < heads:
            q_ref[:, i * LANES : (i + 1) * LANES] = turned
        else:
            k_ref[:, (i - heads) * LANES : (i - heads + 1) * LANES] = turned
    for i in range(keys):
        v = head_of(rows, heads + keys + i)
        v_ref[:, i * LANES : (i + 1) * LANES] = jnp.where(inside, v, 0.0).astype(jnp.bfloat16)


def qkv_call(x, gain, weight, cosine, sine, heads, keys):
    total, width = x.shape
    block = 256
    bf = jnp.bfloat16
    row = lambda n: pl.BlockSpec((block, n), lambda i: (i, 0))
    whole = lambda a: pl.BlockSpec(a.shape, lambda i: (0, 0))
    return pl.pallas_call(
        functools.partial(qkv_kernel, heads, keys),
        grid=(total // block,),
        in_specs=[row(width), whole(gain), whole(weight), row(LANES), row(LANES)],
        out_specs=[row(width), row(heads * LANES), row(keys * LANES), row(keys * LANES)],
        out_shape=[
            jax.ShapeDtypeStruct((total, width), bf),
            jax.ShapeDtypeStruct((total, heads * LANES), bf),
            jax.ShapeDtypeStruct((total, keys * LANES), bf),
            jax.ShapeDtypeStruct((total, keys * LANES), bf),
        ],
        compiler_params=pltpu.CompilerParams(vmem_limit_bytes=48 * 2**20),
        cost_estimate=pl.CostEstimate(
            flops=2 * total * width * weight.shape[1], bytes_accessed=20 * 2**20, transcendentals=0
        ),
    )(x, gain, weight, cosine, sine)


def attend_kernel(heads, keys, block, q_ref, k_ref, v_ref, start_ref, mixed_ref, lse_ref, bias_ref):
    total = q_ref.shape[0]
    group = heads // keys
    factor = HEAD_SIZE**-0.5 * log2e
    for i in range(total // block):
        first, stop = i * block, (i + 1) * block
        column = lax.broadcasted_iota(jnp.int32, (block, stop), 1)
        row = lax.broadcasted_iota(jnp.int32, (block, stop), 0) + first
        good = (column >= start_ref[first:stop, :]) & (column <= row)
        bias_ref[:, :stop] = jnp.where(good, 0.0, -1e30)
        for head in range(heads):
            lanes = slice(head * LANES, (head + 1) * LANES)
            key = slice(head // group * LANES, (head // group + 1) * LANES)
            scores = dot_cols(q_ref[first:stop, lanes], k_ref[:stop, key]) * factor + bias_ref[:, :stop]
            top = jnp.max(scores, axis=1, keepdims=True)
            weights = jnp.exp2(scores - top)
            summed = jnp.sum(weights, axis=1, keepdims=True)
            mixed = jnp.dot(
                weights.astype(jnp.bfloat16), v_ref[:stop, key], preferred_element_type=jnp.float32
            ) / summed
            mixed_ref[first:stop, head * HEAD_SIZE : (head + 1) * HEAD_SIZE] = mixed[:, :HEAD_SIZE].astype(
                jnp.bfloat16
            )
            lse_ref[first:stop, head : head + 1] = top + jnp.log2(summed)


def attend_call(q, k, v, start, block=256):
    total = q.shape[0]
    heads, keys = q.shape[1] // LANES, k.shape[1] // LANES
    return pl.pallas_call(
        functools.partial(attend_kernel, heads, keys, block),
        out_shape=[
            jax.ShapeDtypeStruct((total, heads * HEAD_SIZE), jnp.bfloat16),
            jax.ShapeDtypeStruct((total, heads), jnp.float32),
        ],
        scratch_shapes=[pltpu.VMEM((block, total), jnp.float32)],
        compiler_params=pltpu.CompilerParams(vmem_limit_bytes=56 * 2**20),
        cost_estimate=pl.CostEstimate(
            flops=heads * total * total * 512, bytes_accessed=8 * 2**20, transcendentals=heads * total * total // 2
        ),
    )(q, k, v, start)


def attend_back_kernel(
    heads, keys, block, q_ref, k_ref, v_ref, grad_ref, lse_ref, start_ref, cos_ref, sin_ref, out_ref, bias_ref, dk_ref, dv_ref
):
    total = q_ref.shape[0]
    group = heads // keys
    scale = HEAD_SIZE**-0.5
    factor = scale * log2e
    low = jnp.bfloat16
    dk_ref[...] = jnp.zeros_like(dk_ref)
    dv_ref[...] = jnp.zeros_like(dv_ref)
    inside = lax.broadcasted_iota(jnp.int32, (block, LANES), 1) < HEAD_SIZE
    half = HEAD_SIZE // 2

    def turned_back(w, rows):
        w = w.astype(low).astype(jnp.float32)
        scaled = w * sin_ref[rows, :]
        lane = lax.broadcasted_iota(jnp.int32, w.shape, 1)
        moved = jnp.where(lane < half, pltpu.roll(scaled, LANES - half, 1), pltpu.roll(scaled, half, 1))
        return (w * cos_ref[rows, :] + moved).astype(low)

    for i in range(total // block):
        first, stop = i * block, (i + 1) * block
        rows = slice(first, stop)
        key_place = lax.broadcasted_iota(jnp.int32, (stop, block), 0)
        place = lax.broadcasted_iota(jnp.int32, (stop, block), 1) + first
        good = (key_place >= start_ref[:, rows]) & (key_place <= place)
        bias_ref[:stop, :] = jnp.where(good, 0.0, -1e30)
        grads = grad_ref[rows, :].astype(jnp.float32)
        for head in range(heads):
            lanes = slice(head * LANES, (head + 1) * LANES)
            key = slice(head // group * LANES, (head // group + 1) * LANES)
            query = q_ref[rows, lanes]
            grad = jnp.where(inside, head_of(grads, head), 0.0).astype(low)
            scores = dot_cols(k_ref[:stop, key], query) * factor + bias_ref[:stop, :]
            probs = jnp.exp2(scores - lse_ref[head : head + 1, rows])
            dv_ref[:stop, key] += jnp.dot(probs.astype(low), grad, preferred_element_type=jnp.float32)
            d_probs = dot_cols(v_ref[:stop, key], grad)
            delta = jnp.sum(probs * d_probs, axis=0, keepdims=True)
            d_scores = (probs * (d_probs - delta)).astype(low)
            dk_ref[:stop, key] += jnp.dot(d_scores, query, preferred_element_type=jnp.float32)
            d_query = dot_rows(d_scores, k_ref[:stop, key]) * scale
            out_ref[rows, head * HEAD_SIZE : (head + 1) * HEAD_SIZE] = turned_back(d_query, rows)[:, :HEAD_SIZE]
    for i in range(total // block):
        rows = slice(i * block, (i + 1) * block)
        for j in range(keys):
            lanes = slice(j * LANES, (j + 1) * LANES)
            at = (heads + j) * HEAD_SIZE
            out_ref[rows, at : at + HEAD_SIZE] = turned_back(dk_ref[rows, lanes] * scale, rows)[:, :HEAD_SIZE]
            at = (heads + keys + j) * HEAD_SIZE
            out_ref[rows, at : at + HEAD_SIZE] = dv_ref[rows, lanes][:, :HEAD_SIZE].astype(low)


def attend_back_call(q, k, v, grad, lse_rows, start_row, cosine, sine_back, block=256):
    total = q.shape[0]
    heads, keys = q.shape[1] // LANES, k.shape[1] // LANES
    return pl.pallas_call(
        functools.partial(attend_back_kernel, heads, keys, block),
        out_shape=jax.ShapeDtypeStruct((total, (heads + 2 * keys) * HEAD_SIZE), jnp.bfloat16),
        scratch_shapes=[
            pltpu.VMEM((total, block), jnp.float32),
            pltpu.VMEM((total, keys * LANES), jnp.float32),
            pltpu.VMEM((total, keys * LANES), jnp.float32),
        ],
        compiler_params=pltpu.CompilerParams(vmem_limit_bytes=56 * 2**20),
        cost_estimate=pl.CostEstimate(
            flops=8000 * heads * total * total * 128, bytes_accessed=12 * 2**20, transcendentals=heads * total * total // 2
        ),
    )(q, k, v, grad, lse_rows, start_row, cosine, sine_back)

def gate_up_kernel(x_ref, gate_weight_ref, up_weight_ref, active_ref, gate_ref, up_ref):
    x = x_ref[...]
    gate = jnp.dot(x, gate_weight_ref[...], preferred_element_type=jnp.float32)
    upward = jnp.dot(x, up_weight_ref[...], preferred_element_type=jnp.float32)
    active_ref[...] = (gate / (1.0 + jnp.exp(-gate)) * upward).astype(jnp.bfloat16)
    gate_ref[...] = gate.astype(jnp.bfloat16)
    up_ref[...] = upward.astype(jnp.bfloat16)


def unit_block(units):
    return 256 if units % 256 == 0 else 128


def gate_up_call(x, weights):
    total, width = x.shape
    units = weights.shape[1] // 2
    block = unit_block(units)
    count = units // block
    out = pl.BlockSpec((total, block), lambda j: (0, j))
    return pl.pallas_call(
        gate_up_kernel,
        grid=(count,),
        in_specs=[
            pl.BlockSpec((total, width), lambda j: (0, 0)),
            pl.BlockSpec((width, block), lambda j: (0, j)),
            pl.BlockSpec((width, block), lambda j: (0, j + count)),
        ],
        out_specs=[out] * 3,
        out_shape=[jax.ShapeDtypeStruct((total, units), jnp.bfloat16)] * 3,
        compiler_params=pltpu.CompilerParams(vmem_limit_bytes=56 * 2**20),
        cost_estimate=pl.CostEstimate(
            flops=4 * total * width * units, bytes_accessed=45 * 2**20, transcendentals=0
        ),
    )(x, weights, weights)


def unit_back_kernel(incoming_ref, down_ref, gate_ref, up_ref, d_gate_ref, d_up_ref):
    d_active = dot_cols(incoming_ref[...], down_ref[...])
    gate = gate_ref[...].astype(jnp.float32)
    upward = up_ref[...].astype(jnp.float32)
    logistic = 1.0 / (1.0 + jnp.exp(-gate))
    d_gate_ref[...] = (d_active * upward * logistic * (1.0 + gate * (1.0 - logistic))).astype(jnp.bfloat16)
    d_up_ref[...] = (d_active * gate * logistic).astype(jnp.bfloat16)


def unit_back_call(incoming, down, gate, up):
    total, width = incoming.shape
    units = down.shape[0]
    block = unit_block(units)
    column = pl.BlockSpec((total, block), lambda j: (0, j))
    return pl.pallas_call(
        unit_back_kernel,
        grid=(units // block,),
        in_specs=[
            pl.BlockSpec((total, width), lambda j: (0, 0)),
            pl.BlockSpec((block, width), lambda j: (j, 0)),
            column,
            column,
        ],
        out_specs=[column] * 2,
        out_shape=[jax.ShapeDtypeStruct((total, units), jnp.bfloat16)] * 2,
        compiler_params=pltpu.CompilerParams(vmem_limit_bytes=56 * 2**20),
        cost_estimate=pl.CostEstimate(
            flops=2 * total * width * units, bytes_accessed=40 * 2**20, transcendentals=0
        ),
    )(incoming, down, gate, up)


def norm_back(d_normed, x, gain):
    scale = lax.rsqrt(jnp.mean(x * x, axis=1, keepdims=True) + eps)
    grad_gain = jnp.sum(d_normed * (x * scale), axis=0, keepdims=True)
    scaled = d_normed * gain
    inner = jnp.mean(scaled * x, axis=1, keepdims=True)
    return scale * scaled - x * (scale * scale * scale * inner), grad_gain


def add_up(ref, value):
    @pl.when(pl.program_id(0) == 0)
    def _():
        ref[...] = jnp.zeros_like(ref)

    ref[...] += value


def mlp_back_kernel(d_gate_ref, d_up_ref, weight_ref, x_ref, gain_ref, *refs):
    out_ref, grad_ref = refs[-2:]
    units = d_gate_ref.shape[1]
    d_normed = dot_cols(d_gate_ref[...], weight_ref[:, :units]) + dot_cols(
        d_up_ref[...], weight_ref[:, units:]
    )
    back, grad_gain = norm_back(d_normed, x_ref[...].astype(jnp.float32), gain_ref[...])
    parts, _, share = out_ref.shape
    for i in range(parts):
        out_ref[i] = back[:, i * share : (i + 1) * share].astype(jnp.bfloat16)
    add_up(grad_ref, grad_gain)


def mlp_back_call(d_gate, d_up, weights, x, gain, parts, *when):
    total, units = d_gate.shape
    width = x.shape[1]
    share = width // parts
    block = 512
    row = lambda n: pl.BlockSpec((block, n), lambda i: (i, 0))
    whole = lambda a: pl.BlockSpec(a.shape, lambda i: (0, 0), pipeline_mode=pl.Buffered(1))
    return pl.pallas_call(
        mlp_back_kernel,
        grid=(total // block,),
        in_specs=[row(units), row(units), whole(weights), row(width), whole(gain)]
        + [pl.BlockSpec(memory_space=pl.ANY)] * len(when),
        out_specs=[
            pl.BlockSpec((parts, block, share), lambda i: (0, i, 0)),
            pl.BlockSpec((1, width), lambda i: (0, 0)),
        ],
        out_shape=[
            jax.ShapeDtypeStruct((parts, total, share), jnp.bfloat16),
            jax.ShapeDtypeStruct((1, width), jnp.float32),
        ],
        compiler_params=pltpu.CompilerParams(vmem_limit_bytes=60 * 2**20),
        cost_estimate=pl.CostEstimate(
            flops=4 * total * width * units, bytes_accessed=45 * 2**20, transcendentals=0
        ),
    )(d_gate, d_up, weights, x, gain, *when)


def attend_norm_kernel(parts, place_ref, d_qkv_ref, weight_ref, x_ref, gain_ref, own_ref, *refs):
    out_ref, grad_ref = refs[-2:]
    d_normed = dot_cols(d_qkv_ref[...], weight_ref[:, : d_qkv_ref.shape[1]])
    back, grad_gain = norm_back(d_normed, x_ref[...].astype(jnp.float32), gain_ref[...])
    out_ref[...] = back.astype(jnp.bfloat16)
    share = own_ref.shape[1]
    for place in range(parts):

        @pl.when(place_ref[0] == place)
        def _():
            lanes = slice(place * share, (place + 1) * share)
            out_ref[:, lanes] = (back[:, lanes] + own_ref[...]).astype(jnp.bfloat16)

    add_up(grad_ref, grad_gain)


def attend_norm_call(place, d_qkv, weights, x, gain, own, parts, *when):
    total, width = x.shape
    block = 256
    row = lambda n: pl.BlockSpec((block, n), lambda i: (i, 0))
    whole = lambda a: pl.BlockSpec(a.shape, lambda i: (0, 0), pipeline_mode=pl.Buffered(1))
    return pl.pallas_call(
        functools.partial(attend_norm_kernel, parts),
        grid=(total // block,),
        in_specs=[
            pl.BlockSpec(memory_space=pltpu.SMEM),
            row(d_qkv.shape[1]),
            whole(weights),
            row(width),
            whole(gain),
            row(own.shape[1]),
        ]
        + [pl.BlockSpec(memory_space=pl.ANY)] * len(when),
        out_specs=[row(width), pl.BlockSpec((1, width), lambda i: (0, 0))],
        out_shape=[
            jax.ShapeDtypeStruct((total, width), jnp.bfloat16),
            jax.ShapeDtypeStruct((1, width), jnp.float32),
        ],
        compiler_params=pltpu.CompilerParams(vmem_limit_bytes=56 * 2**20),
        cost_estimate=pl.CostEstimate(
            flops=2 * total * width * d_qkv.shape[1], bytes_accessed=30 * 2**20, transcendentals=0
        ),
    )(place, d_qkv, weights, x, gain, own, *when)


def out_back_kernel(d_ref, weight_ref, *refs):
    refs[-1][0] = dot_cols(d_ref[...], weight_ref[...]).astype(jnp.bfloat16)


def out_back_call(d_branch, weights, parts, *when):
    total, share = d_branch.shape
    rows = weights.shape[0] // parts
    return pl.pallas_call(
        out_back_kernel,
        grid=(parts,),
        in_specs=[
            pl.BlockSpec((total, share), lambda i: (0, 0)),
            pl.BlockSpec((rows, share), lambda i: (i, 0)),
        ]
        + [pl.BlockSpec(memory_space=pl.ANY)] * len(when),
        out_specs=pl.BlockSpec((1, total, rows), lambda i: (i, 0, 0)),
        out_shape=jax.ShapeDtypeStruct((parts, total, rows), jnp.bfloat16),
        compiler_params=pltpu.CompilerParams(vmem_limit_bytes=32 * 2**20),
        cost_estimate=pl.CostEstimate(
            flops=2 * total * share * weights.shape[0], bytes_accessed=14 * 2**20, transcendentals=0
        ),
    )(d_branch, weights, *when)


def rows_kernel(left_ref, right_ref, *refs):
    refs[-1][...] = dot_rows(left_ref[...], right_ref[...]).astype(jnp.bfloat16)


def rows_call(left, right, *when):
    total, rows = left.shape
    columns = right.shape[1]
    block = 256 if columns % 256 == 0 else 128
    return pl.pallas_call(
        rows_kernel,
        grid=(columns // block,),
        in_specs=[
            pl.BlockSpec((total, rows), lambda j: (0, 0)),
            pl.BlockSpec((total, block), lambda j: (0, j)),
        ]
        + [pl.BlockSpec(memory_space=pl.ANY)] * len(when),
        out_specs=pl.BlockSpec((rows, block), lambda j: (0, j)),
        out_shape=jax.ShapeDtypeStruct((rows, columns), jnp.bfloat16),
        compiler_params=pltpu.CompilerParams(vmem_limit_bytes=56 * 2**20),
        cost_estimate=pl.CostEstimate(flops=0, bytes_accessed=0, transcendentals=0),
    )(left, right, *when)


def product_kernel(left_ref, right_ref, *refs):
    refs[-1][...] = jnp.dot(left_ref[...], right_ref[...], preferred_element_type=jnp.float32).astype(
        jnp.bfloat16
    )


def product_call(left, right, *when):
    total, depth = left.shape
    columns = right.shape[1]
    block = 256 if columns % 256 == 0 else 128
    return pl.pallas_call(
        product_kernel,
        grid=(columns // block,),
        in_specs=[
            pl.BlockSpec((total, depth), lambda j: (0, 0)),
            pl.BlockSpec((depth, block), lambda j: (0, j)),
        ]
        + [pl.BlockSpec(memory_space=pl.ANY)] * len(when),
        out_specs=pl.BlockSpec((total, block), lambda j: (0, j)),
        out_shape=jax.ShapeDtypeStruct((total, columns), jnp.bfloat16),
        compiler_params=pltpu.CompilerParams(vmem_limit_bytes=56 * 2**20),
        cost_estimate=pl.CostEstimate(flops=0, bytes_accessed=0, transcendentals=0),
    )(left, right, *when)


def qkv_grad_kernel(normed_ref, d_qkv_ref, gain_ref, out_ref):
    columns = d_qkv_ref.shape[1]
    out_ref[:, :columns] = dot_rows(normed_ref[...], d_qkv_ref[...]).astype(jnp.bfloat16)
    rest = jnp.transpose(gain_ref[...])
    fill = out_ref.shape[1] - columns - rest.shape[1]
    if fill:
        rest = jnp.concatenate([rest, jnp.zeros((rest.shape[0], fill), rest.dtype)], axis=1)
    out_ref[:, columns:] = rest.astype(jnp.bfloat16)


def qkv_grad_call(normed, d_qkv, gain_grads, columns):
    total, width = normed.shape
    block = 512
    return pl.pallas_call(
        qkv_grad_kernel,
        grid=(width // block,),
        in_specs=[
            pl.BlockSpec((total, block), lambda i: (0, i)),
            pl.BlockSpec(d_qkv.shape, lambda i: (0, 0)),
            pl.BlockSpec((gain_grads.shape[0], block), lambda i: (0, i)),
        ],
        out_specs=pl.BlockSpec((block, columns), lambda i: (i, 0)),
        out_shape=jax.ShapeDtypeStruct((width, columns), jnp.bfloat16),
        compiler_params=pltpu.CompilerParams(vmem_limit_bytes=48 * 2**20),
        cost_estimate=pl.CostEstimate(flops=0, bytes_accessed=0, transcendentals=0),
    )(normed, d_qkv, gain_grads)


def pieces_sp(value):
    return [value] + [swap(value, turn) for turn in range(1, lax.axis_size("sp"))]


def spread_kernel(layout, count, place_ref, *refs):
    pieces, outs = refs[:count], refs[count:]
    for place in range(count):

        @pl.when(place_ref[0] == place)
        def _():
            for part in range(count):
                for first, width, out, at, step in layout:
                    goal = at + part * step
                    outs[out][:, goal : goal + width] = pieces[place ^ part][:, first : first + width].astype(
                        jnp.float32
                    )


def spread_call(place, pieces, layout, widths):
    rows, columns = pieces[0].shape
    block = rows // 5 if rows % 80 == 0 else rows
    return pl.pallas_call(
        functools.partial(spread_kernel, layout, len(pieces)),
        grid=(rows // block,),
        in_specs=[pl.BlockSpec(memory_space=pltpu.SMEM)]
        + [pl.BlockSpec((block, columns), lambda i: (i, 0))] * len(pieces),
        out_specs=[pl.BlockSpec((block, w), lambda i: (i, 0)) for w in widths],
        out_shape=[jax.ShapeDtypeStruct((rows, w), jnp.float32) for w in widths],
        compiler_params=pltpu.CompilerParams(vmem_limit_bytes=40 * 2**20),
        cost_estimate=pl.CostEstimate(
            flops=0, bytes_accessed=6 * len(pieces) * rows * columns, transcendentals=0
        ),
    )(place, *pieces)


def stack_kernel(count, place_ref, *refs):
    for turn in range(count):
        refs[count][place_ref[0] ^ turn] = refs[turn][...].astype(jnp.float32)


def stack_call(place, pieces):
    rows, columns = pieces[0].shape
    block = 32 if rows % 32 == 0 else rows
    count = len(pieces)
    return pl.pallas_call(
        functools.partial(stack_kernel, count),
        grid=(rows // block,),
        in_specs=[pl.BlockSpec(memory_space=pltpu.SMEM)]
        + [pl.BlockSpec((block, columns), lambda i: (i, 0))] * count,
        out_specs=pl.BlockSpec((count, block, columns), lambda i: (0, i, 0)),
        out_shape=jax.ShapeDtypeStruct((count, rows, columns), jnp.float32),
        compiler_params=pltpu.CompilerParams(vmem_limit_bytes=40 * 2**20),
        cost_estimate=pl.CostEstimate(flops=0, bytes_accessed=6 * count * rows * columns, transcendentals=0),
    )(place, *pieces).reshape(count * rows, columns)


def pass_kernel(*refs):
    pass


def after(value, *others):
    here = pl.BlockSpec(memory_space=pl.ANY)
    return pl.pallas_call(
        pass_kernel,
        in_specs=[here] * (1 + len(others)),
        out_specs=here,
        out_shape=jax.ShapeDtypeStruct(value.shape, value.dtype),
        input_output_aliases={0: 0},
        cost_estimate=pl.CostEstimate(flops=0, bytes_accessed=0, transcendentals=0),
    )(value, *others)


def pack_kernel(groups, parts, place_ref, gate_ref, up_ref, _, out_ref):
    rows, columns = gate_ref.shape
    share = columns // (groups * parts)
    for place in range(parts):

        @pl.when(place_ref[0] == place)
        def _():
            for i, ref in enumerate((gate_ref, up_ref)):
                for j in range(groups):
                    at = (i * groups + j) * share
                    begin = (j * parts + place) * share
                    out_ref[:, at : at + share] = ref[:, begin : begin + share]


def pack_call(place, gate, up, when, groups, parts):
    rows, columns = gate.shape
    block = rows // 5 if rows % 80 == 0 else rows
    spec = pl.BlockSpec((block, columns), lambda i: (i, 0))
    return pl.pallas_call(
        functools.partial(pack_kernel, groups, parts),
        grid=(rows // block,),
        in_specs=[
            pl.BlockSpec(memory_space=pltpu.SMEM),
            spec,
            spec,
            pl.BlockSpec(memory_space=pl.ANY),
        ],
        out_specs=pl.BlockSpec((block, 2 * columns // parts), lambda i: (i, 0)),
        out_shape=jax.ShapeDtypeStruct((rows, 2 * columns // parts), gate.dtype),
        compiler_params=pltpu.CompilerParams(vmem_limit_bytes=32 * 2**20),
        cost_estimate=pl.CostEstimate(flops=0, bytes_accessed=5 * rows * columns, transcendentals=0),
    )(place, gate, up, when)


def local(
    tokens,
    cotangent,
    attn_gain,
    w_query,
    key_weight,
    value_weight,
    w_out,
    mlp_gain,
    w_gate,
    w_up,
    w_down,
    positions,
    lengths,
    deal_slots,
):
    groups = lax.axis_size("fsdp")
    parts = lax.axis_size("sp")
    width = tokens.shape[-1]
    rows = tokens.shape[1]
    fsdp_place = lax.axis_index("fsdp")
    sp_place = lax.axis_index("sp")
    low = jnp.bfloat16
    wide = jnp.float32

    lanes = jnp.arange(groups, dtype=jnp.int32)
    own_row = deal_slots[fsdp_place, sp_place]
    target = own_row // groups
    pick_send = jnp.sum(jnp.where(target[None, :] == lanes[:, None], lanes[None, :], 0), axis=1)
    column = deal_slots[:, sp_place, :]
    arrived_slot = jnp.sum(jnp.where(column // groups == fsdp_place, column % groups, 0), axis=1)
    pick_place = jnp.sum(
        jnp.where(arrived_slot[None, :] == lanes[:, None], lanes[None, :], 0), axis=1
    )

    def picked(given):
        return jnp.take(given.reshape(groups, -1, width), pick_send, axis=0)

    def deal(blocks):
        return lax.all_to_all(blocks, "fsdp", split_axis=0, concat_axis=0, tiled=True)

    def in_place(came):
        return jnp.take(came, pick_place, axis=0).reshape(rows, width)

    def to_given(owned):
        blocks = jnp.take(owned.reshape(groups, -1, width), arrived_slot, axis=0)
        gone = lax.all_to_all(blocks, "fsdp", split_axis=0, concat_axis=0, tiled=True)
        return jnp.take(gone, target, axis=0).reshape(tokens.shape)

    def column_share(weight):
        share = weight.shape[1] // parts
        return lax.dynamic_slice_in_dim(weight, sp_place * share, share, axis=1)

    def gather_fsdp(shard):
        return lax.all_gather(shard, "fsdp", axis=0, tiled=True)

    ff_rows = w_down.shape[0]
    ff_share = ff_rows // parts

    query_cols = w_query.shape[1] // parts
    key_cols = key_weight.shape[1] // parts
    qkv_cols = query_cols + 2 * key_cols
    extra = -qkv_cols % 128
    extra = extra if extra else 128
    gains = jnp.pad(jnp.stack([attn_gain, mlp_gain], axis=1), ((0, 0), (0, extra - 2)))
    place = sp_place.reshape(1)
    came_tokens = deal(picked(tokens))
    gate_up_shard = pack_call(place, w_gate, w_up, came_tokens, groups, parts)
    qkv_shard = jnp.concatenate(
        [column_share(w_query), column_share(key_weight), column_share(value_weight), gains], axis=1
    )
    qkv_all = gather_fsdp(qkv_shard)
    out_all = gather_fsdp(column_share(w_out))
    gate_up_all = gather_fsdp(gate_up_shard)
    down_all = gather_fsdp(lax.dynamic_slice_in_dim(w_down, sp_place * ff_share, ff_share, axis=0))
    qkv_weight = qkv_all[:, :qkv_cols]
    gain_one = qkv_all[:, qkv_cols].astype(wide)[None, :]
    gain_two = qkv_all[:, qkv_cols + 1].astype(wide)[None, :]

    group_inputs = gather_sp(in_place(came_tokens)).reshape(-1, width)
    came_incoming = deal(after(picked(cotangent), group_inputs))
    group_positions = gather_small(positions.reshape(-1)).reshape(-1)
    total = group_inputs.shape[0]

    cosine, sine = rotary_tables(group_positions)
    heads, keys = query_cols // HEAD_SIZE, key_cols // HEAD_SIZE
    normed, query_low, key_low, value_low = qkv_call(
        group_inputs, gain_one, qkv_all, cosine, sine, heads, keys
    )
    sizes = lengths.reshape(-1)
    ends = jnp.cumsum(sizes)
    places = jnp.arange(total, dtype=jnp.int32)
    start = jnp.sum(jnp.where(places[:, None] >= ends[None, :], sizes[None, :], 0), axis=1)
    own_mixed, logs = attend_call(query_low, key_low, value_low, start[:, None])

    def side_by_side(stacked):
        return jnp.concatenate([stacked[i] for i in range(parts)], axis=1)

    share = width // parts

    def own_columns(matrix):
        return lax.dynamic_slice_in_dim(matrix, sp_place * share, share, axis=1)

    mixed = side_by_side(gather_sp(own_mixed))
    own_hidden = own_columns(group_inputs).astype(wide) + dot(mixed, out_all)
    hidden_low = side_by_side(gather_sp(own_hidden.astype(low)))

    group_incoming = gather_sp(after(in_place(came_incoming), hidden_low)).reshape(-1, width)

    hidden = hidden_low.astype(wide)
    rms_two = lax.rsqrt(jnp.mean(hidden * hidden, axis=-1, keepdims=True) + eps)
    normed_two = (hidden * rms_two * gain_two).astype(low)
    active_low, gate, upward = gate_up_call(normed_two, gate_up_all)
    grad_down = rows_call(active_low, group_incoming)
    down_all = after(down_all, grad_down)
    d_gate, d_up = unit_back_call(group_incoming, down_all, gate, upward)
    grad_gate = rows_call(normed_two, d_gate)
    back_two, grad_gain_two = mlp_back_call(
        d_gate, d_up, gate_up_all, hidden_low, gain_two, parts, grad_gate
    )
    from_others, _ = scatter_sp(back_two)
    grad_up = rows_call(normed_two, d_up, back_two)
    own_d_hidden = own_columns(group_incoming).astype(wide) + from_others
    d_branch = own_d_hidden.astype(low)
    grad_up = after(grad_up, d_branch)
    d_mixed, (sums_mixed, _) = scatter_sp(out_back_call(d_branch, out_all, parts, grad_up))
    d_mixed = d_mixed.astype(low)
    grad_out = rows_call(mixed, d_branch)
    result_part = product_call(active_low, down_all, grad_out, *sums_mixed)
    own_hidden_rows = lax.dynamic_slice_in_dim(hidden_low, sp_place * rows, rows, axis=0)
    result_sum, (sums_result, _) = scatter_sp(after(result_part, d_mixed).reshape(parts, rows, width))
    layer_out = to_given((own_hidden_rows.astype(wide) + result_sum).astype(low))

    d_qkv = attend_back_call(
        query_low, key_low, value_low, d_mixed, logs.T, start[None, :], cosine, sine
    )
    back_one, grad_gain_one = attend_norm_call(
        place, d_qkv, qkv_all, group_inputs, gain_one, own_d_hidden, parts, *sums_result
    )
    gain_grads = jnp.concatenate(
        [grad_gain_one, grad_gain_two, jnp.zeros((6, width), wide)], axis=0
    )
    grad_qkv = qkv_grad_call(normed, d_qkv, gain_grads, qkv_all.shape[1])
    d_inputs = scatter_sp(back_one.reshape(parts, rows, width))[0]
    input_grad = to_given(d_inputs.astype(low))

    def scatter_fsdp(matrix):
        return lax.psum_scatter(matrix.astype(low), "fsdp", scatter_dimension=0, tiled=True)

    down_sum = scatter_fsdp(grad_down)
    gate_sum = scatter_fsdp(grad_gate)
    up_sum = scatter_fsdp(grad_up)
    out_sum = scatter_fsdp(grad_out)
    qkv_sum = scatter_fsdp(grad_qkv)

    down_pieces = pieces_sp(down_sum)
    gate_pieces = pieces_sp(after(gate_sum, *down_pieces[1:]))
    up_pieces = pieces_sp(after(up_sum, *gate_pieces[1:]))
    out_pieces = pieces_sp(after(out_sum, *up_pieces[1:]))
    qkv_pieces = pieces_sp(after(qkv_sum, *out_pieces[1:]))

    down_shard = stack_call(place, down_pieces)
    hidden_layout = [
        (j * ff_share, ff_share, 0, j * parts * ff_share, ff_share) for j in range(groups)
    ]
    (gate_shard,) = spread_call(place, gate_pieces, hidden_layout, [w_gate.shape[1]])
    (up_shard,) = spread_call(place, up_pieces, hidden_layout, [w_up.shape[1]])
    (out_shard,) = spread_call(place, out_pieces, [(0, share, 0, 0, share)], [width])
    qkv_layout = [
        (0, query_cols, 0, 0, query_cols),
        (query_cols, key_cols, 1, 0, key_cols),
        (query_cols + key_cols, key_cols, 2, 0, key_cols),
        (qkv_cols, 2, 3, 0, 2),
    ]
    query_shard, key_shard, value_shard, gain_parts = spread_call(
        place,
        qkv_pieces,
        qkv_layout,
        [w_query.shape[1], key_weight.shape[1], value_weight.shape[1], 2 * parts],
    )
    gain_shards = jnp.sum(gain_parts.reshape(-1, parts, 2), axis=1)
    return (
        layer_out,
        input_grad,
        gain_shards[:, 0],
        query_shard,
        key_shard,
        value_shard,
        out_shard,
        gain_shards[:, 1],
        gate_shard,
        up_shard,
        down_shard,
    )


def solution(mesh):
    placed = (
        P("fsdp", "sp", None),
        P("fsdp", "sp", None),
        P("fsdp"),
        P("fsdp", None),
        P("fsdp", None),
        P("fsdp", None),
        P("fsdp", None),
        P("fsdp"),
        P("fsdp", None),
        P("fsdp", None),
        P("fsdp", None),
        P("fsdp", "sp"),
        P("fsdp", None),
        P(),
    )
    return jax.shard_map(
        local,
        mesh=mesh,
        in_specs=placed,
        out_specs=(
            P("fsdp", "sp", None),
            P("fsdp", "sp", None),
            P("fsdp"),
            P("fsdp", None),
            P("fsdp", None),
            P("fsdp", None),
            P("fsdp", None),
            P("fsdp"),
            P("fsdp", None),
            P("fsdp", None),
            P("fsdp", None),
        ),
        check_vma=False,
    )
```

```python
import functools
import jax
import jax.numpy as jnp
from jax import lax
from jax.experimental import pallas as pl
from jax.experimental.pallas import tpu as pltpu
from jax.experimental.layout import Layout, with_layout_constraint
from jax.sharding import PartitionSpec as P

QUERY_HEADS = 32
KEY_VALUE_HEADS = 8
HEAD_SIZE = 80
LANES = 128


eps = 1e-05
theta = 1000000.0
log2e = 1.4426950408889634


def swap(value, bit):
    size = lax.axis_size("sp")
    return lax.ppermute(value, "sp", [(i, i ^ bit) for i in range(size)])


def row_major(value):
    return with_layout_constraint(value, Layout(major_to_minor=tuple(range(value.ndim))))


def gather_sp(value, *hold):
    size = lax.axis_size("sp")
    if size != 4:
        whole = lax.all_gather(value, "sp", axis=0, tiled=False)
        return whole, (whole,)
    place = lax.axis_index("sp")
    half = value.shape[0] // 2
    first, second = value[:half], value[half:]
    x_first, y_second = swap(first, 1), swap(second, 2)
    x_second, y_first = swap(second, 1), swap(first, 2)
    far_first, far_second = swap(x_first, 2), swap(y_second, 1)
    out = jnp.zeros((size,) + value.shape, value.dtype)
    if hold:
        out = after(out, *hold)
    zeros = (0,) * (value.ndim - 1)
    for turn, low, high in (
        (0, first, second),
        (1, x_first, x_second),
        (2, y_first, y_second),
        (3, far_first, far_second),
    ):
        out = lax.dynamic_update_slice(out, low[None], (place ^ turn, 0) + zeros)
        out = lax.dynamic_update_slice(out, high[None], (place ^ turn, half) + zeros)
    return row_major(out), (x_first, y_second)


def rows_of(blocks, picks):
    return blocks.at[picks].get(mode="promise_in_bounds")


def gather_small(value):
    size = lax.axis_size("sp")
    if size != 4:
        return lax.all_gather(value, "sp", axis=0, tiled=False)
    place = lax.axis_index("sp")
    pieces = [value] + [swap(value, turn) for turn in range(1, size)]
    here = [
        sum(jnp.where(place ^ turn == i, pieces[turn], 0) for turn in range(size)) for i in range(size)
    ]
    return jnp.stack(here, axis=0)


def scatter_sp(parts, *hold):
    size = lax.axis_size("sp")
    if size != 4:
        summed = lax.psum_scatter(parts, "sp", scatter_dimension=0, tiled=False)
        return summed.astype(jnp.float32), ((summed,), (summed,))
    place = lax.axis_index("sp")
    half = parts.shape[1] // 2
    parts = row_major(parts)

    def block(turn, lower):
        start = (place ^ turn, 0 if lower else half) + (0,) * (parts.ndim - 2)
        return lax.dynamic_slice(parts, start, (1, half) + parts.shape[2:])[0]

    wide = jnp.float32
    low = parts.dtype
    from_x, from_y = swap(block(3, True), 1), swap(block(3, False), 2)
    if hold:
        from_x = after(from_x, *hold)
    x_first, y_second = swap(block(1, True), 1), swap(block(2, False), 2)
    y_sent = (block(2, True).astype(wide) + from_x.astype(wide)).astype(low)
    x_sent = (block(1, False).astype(wide) + from_y.astype(wide)).astype(low)
    y_first, x_second = swap(y_sent, 2), swap(x_sent, 1)
    first = block(0, True).astype(wide) + x_first.astype(wide) + y_first.astype(wide)
    second = block(0, False).astype(wide) + x_second.astype(wide) + y_second.astype(wide)
    return jnp.concatenate([first, second], axis=0), ((y_sent, x_sent), (x_first, y_second))


def rotary_tables(positions):
    halves = HEAD_SIZE // 2
    frequency = theta ** (-(2.0 * jnp.arange(halves, dtype=jnp.float32)) / HEAD_SIZE)
    angles = positions.astype(jnp.float32)[:, None] * frequency[None, :]
    cosine, sine = jnp.cos(angles), jnp.sin(angles)
    rest = jnp.zeros((positions.shape[0], LANES - HEAD_SIZE), jnp.float32)
    return (
        jnp.concatenate([cosine, cosine, rest], axis=1),
        jnp.concatenate([-sine, sine, rest], axis=1),
    )


def dot(left, right):
    return jnp.dot(left, right, preferred_element_type=jnp.float32)


def dot_rows(left, right):
    return lax.dot_general(left, right, (((0,), (0,)), ((), ())), preferred_element_type=jnp.float32)


def dot_cols(left, right):
    return lax.dot_general(left, right, (((1,), (1,)), ((), ())), preferred_element_type=jnp.float32)


def head_of(matrix, head):
    first = head * HEAD_SIZE
    if first + LANES <= matrix.shape[1]:
        return matrix[:, first : first + LANES]
    kept = matrix[:, first : first + HEAD_SIZE]
    return jnp.concatenate([kept, jnp.zeros((kept.shape[0], LANES - HEAD_SIZE), kept.dtype)], axis=1)


def half_turn(padded):
    lane = lax.broadcasted_iota(jnp.int32, padded.shape, 1)
    half = HEAD_SIZE // 2
    return jnp.where(lane < half, pltpu.roll(padded, LANES - half, 1), pltpu.roll(padded, half, 1))


def qkv_kernel(heads, keys, x_ref, gain_ref, weight_ref, cos_ref, sin_ref, normed_ref, q_ref, k_ref, v_ref):
    x = x_ref[...].astype(jnp.float32)
    scale = lax.rsqrt(jnp.mean(x * x, axis=1, keepdims=True) + eps)
    normed = (x * scale * gain_ref[...]).astype(jnp.bfloat16)
    normed_ref[...] = normed
    rows = jnp.dot(normed, weight_ref[...], preferred_element_type=jnp.float32)
    cosine, sine = cos_ref[...], sin_ref[...]
    inside = lax.broadcasted_iota(jnp.int32, cosine.shape, 1) < HEAD_SIZE
    for i in range(heads + keys):
        v = head_of(rows, i)
        turned = (v * cosine + half_turn(v) * sine).astype(jnp.bfloat16)
        if i < heads:
            q_ref[:, i * LANES : (i + 1) * LANES] = turned
        else:
            k_ref[:, (i - heads) * LANES : (i - heads + 1) * LANES] = turned
    for i in range(keys):
        v = head_of(rows, heads + keys + i)
        v_ref[:, i * LANES : (i + 1) * LANES] = jnp.where(inside, v, 0.0).astype(jnp.bfloat16)


def qkv_call(x, gain, weight, cosine, sine, heads, keys):
    total, width = x.shape
    block = 256
    bf = jnp.bfloat16
    row = lambda n: pl.BlockSpec((block, n), lambda i: (i, 0))
    whole = lambda a: pl.BlockSpec(a.shape, lambda i: (0, 0))
    return pl.pallas_call(
        functools.partial(qkv_kernel, heads, keys),
        grid=(total // block,),
        in_specs=[row(width), whole(gain), whole(weight), row(LANES), row(LANES)],
        out_specs=[row(width), row(heads * LANES), row(keys * LANES), row(keys * LANES)],
        out_shape=[
            jax.ShapeDtypeStruct((total, width), bf),
            jax.ShapeDtypeStruct((total, heads * LANES), bf),
            jax.ShapeDtypeStruct((total, keys * LANES), bf),
            jax.ShapeDtypeStruct((total, keys * LANES), bf),
        ],
        compiler_params=pltpu.CompilerParams(vmem_limit_bytes=48 * 2**20),
        cost_estimate=pl.CostEstimate(
            flops=72 * 10**9, bytes_accessed=0, transcendentals=0
        ),
    )(x, gain, weight, cosine, sine)


def attend_kernel(heads, keys, block, q_ref, k_ref, v_ref, start_ref, *refs):
    mixed_ref, lse_ref, bias_ref = refs[-3:]
    total = q_ref.shape[0]
    group = heads // keys
    factor = HEAD_SIZE**-0.5 * log2e
    for i in range(total // block):
        first, stop = i * block, (i + 1) * block
        column = lax.broadcasted_iota(jnp.int32, (block, stop), 1)
        row = lax.broadcasted_iota(jnp.int32, (block, stop), 0) + first
        good = (column >= start_ref[first:stop, :]) & (column <= row)
        bias_ref[:, :stop] = jnp.where(good, 0.0, -1e30)
        for head in range(heads):
            lanes = slice(head * LANES, (head + 1) * LANES)
            key = slice(head // group * LANES, (head // group + 1) * LANES)
            scores = dot_cols(q_ref[first:stop, lanes], k_ref[:stop, key]) * factor + bias_ref[:, :stop]
            top = jnp.max(scores, axis=1, keepdims=True)
            weights = jnp.exp2(scores - top)
            summed = jnp.sum(weights, axis=1, keepdims=True)
            mixed = jnp.dot(
                weights.astype(jnp.bfloat16), v_ref[:stop, key], preferred_element_type=jnp.float32
            ) / summed
            mixed_ref[first:stop, head * HEAD_SIZE : (head + 1) * HEAD_SIZE] = mixed[:, :HEAD_SIZE].astype(
                jnp.bfloat16
            )
            lse_ref[first:stop, head : head + 1] = top + jnp.log2(summed)


def attend_call(q, k, v, start, *when):
    block = 256
    total = q.shape[0]
    heads, keys = q.shape[1] // LANES, k.shape[1] // LANES
    return pl.pallas_call(
        functools.partial(attend_kernel, heads, keys, block),
        in_specs=[pl.BlockSpec(memory_space=pltpu.VMEM)] * 4
        + [pl.BlockSpec(memory_space=pl.ANY)] * len(when),
        out_shape=[
            jax.ShapeDtypeStruct((total, heads * HEAD_SIZE), jnp.bfloat16),
            jax.ShapeDtypeStruct((total, heads), jnp.float32),
        ],
        scratch_shapes=[pltpu.VMEM((block, total), jnp.float32)],
        compiler_params=pltpu.CompilerParams(vmem_limit_bytes=56 * 2**20),
        cost_estimate=pl.CostEstimate(
            flops=84 * 10**9, bytes_accessed=0, transcendentals=0
        ),
    )(q, k, v, start, *when)


def attend_back_kernel(
    heads, keys, block, q_ref, k_ref, v_ref, grad_ref, lse_ref, start_ref, cos_ref, sin_ref, *refs
):
    out_ref, bias_ref, dk_ref, dv_ref = refs[-4:]
    total = q_ref.shape[0]
    group = heads // keys
    scale = HEAD_SIZE**-0.5
    factor = scale * log2e
    low = jnp.bfloat16
    dk_ref[...] = jnp.zeros_like(dk_ref)
    dv_ref[...] = jnp.zeros_like(dv_ref)
    inside = lax.broadcasted_iota(jnp.int32, (block, LANES), 1) < HEAD_SIZE
    half = HEAD_SIZE // 2

    def turned_back(w, rows):
        w = w.astype(low).astype(jnp.float32)
        scaled = w * sin_ref[rows, :]
        lane = lax.broadcasted_iota(jnp.int32, w.shape, 1)
        moved = jnp.where(lane < half, pltpu.roll(scaled, LANES - half, 1), pltpu.roll(scaled, half, 1))
        return (w * cos_ref[rows, :] + moved).astype(low)

    for i in range(total // block):
        first, stop = i * block, (i + 1) * block
        rows = slice(first, stop)
        key_place = lax.broadcasted_iota(jnp.int32, (stop, block), 0)
        place = lax.broadcasted_iota(jnp.int32, (stop, block), 1) + first
        good = (key_place >= start_ref[:, rows]) & (key_place <= place)
        bias_ref[:stop, :] = jnp.where(good, 0.0, -1e30)
        grads = grad_ref[rows, :].astype(jnp.float32)
        for head in range(heads):
            lanes = slice(head * LANES, (head + 1) * LANES)
            key = slice(head // group * LANES, (head // group + 1) * LANES)
            query = q_ref[rows, lanes]
            grad = jnp.where(inside, head_of(grads, head), 0.0).astype(low)
            scores = dot_cols(k_ref[:stop, key], query) * factor + bias_ref[:stop, :]
            probs = jnp.exp2(scores - lse_ref[head : head + 1, rows])
            dv_ref[:stop, key] += jnp.dot(probs.astype(low), grad, preferred_element_type=jnp.float32)
            d_probs = dot_cols(v_ref[:stop, key], grad)
            delta = jnp.sum(probs * d_probs, axis=0, keepdims=True)
            d_scores = (probs * (d_probs - delta)).astype(low)
            dk_ref[:stop, key] += jnp.dot(d_scores, query, preferred_element_type=jnp.float32)
            d_query = dot_rows(d_scores, k_ref[:stop, key]) * scale
            out_ref[rows, head * HEAD_SIZE : (head + 1) * HEAD_SIZE] = turned_back(d_query, rows)[:, :HEAD_SIZE]
    for i in range(total // block):
        rows = slice(i * block, (i + 1) * block)
        for j in range(keys):
            lanes = slice(j * LANES, (j + 1) * LANES)
            at = (heads + j) * HEAD_SIZE
            out_ref[rows, at : at + HEAD_SIZE] = turned_back(dk_ref[rows, lanes] * scale, rows)[:, :HEAD_SIZE]
            at = (heads + keys + j) * HEAD_SIZE
            out_ref[rows, at : at + HEAD_SIZE] = dv_ref[rows, lanes][:, :HEAD_SIZE].astype(low)


def attend_back_call(q, k, v, grad, lse_rows, start_row, cosine, sine_back, *when):
    block = 256
    total = q.shape[0]
    heads, keys = q.shape[1] // LANES, k.shape[1] // LANES
    return pl.pallas_call(
        functools.partial(attend_back_kernel, heads, keys, block),
        in_specs=[pl.BlockSpec(memory_space=pltpu.VMEM)] * 8
        + [pl.BlockSpec(memory_space=pl.ANY)] * len(when),
        out_shape=jax.ShapeDtypeStruct((total, (heads + 2 * keys) * HEAD_SIZE), jnp.bfloat16),
        scratch_shapes=[
            pltpu.VMEM((total, block), jnp.float32),
            pltpu.VMEM((total, keys * LANES), jnp.float32),
            pltpu.VMEM((total, keys * LANES), jnp.float32),
        ],
        compiler_params=pltpu.CompilerParams(vmem_limit_bytes=56 * 2**20),
        cost_estimate=pl.CostEstimate(
            flops=150 * 10**9, bytes_accessed=0, transcendentals=0
        ),
    )(q, k, v, grad, lse_rows, start_row, cosine, sine_back, *when)

def gate_up_kernel(x_ref, gate_weight_ref, up_weight_ref, active_ref, gate_ref, up_ref):
    x = x_ref[...]
    gate = jnp.dot(x, gate_weight_ref[...], preferred_element_type=jnp.float32)
    upward = jnp.dot(x, up_weight_ref[...], preferred_element_type=jnp.float32)
    active_ref[...] = (gate / (1.0 + jnp.exp(-gate)) * upward).astype(jnp.bfloat16)
    gate_ref[...] = gate.astype(jnp.bfloat16)
    up_ref[...] = upward.astype(jnp.bfloat16)


def unit_block(units):
    return 256 if units % 256 == 0 else 128


def gate_up_call(x, weights):
    total, width = x.shape
    units = weights.shape[1] // 2
    block = unit_block(units)
    count = units // block
    out = pl.BlockSpec((total, block), lambda j: (0, j))
    return pl.pallas_call(
        gate_up_kernel,
        grid=(count,),
        in_specs=[
            pl.BlockSpec((total, width), lambda j: (0, 0)),
            pl.BlockSpec((width, block), lambda j: (0, j)),
            pl.BlockSpec((width, block), lambda j: (0, j + count)),
        ],
        out_specs=[out] * 3,
        out_shape=[jax.ShapeDtypeStruct((total, units), jnp.bfloat16)] * 3,
        compiler_params=pltpu.CompilerParams(vmem_limit_bytes=56 * 2**20),
        cost_estimate=pl.CostEstimate(
            flops=111 * 10**9, bytes_accessed=0, transcendentals=0
        ),
    )(x, weights, weights)


def unit_back_kernel(incoming_ref, down_ref, gate_ref, up_ref, *refs):
    d_gate_ref, d_up_ref = refs[-2:]
    d_active = dot_cols(incoming_ref[...], down_ref[...])
    gate = gate_ref[...].astype(jnp.float32)
    upward = up_ref[...].astype(jnp.float32)
    logistic = 1.0 / (1.0 + jnp.exp(-gate))
    d_gate_ref[...] = (d_active * upward * logistic * (1.0 + gate * (1.0 - logistic))).astype(jnp.bfloat16)
    d_up_ref[...] = (d_active * gate * logistic).astype(jnp.bfloat16)


def unit_back_call(incoming, down, gate, up, *when):
    total, width = incoming.shape
    units = down.shape[0]
    block = unit_block(units)
    column = pl.BlockSpec((total, block), lambda j: (0, j))
    return pl.pallas_call(
        unit_back_kernel,
        grid=(units // block,),
        in_specs=[
            pl.BlockSpec((total, width), lambda j: (0, 0)),
            pl.BlockSpec((block, width), lambda j: (j, 0)),
            column,
            column,
        ]
        + [pl.BlockSpec(memory_space=pl.ANY)] * len(when),
        out_specs=[column] * 2,
        out_shape=[jax.ShapeDtypeStruct((total, units), jnp.bfloat16)] * 2,
        compiler_params=pltpu.CompilerParams(vmem_limit_bytes=56 * 2**20),
        cost_estimate=pl.CostEstimate(
            flops=78 * 10**9, bytes_accessed=0, transcendentals=0
        ),
    )(incoming, down, gate, up, *when)


def norm_back(d_normed, x, gain):
    scale = lax.rsqrt(jnp.mean(x * x, axis=1, keepdims=True) + eps)
    grad_gain = jnp.sum(d_normed * (x * scale), axis=0, keepdims=True)
    scaled = d_normed * gain
    inner = jnp.mean(scaled * x, axis=1, keepdims=True)
    return scale * scaled - x * (scale * scale * scale * inner), grad_gain


def add_up(ref, value):
    @pl.when(pl.program_id(0) == 0)
    def _():
        ref[...] = jnp.zeros_like(ref)

    ref[...] += value


def mlp_back_kernel(d_gate_ref, d_up_ref, weight_ref, x_ref, gain_ref, *refs):
    out_ref, grad_ref = refs[-2:]
    units = d_gate_ref.shape[1]
    d_normed = dot_cols(d_gate_ref[...], weight_ref[:, :units]) + dot_cols(
        d_up_ref[...], weight_ref[:, units:]
    )
    back, grad_gain = norm_back(d_normed, x_ref[...].astype(jnp.float32), gain_ref[...])
    parts, _, share = out_ref.shape
    for i in range(parts):
        out_ref[i] = back[:, i * share : (i + 1) * share].astype(jnp.bfloat16)
    add_up(grad_ref, grad_gain)


def mlp_back_call(d_gate, d_up, weights, x, gain, parts, *when):
    total, units = d_gate.shape
    width = x.shape[1]
    share = width // parts
    block = 512
    row = lambda n: pl.BlockSpec((block, n), lambda i: (i, 0))
    whole = lambda a: pl.BlockSpec(a.shape, lambda i: (0, 0), pipeline_mode=pl.Buffered(1))
    return pl.pallas_call(
        mlp_back_kernel,
        grid=(total // block,),
        in_specs=[row(units), row(units), whole(weights), row(width), whole(gain)]
        + [pl.BlockSpec(memory_space=pl.ANY)] * len(when),
        out_specs=[
            pl.BlockSpec((parts, block, share), lambda i: (0, i, 0)),
            pl.BlockSpec((1, width), lambda i: (0, 0)),
        ],
        out_shape=[
            jax.ShapeDtypeStruct((parts, total, share), jnp.bfloat16),
            jax.ShapeDtypeStruct((1, width), jnp.float32),
        ],
        compiler_params=pltpu.CompilerParams(vmem_limit_bytes=60 * 2**20),
        cost_estimate=pl.CostEstimate(
            flops=132 * 10**9, bytes_accessed=0, transcendentals=0
        ),
    )(d_gate, d_up, weights, x, gain, *when)


def attend_norm_kernel(parts, place_ref, d_qkv_ref, weight_ref, x_ref, gain_ref, own_ref, *refs):
    out_ref, grad_ref = refs[-2:]
    d_normed = dot_cols(d_qkv_ref[...], weight_ref[:, : d_qkv_ref.shape[1]])
    back, grad_gain = norm_back(d_normed, x_ref[...].astype(jnp.float32), gain_ref[...])
    out_ref[...] = back.astype(jnp.bfloat16)
    share = own_ref.shape[1]
    for place in range(parts):

        @pl.when(place_ref[0] == place)
        def _():
            lanes = slice(place * share, (place + 1) * share)
            out_ref[:, lanes] = (back[:, lanes] + own_ref[...]).astype(jnp.bfloat16)

    add_up(grad_ref, grad_gain)


def attend_norm_call(place, d_qkv, weights, x, gain, own, parts, *when):
    total, width = x.shape
    block = 256
    row = lambda n: pl.BlockSpec((block, n), lambda i: (i, 0))
    whole = lambda a: pl.BlockSpec(a.shape, lambda i: (0, 0), pipeline_mode=pl.Buffered(1))
    return pl.pallas_call(
        functools.partial(attend_norm_kernel, parts),
        grid=(total // block,),
        in_specs=[
            pl.BlockSpec(memory_space=pltpu.SMEM),
            row(d_qkv.shape[1]),
            whole(weights),
            row(width),
            whole(gain),
            row(own.shape[1]),
        ]
        + [pl.BlockSpec(memory_space=pl.ANY)] * len(when),
        out_specs=[row(width), pl.BlockSpec((1, width), lambda i: (0, 0))],
        out_shape=[
            jax.ShapeDtypeStruct((total, width), jnp.bfloat16),
            jax.ShapeDtypeStruct((1, width), jnp.float32),
        ],
        compiler_params=pltpu.CompilerParams(vmem_limit_bytes=56 * 2**20),
        cost_estimate=pl.CostEstimate(
            flops=60 * 10**9, bytes_accessed=0, transcendentals=0
        ),
    )(place, d_qkv, weights, x, gain, own, *when)


def out_back_kernel(d_ref, weight_ref, *refs):
    refs[-1][0] = dot_cols(d_ref[...], weight_ref[...]).astype(jnp.bfloat16)


def out_back_call(d_branch, weights, parts, *when):
    total, share = d_branch.shape
    rows = weights.shape[0] // parts
    return pl.pallas_call(
        out_back_kernel,
        grid=(parts,),
        in_specs=[
            pl.BlockSpec((total, share), lambda i: (0, 0)),
            pl.BlockSpec((rows, share), lambda i: (i, 0)),
        ]
        + [pl.BlockSpec(memory_space=pl.ANY)] * len(when),
        out_specs=pl.BlockSpec((1, total, rows), lambda i: (i, 0, 0)),
        out_shape=jax.ShapeDtypeStruct((parts, total, rows), jnp.bfloat16),
        compiler_params=pltpu.CompilerParams(vmem_limit_bytes=32 * 2**20),
        cost_estimate=pl.CostEstimate(
            flops=24 * 10**9, bytes_accessed=0, transcendentals=0
        ),
    )(d_branch, weights, *when)


def norm_kernel(stack_ref, gain_ref, x_ref, normed_ref):
    parts, _, share = stack_ref.shape
    squares = 0.0
    for i in range(parts):
        piece = stack_ref[i].astype(jnp.float32)
        squares = squares + jnp.sum(piece * piece, axis=1, keepdims=True)
    scale = lax.rsqrt(squares / (parts * share) + eps)
    for i in range(parts):
        lanes = slice(i * share, (i + 1) * share)
        x_ref[:, lanes] = stack_ref[i]
        normed = stack_ref[i].astype(jnp.float32) * scale * gain_ref[:, lanes]
        normed_ref[:, lanes] = normed.astype(jnp.bfloat16)


def norm_call(stack, gain):
    parts, total, share = stack.shape
    block = 256
    row = pl.BlockSpec((block, parts * share), lambda i: (i, 0))
    return pl.pallas_call(
        norm_kernel,
        grid=(total // block,),
        in_specs=[
            pl.BlockSpec((parts, block, share), lambda i: (0, i, 0)),
            pl.BlockSpec((1, parts * share), lambda i: (0, 0)),
        ],
        out_specs=[row, row],
        out_shape=[jax.ShapeDtypeStruct((total, parts * share), jnp.bfloat16)] * 2,
        compiler_params=pltpu.CompilerParams(vmem_limit_bytes=32 * 2**20),
        cost_estimate=pl.CostEstimate(flops=24 * 10**9, bytes_accessed=0, transcendentals=0),
    )(stack, gain)


def out_kernel(stack_ref, weight_ref, x_ref, out_ref):
    parts, _, depth = stack_ref.shape
    total = x_ref[...].astype(jnp.float32)
    for i in range(parts):
        total = total + jnp.dot(
            stack_ref[i], weight_ref[i * depth : (i + 1) * depth, :], preferred_element_type=jnp.float32
        )
    out_ref[...] = total.astype(jnp.bfloat16)


def out_call(stack, weight, x):
    parts, total, depth = stack.shape
    columns = weight.shape[1]
    block = 512
    row = pl.BlockSpec((block, columns), lambda i: (i, 0))
    return pl.pallas_call(
        out_kernel,
        grid=(total // block,),
        in_specs=[
            pl.BlockSpec((parts, block, depth), lambda i: (0, i, 0)),
            pl.BlockSpec(weight.shape, lambda i: (0, 0)),
            row,
        ],
        out_specs=row,
        out_shape=jax.ShapeDtypeStruct((total, columns), jnp.bfloat16),
        compiler_params=pltpu.CompilerParams(vmem_limit_bytes=40 * 2**20),
        cost_estimate=pl.CostEstimate(flops=27 * 10**9, bytes_accessed=0, transcendentals=0),
    )(stack, weight, x)


def stack_rows_kernel(left_ref, right_ref, *refs):
    refs[-1][...] = dot_rows(left_ref[0], right_ref[...]).astype(jnp.bfloat16)


def stack_rows_call(stack, right, *when):
    parts, total, rows = stack.shape
    columns = right.shape[1]
    return pl.pallas_call(
        stack_rows_kernel,
        grid=(parts,),
        in_specs=[
            pl.BlockSpec((1, total, rows), lambda i: (i, 0, 0)),
            pl.BlockSpec((total, columns), lambda i: (0, 0)),
        ]
        + [pl.BlockSpec(memory_space=pl.ANY)] * len(when),
        out_specs=pl.BlockSpec((rows, columns), lambda i: (i, 0)),
        out_shape=jax.ShapeDtypeStruct((parts * rows, columns), jnp.bfloat16),
        compiler_params=pltpu.CompilerParams(vmem_limit_bytes=40 * 2**20),
        cost_estimate=pl.CostEstimate(flops=45 * 10**9, bytes_accessed=0, transcendentals=0),
    )(stack, right, *when)


def rows_kernel(left_ref, right_ref, *refs):
    refs[-1][...] = dot_rows(left_ref[...], right_ref[...]).astype(jnp.bfloat16)


def rows_call(left, right, *when):
    total, rows = left.shape
    columns = right.shape[1]
    block = 256 if columns % 256 == 0 else 128
    return pl.pallas_call(
        rows_kernel,
        grid=(columns // block,),
        in_specs=[
            pl.BlockSpec((total, rows), lambda j: (0, 0)),
            pl.BlockSpec((total, block), lambda j: (0, j)),
        ]
        + [pl.BlockSpec(memory_space=pl.ANY)] * len(when),
        out_specs=pl.BlockSpec((rows, block), lambda j: (0, j)),
        out_shape=jax.ShapeDtypeStruct((rows, columns), jnp.bfloat16),
        compiler_params=pltpu.CompilerParams(vmem_limit_bytes=56 * 2**20),
        cost_estimate=pl.CostEstimate(flops=60 * 10**9, bytes_accessed=0, transcendentals=0),
    )(left, right, *when)


def product_kernel(left_ref, right_ref, *refs):
    refs[-1][...] = jnp.dot(left_ref[...], right_ref[...], preferred_element_type=jnp.float32).astype(
        jnp.bfloat16
    )


def product_call(left, right, *when):
    total, depth = left.shape
    columns = right.shape[1]
    block = 256 if columns % 256 == 0 else 128
    return pl.pallas_call(
        product_kernel,
        grid=(columns // block,),
        in_specs=[
            pl.BlockSpec((total, depth), lambda j: (0, 0)),
            pl.BlockSpec((depth, block), lambda j: (0, j)),
        ]
        + [pl.BlockSpec(memory_space=pl.ANY)] * len(when),
        out_specs=pl.BlockSpec((total, block), lambda j: (0, j)),
        out_shape=jax.ShapeDtypeStruct((total, columns), jnp.bfloat16),
        compiler_params=pltpu.CompilerParams(vmem_limit_bytes=56 * 2**20),
        cost_estimate=pl.CostEstimate(flops=60 * 10**9, bytes_accessed=0, transcendentals=0),
    )(left, right, *when)


def qkv_grad_kernel(normed_ref, d_qkv_ref, gain_ref, *refs):
    out_ref = refs[-1]
    columns = d_qkv_ref.shape[1]
    out_ref[:, :columns] = dot_rows(normed_ref[...], d_qkv_ref[...]).astype(jnp.bfloat16)
    rest = jnp.transpose(gain_ref[...])
    fill = out_ref.shape[1] - columns - rest.shape[1]
    if fill:
        rest = jnp.concatenate([rest, jnp.zeros((rest.shape[0], fill), rest.dtype)], axis=1)
    out_ref[:, columns:] = rest.astype(jnp.bfloat16)


def qkv_grad_call(normed, d_qkv, gain_grads, columns, *when):
    total, width = normed.shape
    block = 512
    return pl.pallas_call(
        qkv_grad_kernel,
        grid=(width // block,),
        in_specs=[
            pl.BlockSpec((total, block), lambda i: (0, i)),
            pl.BlockSpec(d_qkv.shape, lambda i: (0, 0)),
            pl.BlockSpec((gain_grads.shape[0], block), lambda i: (0, i)),
        ]
        + [pl.BlockSpec(memory_space=pl.ANY)] * len(when),
        out_specs=pl.BlockSpec((block, columns), lambda i: (i, 0)),
        out_shape=jax.ShapeDtypeStruct((width, columns), jnp.bfloat16),
        compiler_params=pltpu.CompilerParams(vmem_limit_bytes=48 * 2**20),
        cost_estimate=pl.CostEstimate(flops=36 * 10**9, bytes_accessed=0, transcendentals=0),
    )(normed, d_qkv, gain_grads, *when)


def pieces_sp(value, split):
    size = lax.axis_size("sp")
    columns = value.shape[1]
    if not split or size != 4 or columns % (2 * LANES):
        others = [(swap(value, turn),) for turn in range(1, size)]
        return [(value,)] + others, [piece for (piece,) in others], []
    half = columns // 2
    left, right = value[:, :half], value[:, half:]
    x_left, y_right = swap(left, 1), swap(right, 2)
    x_right, y_left = swap(right, 1), swap(left, 2)
    far_left, far_right = swap(x_left, 2), swap(y_right, 1)
    return (
        [(left, right), (x_left, x_right), (y_left, y_right), (far_left, far_right)],
        [x_left, y_right, x_right, y_left],
        [far_left, far_right],
    )


def spread_kernel(layout, count, chunks, place_ref, *refs):
    pieces, outs = refs[: count * chunks], refs[count * chunks :]
    size = pieces[0].shape[1]
    for place in range(count):

        @pl.when(place_ref[0] == place)
        def _():
            for part in range(count):
                for first, width, out, at, step in layout:
                    goal = at + part * step
                    while width:
                        chunk, begin = divmod(first, size)
                        some = min(width, size - begin)
                        piece = pieces[(place ^ part) * chunks + chunk]
                        outs[out][:, goal : goal + some] = piece[:, begin : begin + some].astype(jnp.float32)
                        first, goal, width = first + some, goal + some, width - some


def spread_call(place, pieces, layout, widths):
    count, chunks = len(pieces), len(pieces[0])
    rows, columns = pieces[0][0].shape
    block = rows // 5 if rows % 80 == 0 else rows
    return pl.pallas_call(
        functools.partial(spread_kernel, layout, count, chunks),
        grid=(rows // block,),
        in_specs=[pl.BlockSpec(memory_space=pltpu.SMEM)]
        + [pl.BlockSpec((block, columns), lambda i: (i, 0))] * (count * chunks),
        out_specs=[pl.BlockSpec((block, w), lambda i: (i, 0)) for w in widths],
        out_shape=[jax.ShapeDtypeStruct((rows, w), jnp.float32) for w in widths],
        compiler_params=pltpu.CompilerParams(vmem_limit_bytes=40 * 2**20),
        cost_estimate=pl.CostEstimate(
            flops=0, bytes_accessed=6 * count * chunks * rows * columns, transcendentals=0
        ),
    )(place, *[chunk for piece in pieces for chunk in piece])


def stack_kernel(count, chunks, place_ref, *refs):
    out_ref = refs[-1]
    size = refs[0].shape[1]
    for turn in range(count):
        for chunk in range(chunks):
            value = refs[turn * chunks + chunk][...].astype(jnp.float32)
            out_ref[place_ref[0] ^ turn, :, chunk * size : (chunk + 1) * size] = value


def stack_call(place, pieces):
    count, chunks = len(pieces), len(pieces[0])
    rows, columns = pieces[0][0].shape
    block = 32 if rows % 32 == 0 else rows
    return pl.pallas_call(
        functools.partial(stack_kernel, count, chunks),
        grid=(rows // block,),
        in_specs=[pl.BlockSpec(memory_space=pltpu.SMEM)]
        + [pl.BlockSpec((block, columns), lambda i: (i, 0))] * (count * chunks),
        out_specs=pl.BlockSpec((count, block, chunks * columns), lambda i: (0, i, 0)),
        out_shape=jax.ShapeDtypeStruct((count, rows, chunks * columns), jnp.float32),
        compiler_params=pltpu.CompilerParams(vmem_limit_bytes=40 * 2**20),
        cost_estimate=pl.CostEstimate(
            flops=0, bytes_accessed=6 * count * chunks * rows * columns, transcendentals=0
        ),
    )(place, *[chunk for piece in pieces for chunk in piece]).reshape(count * rows, chunks * columns)


def pass_kernel(*refs):
    pass


def after(value, *others):
    here = pl.BlockSpec(memory_space=pl.ANY)
    return pl.pallas_call(
        pass_kernel,
        in_specs=[here] * (1 + len(others)),
        out_specs=here,
        out_shape=jax.ShapeDtypeStruct(value.shape, value.dtype),
        input_output_aliases={0: 0},
        cost_estimate=pl.CostEstimate(flops=0, bytes_accessed=0, transcendentals=0),
    )(value, *others)


def pack_kernel(groups, parts, place_ref, gate_ref, up_ref, _, out_ref):
    rows, columns = gate_ref.shape
    share = columns // (groups * parts)
    for place in range(parts):

        @pl.when(place_ref[0] == place)
        def _():
            for i, ref in enumerate((gate_ref, up_ref)):
                for j in range(groups):
                    at = (i * groups + j) * share
                    begin = (j * parts + place) * share
                    out_ref[:, at : at + share] = ref[:, begin : begin + share]


def pack_call(place, gate, up, when, groups, parts):
    rows, columns = gate.shape
    block = rows // 5 if rows % 80 == 0 else rows
    spec = pl.BlockSpec((block, columns), lambda i: (i, 0))
    return pl.pallas_call(
        functools.partial(pack_kernel, groups, parts),
        grid=(rows // block,),
        in_specs=[
            pl.BlockSpec(memory_space=pltpu.SMEM),
            spec,
            spec,
            pl.BlockSpec(memory_space=pl.ANY),
        ],
        out_specs=pl.BlockSpec((block, 2 * columns // parts), lambda i: (i, 0)),
        out_shape=jax.ShapeDtypeStruct((rows, 2 * columns // parts), gate.dtype),
        compiler_params=pltpu.CompilerParams(vmem_limit_bytes=32 * 2**20),
        cost_estimate=pl.CostEstimate(flops=0, bytes_accessed=5 * rows * columns, transcendentals=0),
    )(place, gate, up, when)


def local(
    tokens,
    cotangent,
    attn_gain,
    w_query,
    key_weight,
    value_weight,
    w_out,
    mlp_gain,
    w_gate,
    w_up,
    w_down,
    positions,
    lengths,
    deal_slots,
):
    groups = lax.axis_size("fsdp")
    parts = lax.axis_size("sp")
    width = tokens.shape[-1]
    rows = tokens.shape[1]
    fsdp_place = lax.axis_index("fsdp")
    sp_place = lax.axis_index("sp")
    low = jnp.bfloat16
    wide = jnp.float32

    lanes = jnp.arange(groups, dtype=jnp.int32)
    own_row = deal_slots[fsdp_place, sp_place]
    target = own_row // groups
    pick_send = jnp.sum(jnp.where(target[None, :] == lanes[:, None], lanes[None, :], 0), axis=1)
    column = deal_slots[:, sp_place, :]
    arrived_slot = jnp.sum(jnp.where(column // groups == fsdp_place, column % groups, 0), axis=1)
    pick_place = jnp.sum(
        jnp.where(arrived_slot[None, :] == lanes[:, None], lanes[None, :], 0), axis=1
    )

    def picked(given):
        return rows_of(given.reshape(groups, -1, width), pick_send)

    def deal(blocks):
        return lax.all_to_all(blocks, "fsdp", split_axis=0, concat_axis=0, tiled=True)

    def in_place(came):
        return rows_of(came, pick_place).reshape(rows, width)

    def blocks_back(owned):
        return rows_of(owned.reshape(groups, -1, width), arrived_slot)

    def scatter_fsdp(matrix):
        return lax.psum_scatter(matrix, "fsdp", scatter_dimension=0, tiled=True)

    def column_share(weight):
        share = weight.shape[1] // parts
        return lax.dynamic_slice_in_dim(weight, sp_place * share, share, axis=1)

    def gather_fsdp(shard):
        return lax.all_gather(shard, "fsdp", axis=0, tiled=True)

    ff_rows = w_down.shape[0]
    ff_share = ff_rows // parts

    query_cols = w_query.shape[1] // parts
    key_cols = key_weight.shape[1] // parts
    qkv_cols = query_cols + 2 * key_cols
    extra = -qkv_cols % 128
    extra = extra if extra else 128
    gains = jnp.pad(jnp.stack([attn_gain, mlp_gain], axis=1), ((0, 0), (0, extra - 2)))
    place = sp_place.reshape(1)
    came_tokens = deal(picked(tokens))
    gate_up_shard = pack_call(place, w_gate, w_up, came_tokens, groups, parts)
    qkv_shard = jnp.concatenate(
        [column_share(w_query), column_share(key_weight), column_share(value_weight), gains], axis=1
    )
    came_incoming = deal(after(picked(cotangent), came_tokens))
    qkv_all = gather_fsdp(after(qkv_shard, came_tokens))
    out_all = gather_fsdp(column_share(w_out))
    gate_up_all = gather_fsdp(gate_up_shard)
    down_all = gather_fsdp(lax.dynamic_slice_in_dim(w_down, sp_place * ff_share, ff_share, axis=0))
    gain_one = qkv_all[:, qkv_cols].astype(wide)[None, :]
    gain_two = qkv_all[:, qkv_cols + 1].astype(wide)[None, :]

    group_inputs = gather_sp(in_place(came_tokens))[0].reshape(-1, width)
    group_positions = gather_small(positions.reshape(-1)).reshape(-1)
    total = group_inputs.shape[0]

    cosine, sine = rotary_tables(group_positions)
    heads, keys = query_cols // HEAD_SIZE, key_cols // HEAD_SIZE
    normed, query_low, key_low, value_low = qkv_call(
        group_inputs, gain_one, qkv_all, cosine, sine, heads, keys
    )
    sizes = lengths.reshape(-1)
    ends = jnp.cumsum(sizes)
    places = jnp.arange(total, dtype=jnp.int32)
    start = jnp.sum(jnp.where(places[:, None] >= ends[None, :], sizes[None, :], 0), axis=1)
    own_mixed, logs = attend_call(query_low, key_low, value_low, start[:, None])

    share = width // parts

    def own_columns(matrix):
        return lax.dynamic_slice_in_dim(matrix, sp_place * share, share, axis=1)

    mixed, _ = gather_sp(own_mixed)
    own_hidden = out_call(mixed, out_all, own_columns(group_inputs))
    hidden_low, normed_two = norm_call(gather_sp(own_hidden)[0], gain_two)

    active_low, gate, upward = gate_up_call(normed_two, gate_up_all)
    own_incoming = after(in_place(after(came_incoming, own_hidden)), normed_two)
    group_incoming = gather_sp(own_incoming, active_low)[0].reshape(-1, width)
    grad_down = rows_call(active_low, group_incoming)
    result_part = product_call(active_low, down_all, grad_down)
    d_gate, d_up = unit_back_call(group_incoming, down_all, gate, upward, result_part)
    grad_gate = rows_call(normed_two, d_gate)
    result_sum, (sums_result, _) = scatter_sp(result_part.reshape(parts, rows, width), grad_gate)
    own_hidden_rows = lax.dynamic_slice_in_dim(hidden_low, sp_place * rows, rows, axis=0)
    blocks_result = blocks_back((own_hidden_rows.astype(wide) + result_sum).astype(low))

    back_two, grad_gain_two = mlp_back_call(
        d_gate, d_up, gate_up_all, hidden_low, gain_two, parts, grad_gate, *sums_result
    )
    back_two = after(back_two, result_sum)
    from_others, _ = scatter_sp(back_two)
    grad_up = rows_call(normed_two, d_up, back_two)
    gone_result = deal(blocks_result)
    own_d_hidden = own_columns(group_incoming).astype(wide) + from_others
    d_branch = own_d_hidden.astype(low)
    grad_up = after(grad_up, d_branch)
    grad_out = stack_rows_call(mixed, d_branch)
    d_mixed, _ = scatter_sp(out_back_call(d_branch, out_all, parts, grad_up), grad_out)
    d_mixed = d_mixed.astype(low)

    down_sum = after(scatter_fsdp(grad_down), d_mixed)
    gate_sum = after(scatter_fsdp(grad_gate), d_mixed, down_sum)
    down_pieces, down_first, _ = pieces_sp(down_sum, False)
    gate_pieces, gate_first, _ = pieces_sp(gate_sum, False)
    d_qkv = attend_back_call(
        query_low, key_low, value_low, d_mixed, logs.T, start[None, :], cosine, sine, gone_result
    )
    back_one, grad_gain_one = attend_norm_call(
        place, d_qkv, qkv_all, group_inputs, gain_one, own_d_hidden, parts, *down_first, *gate_first[:-1]
    )
    gain_grads = jnp.concatenate(
        [grad_gain_one, grad_gain_two, jnp.zeros((6, width), wide)], axis=0
    )
    grad_qkv = qkv_grad_call(normed, d_qkv, gain_grads, qkv_all.shape[1])
    d_inputs = scatter_sp(back_one.reshape(parts, rows, width))[0]
    gone_grad = deal(blocks_back(d_inputs.astype(low)))
    layer_out = rows_of(gone_result, target).reshape(tokens.shape)
    input_grad = rows_of(gone_grad, target).reshape(tokens.shape)

    up_pieces = pieces_sp(scatter_fsdp(grad_up), True)[0]
    out_pieces = pieces_sp(scatter_fsdp(grad_out), False)[0]
    qkv_pieces = pieces_sp(scatter_fsdp(grad_qkv), True)[0]

    down_shard = stack_call(place, down_pieces)
    hidden_layout = [
        (j * ff_share, ff_share, 0, j * parts * ff_share, ff_share) for j in range(groups)
    ]
    (gate_shard,) = spread_call(place, gate_pieces, hidden_layout, [w_gate.shape[1]])
    (up_shard,) = spread_call(place, up_pieces, hidden_layout, [w_up.shape[1]])
    (out_shard,) = spread_call(place, out_pieces, [(0, share, 0, 0, share)], [width])
    qkv_layout = [
        (0, query_cols, 0, 0, query_cols),
        (query_cols, key_cols, 1, 0, key_cols),
        (query_cols + key_cols, key_cols, 2, 0, key_cols),
        (qkv_cols, 2, 3, 0, 2),
    ]
    query_shard, key_shard, value_shard, gain_parts = spread_call(
        place,
        qkv_pieces,
        qkv_layout,
        [w_query.shape[1], key_weight.shape[1], value_weight.shape[1], 2 * parts],
    )
    gain_shards = jnp.sum(gain_parts.reshape(-1, parts, 2), axis=1)
    return (
        layer_out,
        input_grad,
        gain_shards[:, 0],
        query_shard,
        key_shard,
        value_shard,
        out_shard,
        gain_shards[:, 1],
        gate_shard,
        up_shard,
        down_shard,
    )


def solution(mesh):
    placed = (
        P("fsdp", "sp", None),
        P("fsdp", "sp", None),
        P("fsdp"),
        P("fsdp", None),
        P("fsdp", None),
        P("fsdp", None),
        P("fsdp", None),
        P("fsdp"),
        P("fsdp", None),
        P("fsdp", None),
        P("fsdp", None),
        P("fsdp", "sp"),
        P("fsdp", None),
        P(),
    )
    return jax.shard_map(
        local,
        mesh=mesh,
        in_specs=placed,
        out_specs=(
            P("fsdp", "sp", None),
            P("fsdp", "sp", None),
            P("fsdp"),
            P("fsdp", None),
            P("fsdp", None),
            P("fsdp", None),
            P("fsdp", None),
            P("fsdp"),
            P("fsdp", None),
            P("fsdp", None),
            P("fsdp", None),
        ),
        check_vma=False,
    )
```

```python
import functools
import jax
import jax.numpy as jnp
from jax import lax
from jax.experimental import pallas as pl
from jax.experimental.pallas import tpu as pltpu
from jax.experimental.layout import Layout, with_layout_constraint
from jax.sharding import PartitionSpec as P

QUERY_HEADS = 32
KEY_VALUE_HEADS = 8
HEAD_SIZE = 80
LANES = 128


eps = 1e-05
theta = 1000000.0
log2e = 1.4426950408889634


def swap(value, bit):
    size = lax.axis_size("sp")
    return lax.ppermute(value, "sp", [(i, i ^ bit) for i in range(size)])


def row_major(value):
    return with_layout_constraint(value, Layout(major_to_minor=tuple(range(value.ndim))))


def gather_sp(value, *hold):
    size = lax.axis_size("sp")
    if size != 4:
        whole = lax.all_gather(value, "sp", axis=0, tiled=False)
        return whole, (whole,)
    place = lax.axis_index("sp")
    half = value.shape[0] // 2
    first, second = value[:half], value[half:]
    x_first, y_second = swap(first, 1), swap(second, 2)
    x_second, y_first = swap(second, 1), swap(first, 2)
    far_first, far_second = (after(v, *hold) if hold else v for v in (x_first, y_second))
    far_first, far_second = swap(far_first, 2), swap(far_second, 1)
    out = jnp.zeros((size,) + value.shape, value.dtype)
    if hold:
        out = after(out, *hold)
    zeros = (0,) * (value.ndim - 1)
    for turn, low, high in (
        (0, first, second),
        (1, x_first, x_second),
        (2, y_first, y_second),
        (3, far_first, far_second),
    ):
        out = lax.dynamic_update_slice(out, low[None], (place ^ turn, 0) + zeros)
        out = lax.dynamic_update_slice(out, high[None], (place ^ turn, half) + zeros)
    return row_major(out), (x_first, y_second)


def rows_of(blocks, picks):
    return blocks.at[picks].get(mode="promise_in_bounds")


def gather_small(value):
    size = lax.axis_size("sp")
    if size != 4:
        return lax.all_gather(value, "sp", axis=0, tiled=False)
    place = lax.axis_index("sp")
    pieces = [value] + [swap(value, turn) for turn in range(1, size)]
    here = [
        sum(jnp.where(place ^ turn == i, pieces[turn], 0) for turn in range(size)) for i in range(size)
    ]
    return jnp.stack(here, axis=0)


def scatter_sp(parts, hook=None):
    size = lax.axis_size("sp")
    if size != 4:
        summed = lax.psum_scatter(parts, "sp", scatter_dimension=0, tiled=False)
        given = hook((summed,)) if hook else ()
        return summed.astype(jnp.float32), (summed,), (summed,), given
    place = lax.axis_index("sp")
    half = parts.shape[1] // 2
    parts = row_major(parts)

    def block(turn, lower):
        start = (place ^ turn, 0 if lower else half) + (0,) * (parts.ndim - 2)
        return lax.dynamic_slice(parts, start, (1, half) + parts.shape[2:])[0]

    wide = jnp.float32
    low = parts.dtype

    def added(*values):
        values = lax.optimization_barrier(values)
        total = values[0].astype(wide)
        for value in values[1:]:
            total = total + value.astype(wide)
        return total

    from_x, from_y = swap(block(3, True), 1), swap(block(3, False), 2)
    given = hook((from_x, from_y)) if hook else ()
    if given:
        from_x, from_y = after(from_x, *given), after(from_y, *given)
    x_first, y_second = swap(block(1, True), 1), swap(block(2, False), 2)
    y_sent = added(block(2, True), from_x).astype(low)
    x_sent = added(block(1, False), from_y).astype(low)
    y_first, x_second = swap(y_sent, 2), swap(x_sent, 1)
    first = added(block(0, True), x_first, y_first)
    second = added(block(0, False), y_second, x_second)
    stage = (y_sent, x_sent, x_first, y_second)
    return jnp.concatenate([first, second], axis=0), stage, (y_first, x_second), given


def rotary_tables(positions):
    halves = HEAD_SIZE // 2
    frequency = theta ** (-(2.0 * jnp.arange(halves, dtype=jnp.float32)) / HEAD_SIZE)
    angles = positions.astype(jnp.float32)[:, None] * frequency[None, :]
    cosine, sine = jnp.cos(angles), jnp.sin(angles)
    rest = jnp.zeros((positions.shape[0], LANES - HEAD_SIZE), jnp.float32)
    return (
        jnp.concatenate([cosine, cosine, rest], axis=1),
        jnp.concatenate([-sine, sine, rest], axis=1),
    )


def dot(left, right):
    return jnp.dot(left, right, preferred_element_type=jnp.float32)


def dot_rows(left, right):
    return lax.dot_general(left, right, (((0,), (0,)), ((), ())), preferred_element_type=jnp.float32)


def dot_cols(left, right):
    return lax.dot_general(left, right, (((1,), (1,)), ((), ())), preferred_element_type=jnp.float32)


def head_of(matrix, head):
    first = head * HEAD_SIZE
    if first + LANES <= matrix.shape[1]:
        return matrix[:, first : first + LANES]
    kept = matrix[:, first : first + HEAD_SIZE]
    return jnp.concatenate([kept, jnp.zeros((kept.shape[0], LANES - HEAD_SIZE), kept.dtype)], axis=1)


def half_turn(padded):
    lane = lax.broadcasted_iota(jnp.int32, padded.shape, 1)
    half = HEAD_SIZE // 2
    return jnp.where(lane < half, pltpu.roll(padded, LANES - half, 1), pltpu.roll(padded, half, 1))


def qkv_kernel(heads, keys, x_ref, gain_ref, weight_ref, cos_ref, sin_ref, normed_ref, q_ref, k_ref, v_ref):
    x = x_ref[...].astype(jnp.float32)
    scale = lax.rsqrt(jnp.mean(x * x, axis=1, keepdims=True) + eps)
    normed = (x * scale * gain_ref[...]).astype(jnp.bfloat16)
    normed_ref[...] = normed
    rows = jnp.dot(normed, weight_ref[...], preferred_element_type=jnp.float32)
    cosine, sine = cos_ref[...], sin_ref[...]
    inside = lax.broadcasted_iota(jnp.int32, cosine.shape, 1) < HEAD_SIZE
    for i in range(heads + keys):
        v = head_of(rows, i)
        turned = (v * cosine + half_turn(v) * sine).astype(jnp.bfloat16)
        if i < heads:
            q_ref[:, i * LANES : (i + 1) * LANES] = turned
        else:
            k_ref[:, (i - heads) * LANES : (i - heads + 1) * LANES] = turned
    for i in range(keys):
        v = head_of(rows, heads + keys + i)
        v_ref[:, i * LANES : (i + 1) * LANES] = jnp.where(inside, v, 0.0).astype(jnp.bfloat16)


def qkv_call(x, gain, weight, cosine, sine, heads, keys):
    total, width = x.shape
    block = 256
    bf = jnp.bfloat16
    row = lambda n: pl.BlockSpec((block, n), lambda i: (i, 0))
    whole = lambda a: pl.BlockSpec(a.shape, lambda i: (0, 0))
    return pl.pallas_call(
        functools.partial(qkv_kernel, heads, keys),
        grid=(total // block,),
        in_specs=[row(width), whole(gain), whole(weight), row(LANES), row(LANES)],
        out_specs=[row(width), row(heads * LANES), row(keys * LANES), row(keys * LANES)],
        out_shape=[
            jax.ShapeDtypeStruct((total, width), bf),
            jax.ShapeDtypeStruct((total, heads * LANES), bf),
            jax.ShapeDtypeStruct((total, keys * LANES), bf),
            jax.ShapeDtypeStruct((total, keys * LANES), bf),
        ],
        compiler_params=pltpu.CompilerParams(vmem_limit_bytes=48 * 2**20),
        cost_estimate=pl.CostEstimate(
            flops=120 * 10**9, bytes_accessed=0, transcendentals=0
        ),
    )(x, gain, weight, cosine, sine)


def attend_kernel(heads, keys, block, q_ref, k_ref, v_ref, start_ref, *refs):
    mixed_ref, lse_ref, bias_ref = refs[-3:]
    total = q_ref.shape[0]
    group = heads // keys
    factor = HEAD_SIZE**-0.5 * log2e
    for i in range(total // block):
        first, stop = i * block, (i + 1) * block
        column = lax.broadcasted_iota(jnp.int32, (block, stop), 1)
        row = lax.broadcasted_iota(jnp.int32, (block, stop), 0) + first
        good = (column >= start_ref[first:stop, :]) & (column <= row)
        bias_ref[:, :stop] = jnp.where(good, 0.0, -1e30)
        for head in range(heads):
            lanes = slice(head * LANES, (head + 1) * LANES)
            key = slice(head // group * LANES, (head // group + 1) * LANES)
            scores = dot_cols(q_ref[first:stop, lanes], k_ref[:stop, key]) * factor + bias_ref[:, :stop]
            top = jnp.max(scores, axis=1, keepdims=True)
            weights = jnp.exp2(scores - top)
            summed = jnp.sum(weights, axis=1, keepdims=True)
            mixed = jnp.dot(
                weights.astype(jnp.bfloat16), v_ref[:stop, key], preferred_element_type=jnp.float32
            ) / summed
            mixed_ref[first:stop, head * HEAD_SIZE : (head + 1) * HEAD_SIZE] = mixed[:, :HEAD_SIZE].astype(
                jnp.bfloat16
            )
            lse_ref[first:stop, head : head + 1] = top + jnp.log2(summed)


def attend_call(q, k, v, start, *when):
    block = 256
    total = q.shape[0]
    heads, keys = q.shape[1] // LANES, k.shape[1] // LANES
    return pl.pallas_call(
        functools.partial(attend_kernel, heads, keys, block),
        in_specs=[pl.BlockSpec(memory_space=pltpu.VMEM)] * 4
        + [pl.BlockSpec(memory_space=pl.ANY)] * len(when),
        out_shape=[
            jax.ShapeDtypeStruct((total, heads * HEAD_SIZE), jnp.bfloat16),
            jax.ShapeDtypeStruct((total, heads), jnp.float32),
        ],
        scratch_shapes=[pltpu.VMEM((block, total), jnp.float32)],
        compiler_params=pltpu.CompilerParams(vmem_limit_bytes=56 * 2**20),
        cost_estimate=pl.CostEstimate(
            flops=140 * 10**9, bytes_accessed=0, transcendentals=0
        ),
    )(q, k, v, start, *when)


def attend_back_kernel(
    heads, keys, block, q_ref, k_ref, v_ref, grad_ref, lse_ref, start_ref, cos_ref, sin_ref, *refs
):
    out_ref, bias_ref, dk_ref, dv_ref = refs[-4:]
    total = q_ref.shape[0]
    group = heads // keys
    scale = HEAD_SIZE**-0.5
    factor = scale * log2e
    low = jnp.bfloat16
    dk_ref[...] = jnp.zeros_like(dk_ref)
    dv_ref[...] = jnp.zeros_like(dv_ref)
    inside = lax.broadcasted_iota(jnp.int32, (block, LANES), 1) < HEAD_SIZE
    half = HEAD_SIZE // 2

    def turned_back(w, rows):
        w = w.astype(low).astype(jnp.float32)
        scaled = w * sin_ref[rows, :]
        lane = lax.broadcasted_iota(jnp.int32, w.shape, 1)
        moved = jnp.where(lane < half, pltpu.roll(scaled, LANES - half, 1), pltpu.roll(scaled, half, 1))
        return (w * cos_ref[rows, :] + moved).astype(low)

    for i in range(total // block):
        first, stop = i * block, (i + 1) * block
        rows = slice(first, stop)
        key_place = lax.broadcasted_iota(jnp.int32, (stop, block), 0)
        place = lax.broadcasted_iota(jnp.int32, (stop, block), 1) + first
        good = (key_place >= start_ref[:, rows]) & (key_place <= place)
        bias_ref[:stop, :] = jnp.where(good, 0.0, -1e30)
        grads = grad_ref[rows, :].astype(jnp.float32)
        for head in range(heads):
            lanes = slice(head * LANES, (head + 1) * LANES)
            key = slice(head // group * LANES, (head // group + 1) * LANES)
            query = q_ref[rows, lanes]
            grad = jnp.where(inside, head_of(grads, head), 0.0).astype(low)
            scores = dot_cols(k_ref[:stop, key], query) * factor + bias_ref[:stop, :]
            probs = jnp.exp2(scores - lse_ref[head : head + 1, rows])
            dv_ref[:stop, key] += jnp.dot(probs.astype(low), grad, preferred_element_type=jnp.float32)
            d_probs = dot_cols(v_ref[:stop, key], grad)
            delta = jnp.sum(probs * d_probs, axis=0, keepdims=True)
            d_scores = (probs * (d_probs - delta)).astype(low)
            dk_ref[:stop, key] += jnp.dot(d_scores, query, preferred_element_type=jnp.float32)
            d_query = dot_rows(d_scores, k_ref[:stop, key]) * scale
            out_ref[rows, head * HEAD_SIZE : (head + 1) * HEAD_SIZE] = turned_back(d_query, rows)[:, :HEAD_SIZE]
    for i in range(total // block):
        rows = slice(i * block, (i + 1) * block)
        for j in range(keys):
            lanes = slice(j * LANES, (j + 1) * LANES)
            at = (heads + j) * HEAD_SIZE
            out_ref[rows, at : at + HEAD_SIZE] = turned_back(dk_ref[rows, lanes] * scale, rows)[:, :HEAD_SIZE]
            at = (heads + keys + j) * HEAD_SIZE
            out_ref[rows, at : at + HEAD_SIZE] = dv_ref[rows, lanes][:, :HEAD_SIZE].astype(low)


def attend_back_call(q, k, v, grad, lse_rows, start_row, cosine, sine_back, *when):
    block = 256
    total = q.shape[0]
    heads, keys = q.shape[1] // LANES, k.shape[1] // LANES
    return pl.pallas_call(
        functools.partial(attend_back_kernel, heads, keys, block),
        in_specs=[pl.BlockSpec(memory_space=pltpu.VMEM)] * 8
        + [pl.BlockSpec(memory_space=pl.ANY)] * len(when),
        out_shape=jax.ShapeDtypeStruct((total, (heads + 2 * keys) * HEAD_SIZE), jnp.bfloat16),
        scratch_shapes=[
            pltpu.VMEM((total, block), jnp.float32),
            pltpu.VMEM((total, keys * LANES), jnp.float32),
            pltpu.VMEM((total, keys * LANES), jnp.float32),
        ],
        compiler_params=pltpu.CompilerParams(vmem_limit_bytes=56 * 2**20),
        cost_estimate=pl.CostEstimate(
            flops=250 * 10**9, bytes_accessed=0, transcendentals=0
        ),
    )(q, k, v, grad, lse_rows, start_row, cosine, sine_back, *when)

def gate_up_kernel(x_ref, gate_weight_ref, up_weight_ref, active_ref, gate_ref, up_ref):
    x = x_ref[...]
    gate = jnp.dot(x, gate_weight_ref[...], preferred_element_type=jnp.float32)
    upward = jnp.dot(x, up_weight_ref[...], preferred_element_type=jnp.float32)
    active_ref[...] = (gate / (1.0 + jnp.exp(-gate)) * upward).astype(jnp.bfloat16)
    gate_ref[...] = gate.astype(jnp.bfloat16)
    up_ref[...] = upward.astype(jnp.bfloat16)


def unit_block(units):
    return 256 if units % 256 == 0 else 128


def gate_up_call(x, weights):
    total, width = x.shape
    units = weights.shape[1] // 2
    block = unit_block(units)
    count = units // block
    out = pl.BlockSpec((total, block), lambda j: (0, j))
    return pl.pallas_call(
        gate_up_kernel,
        grid=(count,),
        in_specs=[
            pl.BlockSpec((total, width), lambda j: (0, 0)),
            pl.BlockSpec((width, block), lambda j: (0, j)),
            pl.BlockSpec((width, block), lambda j: (0, j + count)),
        ],
        out_specs=[out] * 3,
        out_shape=[jax.ShapeDtypeStruct((total, units), jnp.bfloat16)] * 3,
        compiler_params=pltpu.CompilerParams(vmem_limit_bytes=56 * 2**20),
        cost_estimate=pl.CostEstimate(
            flops=185 * 10**9, bytes_accessed=0, transcendentals=0
        ),
    )(x, weights, weights)


def unit_back_kernel(incoming_ref, down_ref, gate_ref, up_ref, *refs):
    d_gate_ref, d_up_ref = refs[-2:]
    d_active = dot_cols(incoming_ref[...], down_ref[...])
    gate = gate_ref[...].astype(jnp.float32)
    upward = up_ref[...].astype(jnp.float32)
    logistic = 1.0 / (1.0 + jnp.exp(-gate))
    d_gate_ref[...] = (d_active * upward * logistic * (1.0 + gate * (1.0 - logistic))).astype(jnp.bfloat16)
    d_up_ref[...] = (d_active * gate * logistic).astype(jnp.bfloat16)


def unit_back_call(incoming, down, gate, up, *when):
    total, width = incoming.shape
    units = down.shape[0]
    block = unit_block(units)
    column = pl.BlockSpec((total, block), lambda j: (0, j))
    return pl.pallas_call(
        unit_back_kernel,
        grid=(units // block,),
        in_specs=[
            pl.BlockSpec((total, width), lambda j: (0, 0)),
            pl.BlockSpec((block, width), lambda j: (j, 0)),
            column,
            column,
        ]
        + [pl.BlockSpec(memory_space=pl.ANY)] * len(when),
        out_specs=[column] * 2,
        out_shape=[jax.ShapeDtypeStruct((total, units), jnp.bfloat16)] * 2,
        compiler_params=pltpu.CompilerParams(vmem_limit_bytes=56 * 2**20),
        cost_estimate=pl.CostEstimate(
            flops=130 * 10**9, bytes_accessed=0, transcendentals=0
        ),
    )(incoming, down, gate, up, *when)


def norm_back(d_normed, x, gain):
    scale = lax.rsqrt(jnp.mean(x * x, axis=1, keepdims=True) + eps)
    grad_gain = jnp.sum(d_normed * (x * scale), axis=0, keepdims=True)
    scaled = d_normed * gain
    inner = jnp.mean(scaled * x, axis=1, keepdims=True)
    return scale * scaled - x * (scale * scale * scale * inner), grad_gain


def add_up(ref, value):
    @pl.when(pl.program_id(0) == 0)
    def _():
        ref[...] = jnp.zeros_like(ref)

    ref[...] += value


def mlp_back_kernel(d_gate_ref, d_up_ref, weight_ref, x_ref, gain_ref, *refs):
    out_ref, grad_ref = refs[-2:]
    units = d_gate_ref.shape[1]
    d_normed = dot_cols(d_gate_ref[...], weight_ref[:, :units]) + dot_cols(
        d_up_ref[...], weight_ref[:, units:]
    )
    back, grad_gain = norm_back(d_normed, x_ref[...].astype(jnp.float32), gain_ref[...])
    parts, _, share = out_ref.shape
    for i in range(parts):
        out_ref[i] = back[:, i * share : (i + 1) * share].astype(jnp.bfloat16)
    add_up(grad_ref, grad_gain)


def mlp_back_call(d_gate, d_up, weights, x, gain, parts, *when):
    total, units = d_gate.shape
    width = x.shape[1]
    share = width // parts
    block = 512
    row = lambda n: pl.BlockSpec((block, n), lambda i: (i, 0))
    whole = lambda a: pl.BlockSpec(a.shape, lambda i: (0, 0), pipeline_mode=pl.Buffered(1))
    return pl.pallas_call(
        mlp_back_kernel,
        grid=(total // block,),
        in_specs=[row(units), row(units), whole(weights), row(width), whole(gain)]
        + [pl.BlockSpec(memory_space=pl.ANY)] * len(when),
        out_specs=[
            pl.BlockSpec((parts, block, share), lambda i: (0, i, 0)),
            pl.BlockSpec((1, width), lambda i: (0, 0)),
        ],
        out_shape=[
            jax.ShapeDtypeStruct((parts, total, share), jnp.bfloat16),
            jax.ShapeDtypeStruct((1, width), jnp.float32),
        ],
        compiler_params=pltpu.CompilerParams(vmem_limit_bytes=60 * 2**20),
        cost_estimate=pl.CostEstimate(
            flops=220 * 10**9, bytes_accessed=0, transcendentals=0
        ),
    )(d_gate, d_up, weights, x, gain, *when)


def attend_norm_kernel(parts, place_ref, d_qkv_ref, weight_ref, x_ref, gain_ref, own_ref, *refs):
    out_ref, grad_ref = refs[-2:]
    d_normed = dot_cols(d_qkv_ref[...], weight_ref[:, : d_qkv_ref.shape[1]])
    back, grad_gain = norm_back(d_normed, x_ref[...].astype(jnp.float32), gain_ref[...])
    out_ref[...] = back.astype(jnp.bfloat16)
    share = own_ref.shape[1]
    for place in range(parts):

        @pl.when(place_ref[0] == place)
        def _():
            lanes = slice(place * share, (place + 1) * share)
            out_ref[:, lanes] = (back[:, lanes] + own_ref[...]).astype(jnp.bfloat16)

    add_up(grad_ref, grad_gain)


def attend_norm_call(place, d_qkv, weights, x, gain, own, parts, *when):
    total, width = x.shape
    block = 256
    row = lambda n: pl.BlockSpec((block, n), lambda i: (i, 0))
    whole = lambda a: pl.BlockSpec(a.shape, lambda i: (0, 0), pipeline_mode=pl.Buffered(1))
    return pl.pallas_call(
        functools.partial(attend_norm_kernel, parts),
        grid=(total // block,),
        in_specs=[
            pl.BlockSpec(memory_space=pltpu.SMEM),
            row(d_qkv.shape[1]),
            whole(weights),
            row(width),
            whole(gain),
            row(own.shape[1]),
        ]
        + [pl.BlockSpec(memory_space=pl.ANY)] * len(when),
        out_specs=[row(width), pl.BlockSpec((1, width), lambda i: (0, 0))],
        out_shape=[
            jax.ShapeDtypeStruct((total, width), jnp.bfloat16),
            jax.ShapeDtypeStruct((1, width), jnp.float32),
        ],
        compiler_params=pltpu.CompilerParams(vmem_limit_bytes=56 * 2**20),
        cost_estimate=pl.CostEstimate(
            flops=100 * 10**9, bytes_accessed=0, transcendentals=0
        ),
    )(place, d_qkv, weights, x, gain, own, *when)


def out_back_kernel(d_ref, weight_ref, *refs):
    refs[-1][0] = dot_cols(d_ref[...], weight_ref[...]).astype(jnp.bfloat16)


def out_back_call(d_branch, weights, parts, *when):
    total, share = d_branch.shape
    rows = weights.shape[0] // parts
    return pl.pallas_call(
        out_back_kernel,
        grid=(parts,),
        in_specs=[
            pl.BlockSpec((total, share), lambda i: (0, 0)),
            pl.BlockSpec((rows, share), lambda i: (i, 0)),
        ]
        + [pl.BlockSpec(memory_space=pl.ANY)] * len(when),
        out_specs=pl.BlockSpec((1, total, rows), lambda i: (i, 0, 0)),
        out_shape=jax.ShapeDtypeStruct((parts, total, rows), jnp.bfloat16),
        compiler_params=pltpu.CompilerParams(vmem_limit_bytes=32 * 2**20),
        cost_estimate=pl.CostEstimate(
            flops=40 * 10**9, bytes_accessed=0, transcendentals=0
        ),
    )(d_branch, weights, *when)


def norm_kernel(stack_ref, gain_ref, x_ref, normed_ref):
    parts, _, share = stack_ref.shape
    squares = 0.0
    for i in range(parts):
        piece = stack_ref[i].astype(jnp.float32)
        squares = squares + jnp.sum(piece * piece, axis=1, keepdims=True)
    scale = lax.rsqrt(squares / (parts * share) + eps)
    for i in range(parts):
        lanes = slice(i * share, (i + 1) * share)
        x_ref[:, lanes] = stack_ref[i]
        normed = stack_ref[i].astype(jnp.float32) * scale * gain_ref[:, lanes]
        normed_ref[:, lanes] = normed.astype(jnp.bfloat16)


def norm_call(stack, gain):
    parts, total, share = stack.shape
    block = 256
    row = pl.BlockSpec((block, parts * share), lambda i: (i, 0))
    return pl.pallas_call(
        norm_kernel,
        grid=(total // block,),
        in_specs=[
            pl.BlockSpec((parts, block, share), lambda i: (0, i, 0)),
            pl.BlockSpec((1, parts * share), lambda i: (0, 0)),
        ],
        out_specs=[row, row],
        out_shape=[jax.ShapeDtypeStruct((total, parts * share), jnp.bfloat16)] * 2,
        compiler_params=pltpu.CompilerParams(vmem_limit_bytes=32 * 2**20),
        cost_estimate=pl.CostEstimate(flops=40 * 10**9, bytes_accessed=0, transcendentals=0),
    )(stack, gain)


def out_kernel(stack_ref, weight_ref, x_ref, out_ref):
    parts, _, depth = stack_ref.shape
    total = x_ref[...].astype(jnp.float32)
    for i in range(parts):
        total = total + jnp.dot(
            stack_ref[i], weight_ref[i * depth : (i + 1) * depth, :], preferred_element_type=jnp.float32
        )
    out_ref[...] = total.astype(jnp.bfloat16)


def out_call(stack, weight, x):
    parts, total, depth = stack.shape
    columns = weight.shape[1]
    block = 512
    row = pl.BlockSpec((block, columns), lambda i: (i, 0))
    return pl.pallas_call(
        out_kernel,
        grid=(total // block,),
        in_specs=[
            pl.BlockSpec((parts, block, depth), lambda i: (0, i, 0)),
            pl.BlockSpec(weight.shape, lambda i: (0, 0)),
            row,
        ],
        out_specs=row,
        out_shape=jax.ShapeDtypeStruct((total, columns), jnp.bfloat16),
        compiler_params=pltpu.CompilerParams(vmem_limit_bytes=40 * 2**20),
        cost_estimate=pl.CostEstimate(flops=45 * 10**9, bytes_accessed=0, transcendentals=0),
    )(stack, weight, x)


def stack_rows_kernel(left_ref, right_ref, *refs):
    refs[-1][...] = dot_rows(left_ref[0], right_ref[...]).astype(jnp.bfloat16)


def stack_rows_call(stack, right, *when):
    parts, total, rows = stack.shape
    columns = right.shape[1]
    return pl.pallas_call(
        stack_rows_kernel,
        grid=(parts,),
        in_specs=[
            pl.BlockSpec((1, total, rows), lambda i: (i, 0, 0)),
            pl.BlockSpec((total, columns), lambda i: (0, 0)),
        ]
        + [pl.BlockSpec(memory_space=pl.ANY)] * len(when),
        out_specs=pl.BlockSpec((rows, columns), lambda i: (i, 0)),
        out_shape=jax.ShapeDtypeStruct((parts * rows, columns), jnp.bfloat16),
        compiler_params=pltpu.CompilerParams(vmem_limit_bytes=40 * 2**20),
        cost_estimate=pl.CostEstimate(flops=0 * 10**9, bytes_accessed=0, transcendentals=0),
    )(stack, right, *when)


def rows_kernel(left_ref, right_ref, *refs):
    refs[-1][...] = dot_rows(left_ref[...], right_ref[...]).astype(jnp.bfloat16)


def rows_call(left, right, *when):
    total, rows = left.shape
    columns = right.shape[1]
    block = 256 if columns % 256 == 0 else 128
    return pl.pallas_call(
        rows_kernel,
        grid=(columns // block,),
        in_specs=[
            pl.BlockSpec((total, rows), lambda j: (0, 0)),
            pl.BlockSpec((total, block), lambda j: (0, j)),
        ]
        + [pl.BlockSpec(memory_space=pl.ANY)] * len(when),
        out_specs=pl.BlockSpec((rows, block), lambda j: (0, j)),
        out_shape=jax.ShapeDtypeStruct((rows, columns), jnp.bfloat16),
        compiler_params=pltpu.CompilerParams(vmem_limit_bytes=56 * 2**20),
        cost_estimate=pl.CostEstimate(flops=0 if when else 100 * 10**9, bytes_accessed=0, transcendentals=0),
    )(left, right, *when)


def product_kernel(left_ref, right_ref, *refs):
    refs[-1][...] = jnp.dot(left_ref[...], right_ref[...], preferred_element_type=jnp.float32).astype(
        jnp.bfloat16
    )


def product_call(left, right, *when):
    total, depth = left.shape
    columns = right.shape[1]
    block = 256 if columns % 256 == 0 else 128
    return pl.pallas_call(
        product_kernel,
        grid=(columns // block,),
        in_specs=[
            pl.BlockSpec((total, depth), lambda j: (0, 0)),
            pl.BlockSpec((depth, block), lambda j: (0, j)),
        ]
        + [pl.BlockSpec(memory_space=pl.ANY)] * len(when),
        out_specs=pl.BlockSpec((total, block), lambda j: (0, j)),
        out_shape=jax.ShapeDtypeStruct((total, columns), jnp.bfloat16),
        compiler_params=pltpu.CompilerParams(vmem_limit_bytes=56 * 2**20),
        cost_estimate=pl.CostEstimate(flops=100 * 10**9, bytes_accessed=0, transcendentals=0),
    )(left, right, *when)


def qkv_grad_kernel(normed_ref, d_qkv_ref, gain_ref, *refs):
    out_ref = refs[-1]
    columns = d_qkv_ref.shape[1]
    out_ref[:, :columns] = dot_rows(normed_ref[...], d_qkv_ref[...]).astype(jnp.bfloat16)
    rest = jnp.transpose(gain_ref[...])
    fill = out_ref.shape[1] - columns - rest.shape[1]
    if fill:
        rest = jnp.concatenate([rest, jnp.zeros((rest.shape[0], fill), rest.dtype)], axis=1)
    out_ref[:, columns:] = rest.astype(jnp.bfloat16)


def qkv_grad_call(normed, d_qkv, gain_grads, columns, *when):
    total, width = normed.shape
    block = 512
    return pl.pallas_call(
        qkv_grad_kernel,
        grid=(width // block,),
        in_specs=[
            pl.BlockSpec((total, block), lambda i: (0, i)),
            pl.BlockSpec(d_qkv.shape, lambda i: (0, 0)),
            pl.BlockSpec((gain_grads.shape[0], block), lambda i: (0, i)),
        ]
        + [pl.BlockSpec(memory_space=pl.ANY)] * len(when),
        out_specs=pl.BlockSpec((block, columns), lambda i: (i, 0)),
        out_shape=jax.ShapeDtypeStruct((width, columns), jnp.bfloat16),
        compiler_params=pltpu.CompilerParams(vmem_limit_bytes=48 * 2**20),
        cost_estimate=pl.CostEstimate(flops=60 * 10**9, bytes_accessed=0, transcendentals=0),
    )(normed, d_qkv, gain_grads, *when)


def pieces_sp(value, split, *hold):
    size = lax.axis_size("sp")
    columns = value.shape[1]
    if not split or size != 4 or columns % (2 * LANES):
        others = [(swap(value, turn),) for turn in range(1, size)]
        return [(value,)] + others, [piece for (piece,) in others], []
    half = columns // 2
    left, right = value[:, :half], value[:, half:]
    x_left, y_right = swap(left, 1), swap(right, 2)
    x_right, y_left = swap(right, 1), swap(left, 2)
    far_left, far_right = (after(v, *hold) if hold else v for v in (x_left, y_right))
    far_left, far_right = swap(far_left, 2), swap(far_right, 1)
    return (
        [(left, right), (x_left, x_right), (y_left, y_right), (far_left, far_right)],
        [x_left, y_right, x_right, y_left],
        [far_left, far_right],
    )


def spread_kernel(layout, count, chunks, place_ref, *refs):
    pieces, outs = refs[: count * chunks], refs[count * chunks :]
    size = pieces[0].shape[1]
    for place in range(count):

        @pl.when(place_ref[0] == place)
        def _():
            for part in range(count):
                for first, width, out, at, step in layout:
                    goal = at + part * step
                    while width:
                        chunk, begin = divmod(first, size)
                        some = min(width, size - begin)
                        piece = pieces[(place ^ part) * chunks + chunk]
                        outs[out][:, goal : goal + some] = piece[:, begin : begin + some].astype(jnp.float32)
                        first, goal, width = first + some, goal + some, width - some


def spread_call(place, pieces, layout, widths):
    count, chunks = len(pieces), len(pieces[0])
    rows, columns = pieces[0][0].shape
    block = rows // 5 if rows % 80 == 0 else rows
    return pl.pallas_call(
        functools.partial(spread_kernel, layout, count, chunks),
        grid=(rows // block,),
        in_specs=[pl.BlockSpec(memory_space=pltpu.SMEM)]
        + [pl.BlockSpec((block, columns), lambda i: (i, 0))] * (count * chunks),
        out_specs=[pl.BlockSpec((block, w), lambda i: (i, 0)) for w in widths],
        out_shape=[jax.ShapeDtypeStruct((rows, w), jnp.float32) for w in widths],
        compiler_params=pltpu.CompilerParams(vmem_limit_bytes=40 * 2**20),
        cost_estimate=pl.CostEstimate(
            flops=0, bytes_accessed=6 * count * chunks * rows * columns, transcendentals=0
        ),
    )(place, *[chunk for piece in pieces for chunk in piece])


def stack_kernel(count, chunks, place_ref, *refs):
    out_ref = refs[-1]
    size = refs[0].shape[1]
    for turn in range(count):
        for chunk in range(chunks):
            value = refs[turn * chunks + chunk][...].astype(jnp.float32)
            out_ref[place_ref[0] ^ turn, :, chunk * size : (chunk + 1) * size] = value


def stack_call(place, pieces, *when):
    count, chunks = len(pieces), len(pieces[0])
    rows, columns = pieces[0][0].shape
    block = 32 if rows % 32 == 0 else rows
    return pl.pallas_call(
        functools.partial(stack_kernel, count, chunks),
        grid=(rows // block,),
        in_specs=[pl.BlockSpec(memory_space=pltpu.SMEM)]
        + [pl.BlockSpec((block, columns), lambda i: (i, 0))] * (count * chunks)
        + [pl.BlockSpec(memory_space=pl.ANY)] * len(when),
        out_specs=pl.BlockSpec((count, block, chunks * columns), lambda i: (0, i, 0)),
        out_shape=jax.ShapeDtypeStruct((count, rows, chunks * columns), jnp.float32),
        compiler_params=pltpu.CompilerParams(vmem_limit_bytes=40 * 2**20),
        cost_estimate=pl.CostEstimate(
            flops=0, bytes_accessed=6 * count * chunks * rows * columns, transcendentals=0
        ),
    )(place, *[chunk for piece in pieces for chunk in piece], *when).reshape(count * rows, chunks * columns)


def pass_kernel(*refs):
    pass


def after(value, *others):
    here = pl.BlockSpec(memory_space=pl.ANY)
    return pl.pallas_call(
        pass_kernel,
        in_specs=[here] * (1 + len(others)),
        out_specs=here,
        out_shape=jax.ShapeDtypeStruct(value.shape, value.dtype),
        input_output_aliases={0: 0},
        cost_estimate=pl.CostEstimate(flops=0, bytes_accessed=0, transcendentals=0),
    )(value, *others)


def pack_kernel(groups, parts, place_ref, gate_ref, up_ref, _, out_ref):
    rows, columns = gate_ref.shape
    share = columns // (groups * parts)
    for place in range(parts):

        @pl.when(place_ref[0] == place)
        def _():
            for i, ref in enumerate((gate_ref, up_ref)):
                for j in range(groups):
                    at = (i * groups + j) * share
                    begin = (j * parts + place) * share
                    out_ref[:, at : at + share] = ref[:, begin : begin + share]


def pack_call(place, gate, up, when, groups, parts):
    rows, columns = gate.shape
    block = rows // 5 if rows % 80 == 0 else rows
    spec = pl.BlockSpec((block, columns), lambda i: (i, 0))
    return pl.pallas_call(
        functools.partial(pack_kernel, groups, parts),
        grid=(rows // block,),
        in_specs=[
            pl.BlockSpec(memory_space=pltpu.SMEM),
            spec,
            spec,
            pl.BlockSpec(memory_space=pl.ANY),
        ],
        out_specs=pl.BlockSpec((block, 2 * columns // parts), lambda i: (i, 0)),
        out_shape=jax.ShapeDtypeStruct((rows, 2 * columns // parts), gate.dtype),
        compiler_params=pltpu.CompilerParams(vmem_limit_bytes=32 * 2**20),
        cost_estimate=pl.CostEstimate(flops=0, bytes_accessed=5 * rows * columns, transcendentals=0),
    )(place, gate, up, when)


def local(
    tokens,
    cotangent,
    attn_gain,
    w_query,
    key_weight,
    value_weight,
    w_out,
    mlp_gain,
    w_gate,
    w_up,
    w_down,
    positions,
    lengths,
    deal_slots,
):
    groups = lax.axis_size("fsdp")
    parts = lax.axis_size("sp")
    width = tokens.shape[-1]
    rows = tokens.shape[1]
    fsdp_place = lax.axis_index("fsdp")
    sp_place = lax.axis_index("sp")
    low = jnp.bfloat16
    wide = jnp.float32

    lanes = jnp.arange(groups, dtype=jnp.int32)
    own_row = deal_slots[fsdp_place, sp_place]
    target = own_row // groups
    pick_send = jnp.sum(jnp.where(target[None, :] == lanes[:, None], lanes[None, :], 0), axis=1)
    column = deal_slots[:, sp_place, :]
    arrived_slot = jnp.sum(jnp.where(column // groups == fsdp_place, column % groups, 0), axis=1)
    pick_place = jnp.sum(
        jnp.where(arrived_slot[None, :] == lanes[:, None], lanes[None, :], 0), axis=1
    )

    def picked(given):
        return rows_of(given.reshape(groups, -1, width), pick_send)

    def deal(blocks):
        return lax.all_to_all(blocks, "fsdp", split_axis=0, concat_axis=0, tiled=True)

    def in_place(came):
        return rows_of(came, pick_place).reshape(rows, width)

    def blocks_back(owned):
        return rows_of(owned.reshape(groups, -1, width), arrived_slot)

    def scatter_fsdp(matrix):
        return lax.psum_scatter(matrix, "fsdp", scatter_dimension=0, tiled=True)

    def column_share(weight):
        share = weight.shape[1] // parts
        return lax.dynamic_slice_in_dim(weight, sp_place * share, share, axis=1)

    def gather_fsdp(shard):
        return lax.all_gather(shard, "fsdp", axis=0, tiled=True)

    ff_rows = w_down.shape[0]
    ff_share = ff_rows // parts

    query_cols = w_query.shape[1] // parts
    key_cols = key_weight.shape[1] // parts
    qkv_cols = query_cols + 2 * key_cols
    extra = -qkv_cols % 128
    extra = extra if extra else 128
    gains = jnp.pad(jnp.stack([attn_gain, mlp_gain], axis=1), ((0, 0), (0, extra - 2)))
    place = sp_place.reshape(1)
    came_tokens = deal(picked(tokens))
    gate_up_shard = pack_call(place, w_gate, w_up, came_tokens, groups, parts)
    qkv_shard = jnp.concatenate(
        [column_share(w_query), column_share(key_weight), column_share(value_weight), gains], axis=1
    )
    came_incoming = deal(after(picked(cotangent), came_tokens))
    out_all = gather_fsdp(column_share(w_out))
    qkv_all = gather_fsdp(after(qkv_shard, came_tokens, out_all))
    gate_up_all = gather_fsdp(gate_up_shard)
    down_all = gather_fsdp(lax.dynamic_slice_in_dim(w_down, sp_place * ff_share, ff_share, axis=0))
    gain_one = qkv_all[:, qkv_cols].astype(wide)[None, :]
    gain_two = qkv_all[:, qkv_cols + 1].astype(wide)[None, :]

    group_inputs = gather_sp(in_place(came_tokens))[0].reshape(-1, width)
    group_positions = gather_small(positions.reshape(-1)).reshape(-1)
    total = group_inputs.shape[0]

    cosine, sine = rotary_tables(group_positions)
    heads, keys = query_cols // HEAD_SIZE, key_cols // HEAD_SIZE
    normed, query_low, key_low, value_low = qkv_call(
        group_inputs, gain_one, qkv_all, cosine, sine, heads, keys
    )
    sizes = lengths.reshape(-1)
    ends = jnp.cumsum(sizes)
    places = jnp.arange(total, dtype=jnp.int32)
    start = jnp.sum(jnp.where(places[:, None] >= ends[None, :], sizes[None, :], 0), axis=1)
    own_mixed, logs = attend_call(query_low, key_low, value_low, start[:, None])

    share = width // parts

    def own_columns(matrix):
        return lax.dynamic_slice_in_dim(matrix, sp_place * share, share, axis=1)

    mixed, _ = gather_sp(own_mixed)
    own_hidden = out_call(mixed, out_all, own_columns(group_inputs))
    hidden_low, normed_two = norm_call(gather_sp(own_hidden)[0], gain_two)

    active_low, gate, upward = gate_up_call(normed_two, gate_up_all)
    own_incoming = after(in_place(after(came_incoming, own_hidden)), normed_two)
    group_incoming = gather_sp(own_incoming, active_low)[0].reshape(-1, width)
    grad_down = rows_call(active_low, group_incoming)
    result_part = product_call(active_low, down_all, grad_down)
    d_gate, d_up = unit_back_call(group_incoming, down_all, gate, upward, result_part)
    grad_gate = rows_call(normed_two, d_gate)
    result_sum, sums_result, last_result, _ = scatter_sp(
        result_part.reshape(parts, rows, width), lambda first: (grad_gate,)
    )
    own_hidden_rows = lax.dynamic_slice_in_dim(hidden_low, sp_place * rows, rows, axis=0)
    blocks_result = blocks_back((own_hidden_rows.astype(wide) + result_sum).astype(low))

    back_two, grad_gain_two = mlp_back_call(
        d_gate, d_up, gate_up_all, hidden_low, gain_two, parts, grad_gate, *sums_result
    )
    from_others, _, _, (grad_up,) = scatter_sp(
        after(back_two, *last_result), lambda first: (rows_call(normed_two, d_up, *first),)
    )
    gone_result = deal(blocks_result)
    own_d_hidden = own_columns(group_incoming).astype(wide) + from_others
    d_branch = own_d_hidden.astype(low)
    d_mixed, _, _, (grad_out,) = scatter_sp(
        out_back_call(d_branch, out_all, parts), lambda first: (stack_rows_call(mixed, d_branch, *first),)
    )
    d_mixed = d_mixed.astype(low)

    down_sum = after(scatter_fsdp(grad_down), d_mixed)
    down_pieces, down_first, _ = pieces_sp(down_sum, False)
    gate_sum = after(scatter_fsdp(grad_gate), *down_first)
    gate_pieces, gate_first, _ = pieces_sp(gate_sum, False)
    d_qkv = attend_back_call(
        query_low, key_low, value_low, d_mixed, logs.T, start[None, :], cosine, sine, gone_result
    )
    back_one, grad_gain_one = attend_norm_call(
        place, d_qkv, qkv_all, group_inputs, gain_one, own_d_hidden, parts, *down_first
    )
    gain_grads = jnp.concatenate(
        [grad_gain_one, grad_gain_two, jnp.zeros((6, width), wide)], axis=0
    )
    layer_out = rows_of(gone_result, target).reshape(tokens.shape)

    grad_qkv = qkv_grad_call(normed, d_qkv, gain_grads, qkv_all.shape[1], *gate_first[:-1])
    d_inputs, _, _, (down_shard, layer_out) = scatter_sp(
        back_one.reshape(parts, rows, width),
        lambda first: (stack_call(place, down_pieces, *first), layer_out),
    )
    gone_grad = deal(blocks_back(d_inputs.astype(low)))
    input_grad = rows_of(gone_grad, target).reshape(tokens.shape)

    hidden_layout = [
        (j * ff_share, ff_share, 0, j * parts * ff_share, ff_share) for j in range(groups)
    ]
    (gate_shard,) = spread_call(place, gate_pieces, hidden_layout, [w_gate.shape[1]])
    up_pieces, up_first, _ = pieces_sp(scatter_fsdp(after(grad_up, d_branch)), True)
    out_sum = after(scatter_fsdp(after(grad_out, d_mixed)), *up_first[:2])
    out_pieces = pieces_sp(out_sum, False)[0]
    qkv_pieces = pieces_sp(after(scatter_fsdp(grad_qkv), out_sum), True, gate_shard)[0]
    (up_shard,) = spread_call(place, up_pieces, hidden_layout, [w_up.shape[1]])
    (out_shard,) = spread_call(place, out_pieces, [(0, share, 0, 0, share)], [width])
    qkv_layout = [
        (0, query_cols, 0, 0, query_cols),
        (query_cols, key_cols, 1, 0, key_cols),
        (query_cols + key_cols, key_cols, 2, 0, key_cols),
        (qkv_cols, 2, 3, 0, 2),
    ]
    query_shard, key_shard, value_shard, gain_parts = spread_call(
        place,
        qkv_pieces,
        qkv_layout,
        [w_query.shape[1], key_weight.shape[1], value_weight.shape[1], 2 * parts],
    )
    gain_shards = jnp.sum(gain_parts.reshape(-1, parts, 2), axis=1)
    return (
        layer_out,
        input_grad,
        gain_shards[:, 0],
        query_shard,
        key_shard,
        value_shard,
        out_shard,
        gain_shards[:, 1],
        gate_shard,
        up_shard,
        down_shard,
    )


def solution(mesh):
    placed = (
        P("fsdp", "sp", None),
        P("fsdp", "sp", None),
        P("fsdp"),
        P("fsdp", None),
        P("fsdp", None),
        P("fsdp", None),
        P("fsdp", None),
        P("fsdp"),
        P("fsdp", None),
        P("fsdp", None),
        P("fsdp", None),
        P("fsdp", "sp"),
        P("fsdp", None),
        P(),
    )
    return jax.shard_map(
        local,
        mesh=mesh,
        in_specs=placed,
        out_specs=(
            P("fsdp", "sp", None),
            P("fsdp", "sp", None),
            P("fsdp"),
            P("fsdp", None),
            P("fsdp", None),
            P("fsdp", None),
            P("fsdp", None),
            P("fsdp"),
            P("fsdp", None),
            P("fsdp", None),
            P("fsdp", None),
        ),
        check_vma=False,
    )
```

```python
import functools
import jax
import jax.numpy as jnp
from jax import lax
from jax.experimental import pallas as pl
from jax.experimental.pallas import tpu as pltpu
from jax.experimental.layout import Layout, with_layout_constraint
from jax.sharding import PartitionSpec as P

QUERY_HEADS = 32
KEY_VALUE_HEADS = 8
HEAD_SIZE = 80
LANES = 128


eps = 1e-05
theta = 1000000.0
log2e = 1.4426950408889634


def swap(value, bit):
    size = lax.axis_size("sp")
    return lax.ppermute(value, "sp", [(i, i ^ bit) for i in range(size)])


def row_major(value):
    return with_layout_constraint(value, Layout(major_to_minor=tuple(range(value.ndim))))


def gather_sp(value, *hold):
    size = lax.axis_size("sp")
    if size != 4:
        whole = lax.all_gather(value, "sp", axis=0, tiled=False)
        return whole, (whole,)
    place = lax.axis_index("sp")
    half = value.shape[0] // 2
    first, second = value[:half], value[half:]
    x_first, y_second = swap(first, 1), swap(second, 2)
    x_second, y_first = swap(second, 1), swap(first, 2)
    far_first, far_second = (after(v, *hold) if hold else v for v in (x_first, y_second))
    far_first, far_second = swap(far_first, 2), swap(far_second, 1)
    out = jnp.zeros((size,) + value.shape, value.dtype)
    if hold:
        out = after(out, *hold)
    zeros = (0,) * (value.ndim - 1)
    for turn, low, high in (
        (0, first, second),
        (1, x_first, x_second),
        (2, y_first, y_second),
        (3, far_first, far_second),
    ):
        out = lax.dynamic_update_slice(out, low[None], (place ^ turn, 0) + zeros)
        out = lax.dynamic_update_slice(out, high[None], (place ^ turn, half) + zeros)
    return row_major(out), (x_first, y_second)


def rows_of(blocks, picks):
    return blocks.at[picks].get(mode="promise_in_bounds")


def gather_small(value):
    size = lax.axis_size("sp")
    if size != 4:
        return lax.all_gather(value, "sp", axis=0, tiled=False)
    place = lax.axis_index("sp")
    pieces = [value] + [swap(value, turn) for turn in range(1, size)]
    here = [
        sum(jnp.where(place ^ turn == i, pieces[turn], 0) for turn in range(size)) for i in range(size)
    ]
    return jnp.stack(here, axis=0)


def scatter_sp(parts, hook=None):
    size = lax.axis_size("sp")
    if size != 4:
        summed = lax.psum_scatter(parts, "sp", scatter_dimension=0, tiled=False)
        given = hook((summed,)) if hook else ()
        return summed.astype(jnp.float32), (summed,), (summed,), given
    place = lax.axis_index("sp")
    half = parts.shape[1] // 2
    parts = row_major(parts)

    def block(parts, turn, lower):
        start = (place ^ turn, 0 if lower else half) + (0,) * (parts.ndim - 2)
        return lax.dynamic_slice(parts, start, (1, half) + parts.shape[2:])[0]

    wide = jnp.float32
    low = parts.dtype

    def added(*values):
        values = lax.optimization_barrier(values)
        total = values[0].astype(wide)
        for value in values[1:]:
            total = total + value.astype(wide)
        return total

    far = block(parts, 3, True), block(parts, 3, False)
    from_x, from_y = swap(far[0], 1), swap(far[1], 2)
    parts = after(parts, *far)
    given = hook((from_x, from_y)) if hook else ()
    if given:
        from_x, from_y = after(from_x, *given), after(from_y, *given)
    x_first, y_second = swap(block(parts, 1, True), 1), swap(block(parts, 2, False), 2)
    y_sent = added(block(parts, 2, True), from_x).astype(low)
    x_sent = added(block(parts, 1, False), from_y).astype(low)
    y_first, x_second = swap(y_sent, 2), swap(x_sent, 1)
    first = added(block(parts, 0, True), x_first, y_first)
    second = added(block(parts, 0, False), y_second, x_second)
    stage = (y_sent, x_sent, x_first, y_second)
    return jnp.concatenate([first, second], axis=0), stage, (y_first, x_second), given


def rotary_tables(positions):
    halves = HEAD_SIZE // 2
    frequency = theta ** (-(2.0 * jnp.arange(halves, dtype=jnp.float32)) / HEAD_SIZE)
    angles = positions.astype(jnp.float32)[:, None] * frequency[None, :]
    cosine, sine = jnp.cos(angles), jnp.sin(angles)
    rest = jnp.zeros((positions.shape[0], LANES - HEAD_SIZE), jnp.float32)
    return (
        jnp.concatenate([cosine, cosine, rest], axis=1),
        jnp.concatenate([-sine, sine, rest], axis=1),
    )


def dot(left, right):
    return jnp.dot(left, right, preferred_element_type=jnp.float32)


def dot_rows(left, right):
    return lax.dot_general(left, right, (((0,), (0,)), ((), ())), preferred_element_type=jnp.float32)


def dot_cols(left, right):
    return lax.dot_general(left, right, (((1,), (1,)), ((), ())), preferred_element_type=jnp.float32)


def head_of(matrix, head):
    first = head * HEAD_SIZE
    if first + LANES <= matrix.shape[1]:
        return matrix[:, first : first + LANES]
    kept = matrix[:, first : first + HEAD_SIZE]
    return jnp.concatenate([kept, jnp.zeros((kept.shape[0], LANES - HEAD_SIZE), kept.dtype)], axis=1)


def half_turn(padded):
    lane = lax.broadcasted_iota(jnp.int32, padded.shape, 1)
    half = HEAD_SIZE // 2
    return jnp.where(lane < half, pltpu.roll(padded, LANES - half, 1), pltpu.roll(padded, half, 1))


def qkv_kernel(heads, keys, width, x_ref, gain_ref, weight_ref, cos_ref, sin_ref, normed_ref, q_ref, k_ref, v_ref):
    x = x_ref[...].astype(jnp.float32)
    scale = lax.rsqrt(jnp.mean(x * x, axis=1, keepdims=True) + eps)
    normed = (x * scale * gain_ref[...]).astype(jnp.bfloat16)
    normed_ref[...] = normed
    rows = jnp.dot(normed, weight_ref[:, :width], preferred_element_type=jnp.float32)
    cosine, sine = cos_ref[...], sin_ref[...]
    inside = lax.broadcasted_iota(jnp.int32, cosine.shape, 1) < HEAD_SIZE
    for i in range(heads + keys):
        v = head_of(rows, i)
        turned = (v * cosine + half_turn(v) * sine).astype(jnp.bfloat16)
        if i < heads:
            q_ref[:, i * LANES : (i + 1) * LANES] = turned
        else:
            k_ref[:, (i - heads) * LANES : (i - heads + 1) * LANES] = turned
    for i in range(keys):
        v = head_of(rows, heads + keys + i)
        v_ref[:, i * LANES : (i + 1) * LANES] = jnp.where(inside, v, 0.0).astype(jnp.bfloat16)


def qkv_call(x, gain, weight, cosine, sine, heads, keys, used):
    total, width = x.shape
    block = 256
    bf = jnp.bfloat16
    row = lambda n: pl.BlockSpec((block, n), lambda i: (i, 0))
    whole = lambda a: pl.BlockSpec(a.shape, lambda i: (0, 0))
    return pl.pallas_call(
        functools.partial(qkv_kernel, heads, keys, used),
        grid=(total // block,),
        in_specs=[row(width), whole(gain), whole(weight), row(LANES), row(LANES)],
        out_specs=[row(width), row(heads * LANES), row(keys * LANES), row(keys * LANES)],
        out_shape=[
            jax.ShapeDtypeStruct((total, width), bf),
            jax.ShapeDtypeStruct((total, heads * LANES), bf),
            jax.ShapeDtypeStruct((total, keys * LANES), bf),
            jax.ShapeDtypeStruct((total, keys * LANES), bf),
        ],
        compiler_params=pltpu.CompilerParams(vmem_limit_bytes=48 * 2**20),
        cost_estimate=pl.CostEstimate(
            flops=96 * 10**9, bytes_accessed=0, transcendentals=0
        ),
    )(x, gain, weight, cosine, sine)


def attend_kernel(heads, keys, block, q_ref, k_ref, v_ref, start_ref, *refs):
    mixed_ref, lse_ref, bias_ref = refs[-3:]
    total = q_ref.shape[0]
    group = heads // keys
    factor = HEAD_SIZE**-0.5 * log2e
    for i in range(total // block):
        first, stop = i * block, (i + 1) * block
        column = lax.broadcasted_iota(jnp.int32, (block, stop), 1)
        row = lax.broadcasted_iota(jnp.int32, (block, stop), 0) + first
        good = (column >= start_ref[first:stop, :]) & (column <= row)
        bias_ref[:, :stop] = jnp.where(good, 0.0, -1e30)
        for head in range(heads):
            lanes = slice(head * LANES, (head + 1) * LANES)
            key = slice(head // group * LANES, (head // group + 1) * LANES)
            scores = dot_cols(q_ref[first:stop, lanes], k_ref[:stop, key]) * factor + bias_ref[:, :stop]
            top = jnp.max(scores, axis=1, keepdims=True)
            weights = jnp.exp2(scores - top)
            summed = jnp.sum(weights, axis=1, keepdims=True)
            mixed = jnp.dot(
                weights.astype(jnp.bfloat16), v_ref[:stop, key], preferred_element_type=jnp.float32
            ) / summed
            mixed_ref[first:stop, head * HEAD_SIZE : (head + 1) * HEAD_SIZE] = mixed[:, :HEAD_SIZE].astype(
                jnp.bfloat16
            )
            lse_ref[first:stop, head : head + 1] = top + jnp.log2(summed)


def attend_call(q, k, v, start, *when):
    block = 256
    total = q.shape[0]
    heads, keys = q.shape[1] // LANES, k.shape[1] // LANES
    return pl.pallas_call(
        functools.partial(attend_kernel, heads, keys, block),
        in_specs=[pl.BlockSpec(memory_space=pltpu.VMEM)] * 4
        + [pl.BlockSpec(memory_space=pl.ANY)] * len(when),
        out_shape=[
            jax.ShapeDtypeStruct((total, heads * HEAD_SIZE), jnp.bfloat16),
            jax.ShapeDtypeStruct((total, heads), jnp.float32),
        ],
        scratch_shapes=[pltpu.VMEM((block, total), jnp.float32)],
        compiler_params=pltpu.CompilerParams(vmem_limit_bytes=56 * 2**20),
        cost_estimate=pl.CostEstimate(
            flops=112 * 10**9, bytes_accessed=0, transcendentals=0
        ),
    )(q, k, v, start, *when)


def attend_back_kernel(
    heads, keys, block, q_ref, k_ref, v_ref, grad_ref, lse_ref, start_ref, cos_ref, sin_ref, *refs
):
    out_ref, bias_ref, dk_ref, dv_ref = refs[-4:]
    total = q_ref.shape[0]
    group = heads // keys
    scale = HEAD_SIZE**-0.5
    factor = scale * log2e
    low = jnp.bfloat16
    dk_ref[...] = jnp.zeros_like(dk_ref)
    dv_ref[...] = jnp.zeros_like(dv_ref)
    inside = lax.broadcasted_iota(jnp.int32, (block, LANES), 1) < HEAD_SIZE
    half = HEAD_SIZE // 2

    def turned_back(w, rows):
        w = w.astype(low).astype(jnp.float32)
        scaled = w * sin_ref[rows, :]
        lane = lax.broadcasted_iota(jnp.int32, w.shape, 1)
        moved = jnp.where(lane < half, pltpu.roll(scaled, LANES - half, 1), pltpu.roll(scaled, half, 1))
        return (w * cos_ref[rows, :] + moved).astype(low)

    for i in range(total // block):
        first, stop = i * block, (i + 1) * block
        rows = slice(first, stop)
        key_place = lax.broadcasted_iota(jnp.int32, (stop, block), 0)
        place = lax.broadcasted_iota(jnp.int32, (stop, block), 1) + first
        good = (key_place >= start_ref[:, rows]) & (key_place <= place)
        bias_ref[:stop, :] = jnp.where(good, 0.0, -1e30)
        grads = grad_ref[rows, :].astype(jnp.float32)
        for head in range(heads):
            lanes = slice(head * LANES, (head + 1) * LANES)
            key = slice(head // group * LANES, (head // group + 1) * LANES)
            query = q_ref[rows, lanes]
            grad = jnp.where(inside, head_of(grads, head), 0.0).astype(low)
            scores = dot_cols(k_ref[:stop, key], query) * factor + bias_ref[:stop, :]
            probs = jnp.exp2(scores - lse_ref[head : head + 1, rows])
            dv_ref[:stop, key] += jnp.dot(probs.astype(low), grad, preferred_element_type=jnp.float32)
            d_probs = dot_cols(v_ref[:stop, key], grad)
            delta = jnp.sum(probs * d_probs, axis=0, keepdims=True)
            d_scores = (probs * (d_probs - delta)).astype(low)
            dk_ref[:stop, key] += jnp.dot(d_scores, query, preferred_element_type=jnp.float32)
            d_query = dot_rows(d_scores, k_ref[:stop, key]) * scale
            out_ref[rows, head * HEAD_SIZE : (head + 1) * HEAD_SIZE] = turned_back(d_query, rows)[:, :HEAD_SIZE]
    for i in range(total // block):
        rows = slice(i * block, (i + 1) * block)
        for j in range(keys):
            lanes = slice(j * LANES, (j + 1) * LANES)
            at = (heads + j) * HEAD_SIZE
            out_ref[rows, at : at + HEAD_SIZE] = turned_back(dk_ref[rows, lanes] * scale, rows)[:, :HEAD_SIZE]
            at = (heads + keys + j) * HEAD_SIZE
            out_ref[rows, at : at + HEAD_SIZE] = dv_ref[rows, lanes][:, :HEAD_SIZE].astype(low)


def attend_back_call(q, k, v, grad, lse_rows, start_row, cosine, sine_back, *when):
    block = 256
    total = q.shape[0]
    heads, keys = q.shape[1] // LANES, k.shape[1] // LANES
    return pl.pallas_call(
        functools.partial(attend_back_kernel, heads, keys, block),
        in_specs=[pl.BlockSpec(memory_space=pltpu.VMEM)] * 8
        + [pl.BlockSpec(memory_space=pl.ANY)] * len(when),
        out_shape=jax.ShapeDtypeStruct((total, (heads + 2 * keys) * HEAD_SIZE), jnp.bfloat16),
        scratch_shapes=[
            pltpu.VMEM((total, block), jnp.float32),
            pltpu.VMEM((total, keys * LANES), jnp.float32),
            pltpu.VMEM((total, keys * LANES), jnp.float32),
        ],
        compiler_params=pltpu.CompilerParams(vmem_limit_bytes=56 * 2**20),
        cost_estimate=pl.CostEstimate(
            flops=200 * 10**9, bytes_accessed=0, transcendentals=0
        ),
    )(q, k, v, grad, lse_rows, start_row, cosine, sine_back, *when)

def gate_up_kernel(x_ref, gate_weight_ref, up_weight_ref, active_ref, gate_ref, up_ref):
    x = x_ref[...]
    gate = jnp.dot(x, gate_weight_ref[...], preferred_element_type=jnp.float32)
    upward = jnp.dot(x, up_weight_ref[...], preferred_element_type=jnp.float32)
    active_ref[...] = (gate / (1.0 + jnp.exp(-gate)) * upward).astype(jnp.bfloat16)
    gate_ref[...] = gate.astype(jnp.bfloat16)
    up_ref[...] = upward.astype(jnp.bfloat16)


def unit_block(units):
    return 256 if units % 256 == 0 else 128


def gate_up_call(x, weights):
    total, width = x.shape
    units = weights.shape[1] // 2
    block = unit_block(units)
    count = units // block
    out = pl.BlockSpec((total, block), lambda j: (0, j))
    return pl.pallas_call(
        gate_up_kernel,
        grid=(count,),
        in_specs=[
            pl.BlockSpec((total, width), lambda j: (0, 0)),
            pl.BlockSpec((width, block), lambda j: (0, j)),
            pl.BlockSpec((width, block), lambda j: (0, j + count)),
        ],
        out_specs=[out] * 3,
        out_shape=[jax.ShapeDtypeStruct((total, units), jnp.bfloat16)] * 3,
        compiler_params=pltpu.CompilerParams(vmem_limit_bytes=56 * 2**20),
        cost_estimate=pl.CostEstimate(
            flops=148 * 10**9, bytes_accessed=0, transcendentals=0
        ),
    )(x, weights, weights)


def unit_back_kernel(incoming_ref, down_ref, gate_ref, up_ref, *refs):
    d_gate_ref, d_up_ref = refs[-2:]
    d_active = dot_cols(incoming_ref[...], down_ref[...])
    gate = gate_ref[...].astype(jnp.float32)
    upward = up_ref[...].astype(jnp.float32)
    logistic = 1.0 / (1.0 + jnp.exp(-gate))
    d_gate_ref[...] = (d_active * upward * logistic * (1.0 + gate * (1.0 - logistic))).astype(jnp.bfloat16)
    d_up_ref[...] = (d_active * gate * logistic).astype(jnp.bfloat16)


def unit_back_call(incoming, down, gate, up, *when):
    total, width = incoming.shape
    units = down.shape[0]
    block = unit_block(units)
    column = pl.BlockSpec((total, block), lambda j: (0, j))
    return pl.pallas_call(
        unit_back_kernel,
        grid=(units // block,),
        in_specs=[
            pl.BlockSpec((total, width), lambda j: (0, 0)),
            pl.BlockSpec((block, width), lambda j: (j, 0)),
            column,
            column,
        ]
        + [pl.BlockSpec(memory_space=pl.ANY)] * len(when),
        out_specs=[column] * 2,
        out_shape=[jax.ShapeDtypeStruct((total, units), jnp.bfloat16)] * 2,
        compiler_params=pltpu.CompilerParams(vmem_limit_bytes=56 * 2**20),
        cost_estimate=pl.CostEstimate(
            flops=104 * 10**9, bytes_accessed=0, transcendentals=0
        ),
    )(incoming, down, gate, up, *when)


def norm_back(d_normed, x, gain):
    scale = lax.rsqrt(jnp.mean(x * x, axis=1, keepdims=True) + eps)
    grad_gain = jnp.sum(d_normed * (x * scale), axis=0, keepdims=True)
    scaled = d_normed * gain
    inner = jnp.mean(scaled * x, axis=1, keepdims=True)
    return scale * scaled - x * (scale * scale * scale * inner), grad_gain


def add_up(ref, value):
    @pl.when(pl.program_id(0) == 0)
    def _():
        ref[...] = jnp.zeros_like(ref)

    ref[...] += value


def mlp_back_kernel(d_gate_ref, d_up_ref, weight_ref, x_ref, gain_ref, *refs):
    out_ref, grad_ref = refs[-2:]
    units = d_gate_ref.shape[1]
    d_normed = dot_cols(d_gate_ref[...], weight_ref[:, :units]) + dot_cols(
        d_up_ref[...], weight_ref[:, units:]
    )
    back, grad_gain = norm_back(d_normed, x_ref[...].astype(jnp.float32), gain_ref[...])
    parts, _, share = out_ref.shape
    for i in range(parts):
        out_ref[i] = back[:, i * share : (i + 1) * share].astype(jnp.bfloat16)
    add_up(grad_ref, grad_gain)


def mlp_back_call(d_gate, d_up, weights, x, gain, parts, *when):
    total, units = d_gate.shape
    width = x.shape[1]
    share = width // parts
    block = 512
    row = lambda n: pl.BlockSpec((block, n), lambda i: (i, 0))
    whole = lambda a: pl.BlockSpec(a.shape, lambda i: (0, 0), pipeline_mode=pl.Buffered(1))
    return pl.pallas_call(
        mlp_back_kernel,
        grid=(total // block,),
        in_specs=[row(units), row(units), whole(weights), row(width), whole(gain)]
        + [pl.BlockSpec(memory_space=pl.ANY)] * len(when),
        out_specs=[
            pl.BlockSpec((parts, block, share), lambda i: (0, i, 0)),
            pl.BlockSpec((1, width), lambda i: (0, 0)),
        ],
        out_shape=[
            jax.ShapeDtypeStruct((parts, total, share), jnp.bfloat16),
            jax.ShapeDtypeStruct((1, width), jnp.float32),
        ],
        compiler_params=pltpu.CompilerParams(vmem_limit_bytes=60 * 2**20),
        cost_estimate=pl.CostEstimate(
            flops=176 * 10**9, bytes_accessed=0, transcendentals=0
        ),
    )(d_gate, d_up, weights, x, gain, *when)


def attend_norm_kernel(parts, place_ref, d_qkv_ref, weight_ref, x_ref, gain_ref, own_ref, *refs):
    out_ref, grad_ref = refs[-2:]
    d_normed = dot_cols(d_qkv_ref[...], weight_ref[:, : d_qkv_ref.shape[1]])
    back, grad_gain = norm_back(d_normed, x_ref[...].astype(jnp.float32), gain_ref[...])
    out_ref[...] = back.astype(jnp.bfloat16)
    share = own_ref.shape[1]
    for place in range(parts):

        @pl.when(place_ref[0] == place)
        def _():
            lanes = slice(place * share, (place + 1) * share)
            out_ref[:, lanes] = (back[:, lanes] + own_ref[...]).astype(jnp.bfloat16)

    add_up(grad_ref, grad_gain)


def attend_norm_call(place, d_qkv, weights, x, gain, own, parts, *when):
    total, width = x.shape
    block = 256
    row = lambda n: pl.BlockSpec((block, n), lambda i: (i, 0))
    whole = lambda a: pl.BlockSpec(a.shape, lambda i: (0, 0), pipeline_mode=pl.Buffered(1))
    return pl.pallas_call(
        functools.partial(attend_norm_kernel, parts),
        grid=(total // block,),
        in_specs=[
            pl.BlockSpec(memory_space=pltpu.SMEM),
            row(d_qkv.shape[1]),
            whole(weights),
            row(width),
            whole(gain),
            row(own.shape[1]),
        ]
        + [pl.BlockSpec(memory_space=pl.ANY)] * len(when),
        out_specs=[row(width), pl.BlockSpec((1, width), lambda i: (0, 0))],
        out_shape=[
            jax.ShapeDtypeStruct((total, width), jnp.bfloat16),
            jax.ShapeDtypeStruct((1, width), jnp.float32),
        ],
        compiler_params=pltpu.CompilerParams(vmem_limit_bytes=56 * 2**20),
        cost_estimate=pl.CostEstimate(
            flops=80 * 10**9, bytes_accessed=0, transcendentals=0
        ),
    )(place, d_qkv, weights, x, gain, own, *when)


def out_back_kernel(d_ref, weight_ref, *refs):
    refs[-1][0] = dot_cols(d_ref[...], weight_ref[...]).astype(jnp.bfloat16)


def out_back_call(d_branch, weights, parts, *when):
    total, share = d_branch.shape
    rows = weights.shape[0] // parts
    return pl.pallas_call(
        out_back_kernel,
        grid=(parts,),
        in_specs=[
            pl.BlockSpec((total, share), lambda i: (0, 0)),
            pl.BlockSpec((rows, share), lambda i: (i, 0)),
        ]
        + [pl.BlockSpec(memory_space=pl.ANY)] * len(when),
        out_specs=pl.BlockSpec((1, total, rows), lambda i: (i, 0, 0)),
        out_shape=jax.ShapeDtypeStruct((parts, total, rows), jnp.bfloat16),
        compiler_params=pltpu.CompilerParams(vmem_limit_bytes=32 * 2**20),
        cost_estimate=pl.CostEstimate(
            flops=32 * 10**9, bytes_accessed=0, transcendentals=0
        ),
    )(d_branch, weights, *when)


def norm_kernel(stack_ref, gain_ref, x_ref, normed_ref):
    parts, _, share = stack_ref.shape
    squares = 0.0
    for i in range(parts):
        piece = stack_ref[i].astype(jnp.float32)
        squares = squares + jnp.sum(piece * piece, axis=1, keepdims=True)
    scale = lax.rsqrt(squares / (parts * share) + eps)
    for i in range(parts):
        lanes = slice(i * share, (i + 1) * share)
        x_ref[:, lanes] = stack_ref[i]
        normed = stack_ref[i].astype(jnp.float32) * scale * gain_ref[:, lanes]
        normed_ref[:, lanes] = normed.astype(jnp.bfloat16)


def norm_call(stack, gain):
    parts, total, share = stack.shape
    block = 256
    row = pl.BlockSpec((block, parts * share), lambda i: (i, 0))
    return pl.pallas_call(
        norm_kernel,
        grid=(total // block,),
        in_specs=[
            pl.BlockSpec((parts, block, share), lambda i: (0, i, 0)),
            pl.BlockSpec((1, parts * share), lambda i: (0, 0)),
        ],
        out_specs=[row, row],
        out_shape=[jax.ShapeDtypeStruct((total, parts * share), jnp.bfloat16)] * 2,
        compiler_params=pltpu.CompilerParams(vmem_limit_bytes=32 * 2**20),
        cost_estimate=pl.CostEstimate(flops=32 * 10**9, bytes_accessed=0, transcendentals=0),
    )(stack, gain)


def out_kernel(stack_ref, weight_ref, x_ref, out_ref):
    parts, _, depth = stack_ref.shape
    total = x_ref[...].astype(jnp.float32)
    for i in range(parts):
        total = total + jnp.dot(
            stack_ref[i], weight_ref[i * depth : (i + 1) * depth, :], preferred_element_type=jnp.float32
        )
    out_ref[...] = total.astype(jnp.bfloat16)


def out_call(stack, weight, x):
    parts, total, depth = stack.shape
    columns = weight.shape[1]
    block = 512
    row = pl.BlockSpec((block, columns), lambda i: (i, 0))
    return pl.pallas_call(
        out_kernel,
        grid=(total // block,),
        in_specs=[
            pl.BlockSpec((parts, block, depth), lambda i: (0, i, 0)),
            pl.BlockSpec(weight.shape, lambda i: (0, 0)),
            row,
        ],
        out_specs=row,
        out_shape=jax.ShapeDtypeStruct((total, columns), jnp.bfloat16),
        compiler_params=pltpu.CompilerParams(vmem_limit_bytes=40 * 2**20),
        cost_estimate=pl.CostEstimate(flops=36 * 10**9, bytes_accessed=0, transcendentals=0),
    )(stack, weight, x)


def stack_rows_kernel(left_ref, right_ref, *refs):
    refs[-1][...] = dot_rows(left_ref[0], right_ref[...]).astype(jnp.bfloat16)


def stack_rows_call(stack, right, *when):
    parts, total, rows = stack.shape
    columns = right.shape[1]
    return pl.pallas_call(
        stack_rows_kernel,
        grid=(parts,),
        in_specs=[
            pl.BlockSpec((1, total, rows), lambda i: (i, 0, 0)),
            pl.BlockSpec((total, columns), lambda i: (0, 0)),
        ]
        + [pl.BlockSpec(memory_space=pl.ANY)] * len(when),
        out_specs=pl.BlockSpec((rows, columns), lambda i: (i, 0)),
        out_shape=jax.ShapeDtypeStruct((parts * rows, columns), jnp.bfloat16),
        compiler_params=pltpu.CompilerParams(vmem_limit_bytes=40 * 2**20),
        cost_estimate=pl.CostEstimate(flops=0 * 10**9, bytes_accessed=0, transcendentals=0),
    )(stack, right, *when)


def rows_kernel(left_ref, right_ref, *refs):
    refs[-1][...] = dot_rows(left_ref[...], right_ref[...]).astype(jnp.bfloat16)


def rows_call(left, right, *when):
    total, rows = left.shape
    columns = right.shape[1]
    block = 256 if columns % 256 == 0 else 128
    return pl.pallas_call(
        rows_kernel,
        grid=(columns // block,),
        in_specs=[
            pl.BlockSpec((total, rows), lambda j: (0, 0)),
            pl.BlockSpec((total, block), lambda j: (0, j)),
        ]
        + [pl.BlockSpec(memory_space=pl.ANY)] * len(when),
        out_specs=pl.BlockSpec((rows, block), lambda j: (0, j)),
        out_shape=jax.ShapeDtypeStruct((rows, columns), jnp.bfloat16),
        compiler_params=pltpu.CompilerParams(vmem_limit_bytes=56 * 2**20),
        cost_estimate=pl.CostEstimate(flops=0 if when else 80 * 10**9, bytes_accessed=0, transcendentals=0),
    )(left, right, *when)


def product_kernel(left_ref, right_ref, *refs):
    refs[-1][...] = jnp.dot(left_ref[...], right_ref[...], preferred_element_type=jnp.float32).astype(
        jnp.bfloat16
    )


def product_call(left, right, *when):
    total, depth = left.shape
    columns = right.shape[1]
    block = 256 if columns % 256 == 0 else 128
    return pl.pallas_call(
        product_kernel,
        grid=(columns // block,),
        in_specs=[
            pl.BlockSpec((total, depth), lambda j: (0, 0)),
            pl.BlockSpec((depth, block), lambda j: (0, j)),
        ]
        + [pl.BlockSpec(memory_space=pl.ANY)] * len(when),
        out_specs=pl.BlockSpec((total, block), lambda j: (0, j)),
        out_shape=jax.ShapeDtypeStruct((total, columns), jnp.bfloat16),
        compiler_params=pltpu.CompilerParams(vmem_limit_bytes=56 * 2**20),
        cost_estimate=pl.CostEstimate(flops=80 * 10**9, bytes_accessed=0, transcendentals=0),
    )(left, right, *when)


def qkv_grad_kernel(normed_ref, d_qkv_ref, gain_ref, *refs):
    out_ref = refs[-1]
    columns = d_qkv_ref.shape[1]
    out_ref[:, :columns] = dot_rows(normed_ref[...], d_qkv_ref[...]).astype(jnp.bfloat16)
    rest = jnp.transpose(gain_ref[...])
    fill = out_ref.shape[1] - columns - rest.shape[1]
    if fill:
        rest = jnp.concatenate([rest, jnp.zeros((rest.shape[0], fill), rest.dtype)], axis=1)
    out_ref[:, columns:] = rest.astype(jnp.bfloat16)


def qkv_grad_call(normed, d_qkv, gain_grads, columns, *when):
    total, width = normed.shape
    block = 512
    return pl.pallas_call(
        qkv_grad_kernel,
        grid=(width // block,),
        in_specs=[
            pl.BlockSpec((total, block), lambda i: (0, i)),
            pl.BlockSpec(d_qkv.shape, lambda i: (0, 0)),
            pl.BlockSpec((gain_grads.shape[0], block), lambda i: (0, i)),
        ]
        + [pl.BlockSpec(memory_space=pl.ANY)] * len(when),
        out_specs=pl.BlockSpec((block, columns), lambda i: (i, 0)),
        out_shape=jax.ShapeDtypeStruct((width, columns), jnp.bfloat16),
        compiler_params=pltpu.CompilerParams(vmem_limit_bytes=48 * 2**20),
        cost_estimate=pl.CostEstimate(flops=48 * 10**9, bytes_accessed=0, transcendentals=0),
    )(normed, d_qkv, gain_grads, *when)


def pieces_sp(value, split, *hold):
    size = lax.axis_size("sp")
    columns = value.shape[1]
    if not split or size != 4 or columns % (2 * LANES):
        others = [(swap(value, turn),) for turn in range(1, size)]
        return [(value,)] + others, [piece for (piece,) in others], []
    half = columns // 2
    left, right = value[:, :half], value[:, half:]
    x_left, y_right = swap(left, 1), swap(right, 2)
    x_right, y_left = swap(right, 1), swap(left, 2)
    far_left, far_right = (after(v, *hold) if hold else v for v in (x_left, y_right))
    far_left, far_right = swap(far_left, 2), swap(far_right, 1)
    return (
        [(left, right), (x_left, x_right), (y_left, y_right), (far_left, far_right)],
        [x_left, y_right, x_right, y_left],
        [far_left, far_right],
    )


def spread_kernel(layout, count, chunks, outputs, place_ref, *refs):
    pieces, outs = refs[: count * chunks], refs[-outputs:]
    size = pieces[0].shape[1]
    for place in range(count):

        @pl.when(place_ref[0] == place)
        def _():
            for part in range(count):
                for first, width, out, at, step in layout:
                    goal = at + part * step
                    while width:
                        chunk, begin = divmod(first, size)
                        some = min(width, size - begin)
                        piece = pieces[(place ^ part) * chunks + chunk]
                        outs[out][:, goal : goal + some] = piece[:, begin : begin + some].astype(jnp.float32)
                        first, goal, width = first + some, goal + some, width - some


def spread_call(place, pieces, layout, widths, *when):
    count, chunks = len(pieces), len(pieces[0])
    rows, columns = pieces[0][0].shape
    block = rows // 5 if rows % 80 == 0 else rows
    return pl.pallas_call(
        functools.partial(spread_kernel, layout, count, chunks, len(widths)),
        grid=(rows // block,),
        in_specs=[pl.BlockSpec(memory_space=pltpu.SMEM)]
        + [pl.BlockSpec((block, columns), lambda i: (i, 0))] * (count * chunks)
        + [pl.BlockSpec(memory_space=pl.ANY)] * len(when),
        out_specs=[pl.BlockSpec((block, w), lambda i: (i, 0)) for w in widths],
        out_shape=[jax.ShapeDtypeStruct((rows, w), jnp.float32) for w in widths],
        compiler_params=pltpu.CompilerParams(vmem_limit_bytes=40 * 2**20),
        cost_estimate=pl.CostEstimate(
            flops=0, bytes_accessed=6 * count * chunks * rows * columns, transcendentals=0
        ),
    )(place, *[chunk for piece in pieces for chunk in piece], *when)


def stack_kernel(count, chunks, place_ref, *refs):
    out_ref = refs[-1]
    size = refs[0].shape[1]
    for turn in range(count):
        for chunk in range(chunks):
            value = refs[turn * chunks + chunk][...].astype(jnp.float32)
            out_ref[place_ref[0] ^ turn, :, chunk * size : (chunk + 1) * size] = value


def stack_call(place, pieces, *when):
    count, chunks = len(pieces), len(pieces[0])
    rows, columns = pieces[0][0].shape
    block = 32 if rows % 32 == 0 else rows
    return pl.pallas_call(
        functools.partial(stack_kernel, count, chunks),
        grid=(rows // block,),
        in_specs=[pl.BlockSpec(memory_space=pltpu.SMEM)]
        + [pl.BlockSpec((block, columns), lambda i: (i, 0))] * (count * chunks)
        + [pl.BlockSpec(memory_space=pl.ANY)] * len(when),
        out_specs=pl.BlockSpec((count, block, chunks * columns), lambda i: (0, i, 0)),
        out_shape=jax.ShapeDtypeStruct((count, rows, chunks * columns), jnp.float32),
        compiler_params=pltpu.CompilerParams(vmem_limit_bytes=40 * 2**20),
        cost_estimate=pl.CostEstimate(
            flops=0, bytes_accessed=6 * count * chunks * rows * columns, transcendentals=0
        ),
    )(place, *[chunk for piece in pieces for chunk in piece], *when).reshape(count * rows, chunks * columns)


def pass_kernel(*refs):
    pass


def after(value, *others):
    here = pl.BlockSpec(memory_space=pl.ANY)
    return pl.pallas_call(
        pass_kernel,
        in_specs=[here] * (1 + len(others)),
        out_specs=here,
        out_shape=jax.ShapeDtypeStruct(value.shape, value.dtype),
        input_output_aliases={0: 0},
        cost_estimate=pl.CostEstimate(flops=0, bytes_accessed=0, transcendentals=0),
    )(value, *others)


def pack_kernel(groups, parts, place_ref, gate_ref, up_ref, _, out_ref):
    rows, columns = gate_ref.shape
    share = columns // (groups * parts)
    for place in range(parts):

        @pl.when(place_ref[0] == place)
        def _():
            for i, ref in enumerate((gate_ref, up_ref)):
                for j in range(groups):
                    at = (i * groups + j) * share
                    begin = (j * parts + place) * share
                    out_ref[:, at : at + share] = ref[:, begin : begin + share]


def pack_call(place, gate, up, when, groups, parts):
    rows, columns = gate.shape
    block = rows // 5 if rows % 80 == 0 else rows
    spec = pl.BlockSpec((block, columns), lambda i: (i, 0))
    return pl.pallas_call(
        functools.partial(pack_kernel, groups, parts),
        grid=(rows // block,),
        in_specs=[
            pl.BlockSpec(memory_space=pltpu.SMEM),
            spec,
            spec,
            pl.BlockSpec(memory_space=pl.ANY),
        ],
        out_specs=pl.BlockSpec((block, 2 * columns // parts), lambda i: (i, 0)),
        out_shape=jax.ShapeDtypeStruct((rows, 2 * columns // parts), gate.dtype),
        compiler_params=pltpu.CompilerParams(vmem_limit_bytes=32 * 2**20),
        cost_estimate=pl.CostEstimate(flops=0, bytes_accessed=5 * rows * columns, transcendentals=0),
    )(place, gate, up, when)


def local(
    tokens,
    cotangent,
    attn_gain,
    w_query,
    key_weight,
    value_weight,
    w_out,
    mlp_gain,
    w_gate,
    w_up,
    w_down,
    positions,
    lengths,
    deal_slots,
):
    groups = lax.axis_size("fsdp")
    parts = lax.axis_size("sp")
    width = tokens.shape[-1]
    rows = tokens.shape[1]
    fsdp_place = lax.axis_index("fsdp")
    sp_place = lax.axis_index("sp")
    low = jnp.bfloat16
    wide = jnp.float32

    lanes = jnp.arange(groups, dtype=jnp.int32)
    own_row = deal_slots[fsdp_place, sp_place]
    target = own_row // groups
    pick_send = jnp.sum(jnp.where(target[None, :] == lanes[:, None], lanes[None, :], 0), axis=1)
    column = deal_slots[:, sp_place, :]
    arrived_slot = jnp.sum(jnp.where(column // groups == fsdp_place, column % groups, 0), axis=1)
    pick_place = jnp.sum(
        jnp.where(arrived_slot[None, :] == lanes[:, None], lanes[None, :], 0), axis=1
    )

    def picked(given):
        return rows_of(given.reshape(groups, -1, width), pick_send)

    def deal(blocks):
        return lax.all_to_all(blocks, "fsdp", split_axis=0, concat_axis=0, tiled=True)

    def in_place(came):
        return rows_of(came, pick_place).reshape(rows, width)

    def blocks_back(owned):
        return rows_of(owned.reshape(groups, -1, width), arrived_slot)

    def scatter_fsdp(matrix):
        return lax.psum_scatter(matrix, "fsdp", scatter_dimension=0, tiled=True)

    def column_share(weight):
        share = weight.shape[1] // parts
        return lax.dynamic_slice_in_dim(weight, sp_place * share, share, axis=1)

    def gather_fsdp(shard):
        return lax.all_gather(shard, "fsdp", axis=0, tiled=True)

    ff_rows = w_down.shape[0]
    ff_share = ff_rows // parts

    query_cols = w_query.shape[1] // parts
    key_cols = key_weight.shape[1] // parts
    qkv_cols = query_cols + 2 * key_cols
    extra = -qkv_cols % 128
    extra = extra if extra else 128
    gains = jnp.pad(jnp.stack([attn_gain, mlp_gain], axis=1), ((0, 0), (0, extra - 2)))
    place = sp_place.reshape(1)
    came_tokens = deal(picked(tokens))
    gate_up_shard = pack_call(place, w_gate, w_up, came_tokens, groups, parts)
    qkv_shard = jnp.concatenate(
        [column_share(w_query), column_share(key_weight), column_share(value_weight), gains], axis=1
    )
    came_incoming = deal(after(picked(cotangent), came_tokens))
    qkv_width = qkv_shard.shape[1]
    qkv_shard = jnp.concatenate([qkv_shard, column_share(w_out)], axis=1)
    qkv_all = gather_fsdp(after(qkv_shard, came_tokens))
    out_all = qkv_all[:, qkv_width:]
    gate_up_all = gather_fsdp(gate_up_shard)
    down_all = gather_fsdp(lax.dynamic_slice_in_dim(w_down, sp_place * ff_share, ff_share, axis=0))
    gain_one = qkv_all[:, qkv_cols].astype(wide)[None, :]
    gain_two = qkv_all[:, qkv_cols + 1].astype(wide)[None, :]

    group_inputs, passed = gather_sp(in_place(came_tokens))
    group_inputs = group_inputs.reshape(-1, width)
    group_positions = gather_small(after(positions.reshape(-1), passed[0])).reshape(-1)
    total = group_inputs.shape[0]

    cosine, sine = rotary_tables(group_positions)
    heads, keys = query_cols // HEAD_SIZE, key_cols // HEAD_SIZE
    normed, query_low, key_low, value_low = qkv_call(
        group_inputs, gain_one, qkv_all, cosine, sine, heads, keys, qkv_width
    )
    sizes = lengths.reshape(-1)
    ends = jnp.cumsum(sizes)
    places = jnp.arange(total, dtype=jnp.int32)
    start = jnp.sum(jnp.where(places[:, None] >= ends[None, :], sizes[None, :], 0), axis=1)
    own_mixed, logs = attend_call(query_low, key_low, value_low, start[:, None])

    share = width // parts

    def own_columns(matrix):
        return lax.dynamic_slice_in_dim(matrix, sp_place * share, share, axis=1)

    mixed, _ = gather_sp(own_mixed)
    own_hidden = out_call(mixed, out_all, own_columns(group_inputs))
    hidden_low, normed_two = norm_call(gather_sp(own_hidden)[0], gain_two)

    active_low, gate, upward = gate_up_call(normed_two, gate_up_all)
    own_incoming = after(in_place(after(came_incoming, own_hidden)), normed_two)
    group_incoming = gather_sp(own_incoming, active_low)[0].reshape(-1, width)
    grad_down = rows_call(active_low, group_incoming)
    result_part = product_call(active_low, down_all, grad_down)
    d_gate, d_up = unit_back_call(group_incoming, down_all, gate, upward, result_part)
    grad_gate = rows_call(normed_two, d_gate)
    result_sum, sums_result, last_result, _ = scatter_sp(
        result_part.reshape(parts, rows, width), lambda first: (grad_gate,)
    )
    own_hidden_rows = lax.dynamic_slice_in_dim(hidden_low, sp_place * rows, rows, axis=0)
    blocks_result = blocks_back((own_hidden_rows.astype(wide) + result_sum).astype(low))

    back_two, grad_gain_two = mlp_back_call(
        d_gate, d_up, gate_up_all, hidden_low, gain_two, parts, grad_gate, *sums_result
    )
    from_others, _, _, (grad_up,) = scatter_sp(
        after(back_two, *last_result), lambda first: (rows_call(normed_two, d_up, *first),)
    )
    gone_result = deal(blocks_result)
    own_d_hidden = own_columns(group_incoming).astype(wide) + from_others
    d_branch = own_d_hidden.astype(low)
    d_mixed, _, _, (grad_out,) = scatter_sp(
        out_back_call(d_branch, out_all, parts), lambda first: (stack_rows_call(mixed, d_branch, *first),)
    )
    d_mixed = d_mixed.astype(low)

    down_sum = after(scatter_fsdp(grad_down), d_mixed)
    down_pieces, down_first, _ = pieces_sp(down_sum, False)
    gate_sum = after(scatter_fsdp(grad_gate), d_mixed, down_sum)
    gate_pieces, gate_first, _ = pieces_sp(gate_sum, False)
    d_qkv = attend_back_call(
        query_low, key_low, value_low, d_mixed, logs.T, start[None, :], cosine, sine
    )
    back_one, grad_gain_one = attend_norm_call(
        place, d_qkv, qkv_all, group_inputs, gain_one, own_d_hidden, parts, gone_result, *down_first, *gate_first[:2]
    )
    gain_grads = jnp.concatenate(
        [grad_gain_one, grad_gain_two, jnp.zeros((6, width), wide)], axis=0
    )
    layer_out = rows_of(gone_result, target).reshape(tokens.shape)

    grad_qkv = qkv_grad_call(normed, d_qkv, gain_grads, qkv_width, *gate_first[2:])
    hidden_layout = [
        (j * ff_share, ff_share, 0, j * parts * ff_share, ff_share) for j in range(groups)
    ]

    def beside(first):
        gate_shard = spread_call(place, gate_pieces, hidden_layout, [w_gate.shape[1]], *first)[0]
        return stack_call(place, down_pieces, *first), gate_shard, layer_out

    d_inputs, _, _, (down_shard, gate_shard, layer_out) = scatter_sp(
        back_one.reshape(parts, rows, width), beside
    )
    gone_grad = deal(blocks_back(d_inputs.astype(low)))
    input_grad = rows_of(gone_grad, target).reshape(tokens.shape)

    up_pieces, up_first, _ = pieces_sp(scatter_fsdp(after(grad_up, d_branch)), True)
    out_sum = after(scatter_fsdp(after(grad_out, d_mixed)), *up_first[:2])
    out_pieces = pieces_sp(out_sum, False)[0]
    qkv_pieces = pieces_sp(after(scatter_fsdp(grad_qkv), out_sum), True)[0]
    (up_shard,) = spread_call(place, up_pieces, hidden_layout, [w_up.shape[1]])
    (out_shard,) = spread_call(place, out_pieces, [(0, share, 0, 0, share)], [width])
    qkv_layout = [
        (0, query_cols, 0, 0, query_cols),
        (query_cols, key_cols, 1, 0, key_cols),
        (query_cols + key_cols, key_cols, 2, 0, key_cols),
        (qkv_cols, 2, 3, 0, 2),
    ]
    query_shard, key_shard, value_shard, gain_parts = spread_call(
        place,
        qkv_pieces,
        qkv_layout,
        [w_query.shape[1], key_weight.shape[1], value_weight.shape[1], 2 * parts],
    )
    gain_shards = jnp.sum(gain_parts.reshape(-1, parts, 2), axis=1)
    return (
        layer_out,
        input_grad,
        gain_shards[:, 0],
        query_shard,
        key_shard,
        value_shard,
        out_shard,
        gain_shards[:, 1],
        gate_shard,
        up_shard,
        down_shard,
    )


def solution(mesh):
    placed = (
        P("fsdp", "sp", None),
        P("fsdp", "sp", None),
        P("fsdp"),
        P("fsdp", None),
        P("fsdp", None),
        P("fsdp", None),
        P("fsdp", None),
        P("fsdp"),
        P("fsdp", None),
        P("fsdp", None),
        P("fsdp", None),
        P("fsdp", "sp"),
        P("fsdp", None),
        P(),
    )
    return jax.shard_map(
        local,
        mesh=mesh,
        in_specs=placed,
        out_specs=(
            P("fsdp", "sp", None),
            P("fsdp", "sp", None),
            P("fsdp"),
            P("fsdp", None),
            P("fsdp", None),
            P("fsdp", None),
            P("fsdp", None),
            P("fsdp"),
            P("fsdp", None),
            P("fsdp", None),
            P("fsdp", None),
        ),
        check_vma=False,
    )
```

```python
import functools
import jax
import jax.numpy as jnp
from jax import lax
from jax.experimental import pallas as pl
from jax.experimental.pallas import tpu as pltpu
from jax.experimental.layout import Layout, with_layout_constraint
from jax.sharding import PartitionSpec as P

QUERY_HEADS = 32
KEY_VALUE_HEADS = 8
HEAD_SIZE = 80
LANES = 128


eps = 1e-05
theta = 1000000.0
log2e = 1.4426950408889634


def swap(value, bit):
    size = lax.axis_size("sp")
    return lax.ppermute(value, "sp", [(i, i ^ bit) for i in range(size)])


def row_major(value):
    return with_layout_constraint(value, Layout(major_to_minor=tuple(range(value.ndim))))


def gather_sp(value, *hold):
    size = lax.axis_size("sp")
    if size != 4:
        whole = lax.all_gather(value, "sp", axis=0, tiled=False)
        return whole, (whole,)
    place = lax.axis_index("sp")
    half = value.shape[0] // 2
    first, second = value[:half], value[half:]
    x_first, y_second = swap(first, 1), swap(second, 2)
    x_second, y_first = swap(second, 1), swap(first, 2)
    far_first, far_second = (after(v, *hold) if hold else v for v in (x_first, y_second))
    far_first, far_second = swap(far_first, 2), swap(far_second, 1)
    out = jnp.zeros((size,) + value.shape, value.dtype)
    if hold:
        out = after(out, *hold)
    zeros = (0,) * (value.ndim - 1)
    for turn, low, high in (
        (0, first, second),
        (1, x_first, x_second),
        (2, y_first, y_second),
        (3, far_first, far_second),
    ):
        out = lax.dynamic_update_slice(out, low[None], (place ^ turn, 0) + zeros)
        out = lax.dynamic_update_slice(out, high[None], (place ^ turn, half) + zeros)
    return row_major(out), (x_first, y_second)


def rows_of(blocks, picks):
    return blocks.at[picks].get(mode="promise_in_bounds")


def gather_small(value):
    size = lax.axis_size("sp")
    if size != 4:
        return lax.all_gather(value, "sp", axis=0, tiled=False)
    place = lax.axis_index("sp")
    pieces = [value] + [swap(value, turn) for turn in range(1, size)]
    here = [
        sum(jnp.where(place ^ turn == i, pieces[turn], 0) for turn in range(size)) for i in range(size)
    ]
    return jnp.stack(here, axis=0)


def scatter_sp(parts, hook=None):
    size = lax.axis_size("sp")
    if size != 4:
        summed = lax.psum_scatter(parts, "sp", scatter_dimension=0, tiled=False)
        given = hook((summed,)) if hook else ()
        return summed.astype(jnp.float32), (summed,), (summed,), given
    place = lax.axis_index("sp")
    half = parts.shape[1] // 2
    parts = row_major(parts)

    def block(parts, turn, lower):
        start = (place ^ turn, 0 if lower else half) + (0,) * (parts.ndim - 2)
        return lax.dynamic_slice(parts, start, (1, half) + parts.shape[2:])[0]

    wide = jnp.float32
    low = parts.dtype

    def added(*values):
        values = lax.optimization_barrier(values)
        total = values[0].astype(wide)
        for value in values[1:]:
            total = total + value.astype(wide)
        return total

    far = block(parts, 3, True), block(parts, 3, False)
    from_x, from_y = swap(far[0], 1), swap(far[1], 2)
    parts = after(parts, *far)
    given = hook((from_x, from_y)) if hook else ()
    if given:
        from_x, from_y = after(from_x, *given), after(from_y, *given)
    x_first, y_second = swap(block(parts, 1, True), 1), swap(block(parts, 2, False), 2)
    y_sent = added(block(parts, 2, True), from_x).astype(low)
    x_sent = added(block(parts, 1, False), from_y).astype(low)
    y_first, x_second = swap(y_sent, 2), swap(x_sent, 1)
    first = added(block(parts, 0, True), x_first, y_first)
    second = added(block(parts, 0, False), y_second, x_second)
    stage = (y_sent, x_sent, x_first, y_second)
    return jnp.concatenate([first, second], axis=0), stage, (y_first, x_second), given


def rotary_tables(positions):
    halves = HEAD_SIZE // 2
    frequency = theta ** (-(2.0 * jnp.arange(halves, dtype=jnp.float32)) / HEAD_SIZE)
    angles = positions.astype(jnp.float32)[:, None] * frequency[None, :]
    cosine, sine = jnp.cos(angles), jnp.sin(angles)
    rest = jnp.zeros((positions.shape[0], LANES - HEAD_SIZE), jnp.float32)
    return (
        jnp.concatenate([cosine, cosine, rest], axis=1),
        jnp.concatenate([-sine, sine, rest], axis=1),
    )


def dot(left, right):
    return jnp.dot(left, right, preferred_element_type=jnp.float32)


def dot_rows(left, right):
    return lax.dot_general(left, right, (((0,), (0,)), ((), ())), preferred_element_type=jnp.float32)


def dot_cols(left, right):
    return lax.dot_general(left, right, (((1,), (1,)), ((), ())), preferred_element_type=jnp.float32)


def head_of(matrix, head):
    first = head * HEAD_SIZE
    if first + LANES <= matrix.shape[1]:
        return matrix[:, first : first + LANES]
    kept = matrix[:, first : first + HEAD_SIZE]
    return jnp.concatenate([kept, jnp.zeros((kept.shape[0], LANES - HEAD_SIZE), kept.dtype)], axis=1)


def half_turn(padded):
    lane = lax.broadcasted_iota(jnp.int32, padded.shape, 1)
    half = HEAD_SIZE // 2
    return jnp.where(lane < half, pltpu.roll(padded, LANES - half, 1), pltpu.roll(padded, half, 1))


def qkv_kernel(heads, keys, width, x_ref, gain_ref, weight_ref, cos_ref, sin_ref, normed_ref, q_ref, k_ref, v_ref):
    x = x_ref[...].astype(jnp.float32)
    scale = lax.rsqrt(jnp.mean(x * x, axis=1, keepdims=True) + eps)
    normed = (x * scale * gain_ref[...]).astype(jnp.bfloat16)
    normed_ref[...] = normed
    rows = jnp.dot(normed, weight_ref[:, :width], preferred_element_type=jnp.float32)
    cosine, sine = cos_ref[...], sin_ref[...]
    inside = lax.broadcasted_iota(jnp.int32, cosine.shape, 1) < HEAD_SIZE
    for i in range(heads + keys):
        v = head_of(rows, i)
        turned = (v * cosine + half_turn(v) * sine).astype(jnp.bfloat16)
        if i < heads:
            q_ref[:, i * LANES : (i + 1) * LANES] = turned
        else:
            k_ref[:, (i - heads) * LANES : (i - heads + 1) * LANES] = turned
    for i in range(keys):
        v = head_of(rows, heads + keys + i)
        v_ref[:, i * LANES : (i + 1) * LANES] = jnp.where(inside, v, 0.0).astype(jnp.bfloat16)


def qkv_call(x, gain, weight, cosine, sine, heads, keys, used):
    total, width = x.shape
    block = 256
    bf = jnp.bfloat16
    row = lambda n: pl.BlockSpec((block, n), lambda i: (i, 0))
    whole = lambda a: pl.BlockSpec(a.shape, lambda i: (0, 0))
    return pl.pallas_call(
        functools.partial(qkv_kernel, heads, keys, used),
        grid=(total // block,),
        in_specs=[row(width), whole(gain), whole(weight), row(LANES), row(LANES)],
        out_specs=[row(width), row(heads * LANES), row(keys * LANES), row(keys * LANES)],
        out_shape=[
            jax.ShapeDtypeStruct((total, width), bf),
            jax.ShapeDtypeStruct((total, heads * LANES), bf),
            jax.ShapeDtypeStruct((total, keys * LANES), bf),
            jax.ShapeDtypeStruct((total, keys * LANES), bf),
        ],
        compiler_params=pltpu.CompilerParams(vmem_limit_bytes=48 * 2**20),
        cost_estimate=pl.CostEstimate(
            flops=96 * 10**9, bytes_accessed=0, transcendentals=0
        ),
    )(x, gain, weight, cosine, sine)


def attend_kernel(heads, keys, block, q_ref, k_ref, v_ref, start_ref, *refs):
    mixed_ref, lse_ref, bias_ref = refs[-3:]
    total = q_ref.shape[0]
    group = heads // keys
    factor = HEAD_SIZE**-0.5 * log2e
    for i in range(total // block):
        first, stop = i * block, (i + 1) * block
        column = lax.broadcasted_iota(jnp.int32, (block, stop), 1)
        row = lax.broadcasted_iota(jnp.int32, (block, stop), 0) + first
        good = (column >= start_ref[first:stop, :]) & (column <= row)
        bias_ref[:, :stop] = jnp.where(good, 0.0, -1e30)
        for head in range(heads):
            lanes = slice(head * LANES, (head + 1) * LANES)
            key = slice(head // group * LANES, (head // group + 1) * LANES)
            scores = dot_cols(q_ref[first:stop, lanes], k_ref[:stop, key]) * factor + bias_ref[:, :stop]
            top = jnp.max(scores, axis=1, keepdims=True)
            weights = jnp.exp2(scores - top)
            summed = jnp.sum(weights, axis=1, keepdims=True)
            mixed = jnp.dot(
                weights.astype(jnp.bfloat16), v_ref[:stop, key], preferred_element_type=jnp.float32
            ) / summed
            mixed_ref[first:stop, head * HEAD_SIZE : (head + 1) * HEAD_SIZE] = mixed[:, :HEAD_SIZE].astype(
                jnp.bfloat16
            )
            lse_ref[first:stop, head : head + 1] = top + jnp.log2(summed)


def attend_call(q, k, v, start, *when):
    block = 256
    total = q.shape[0]
    heads, keys = q.shape[1] // LANES, k.shape[1] // LANES
    return pl.pallas_call(
        functools.partial(attend_kernel, heads, keys, block),
        in_specs=[pl.BlockSpec(memory_space=pltpu.VMEM)] * 4
        + [pl.BlockSpec(memory_space=pl.ANY)] * len(when),
        out_shape=[
            jax.ShapeDtypeStruct((total, heads * HEAD_SIZE), jnp.bfloat16),
            jax.ShapeDtypeStruct((total, heads), jnp.float32),
        ],
        scratch_shapes=[pltpu.VMEM((block, total), jnp.float32)],
        compiler_params=pltpu.CompilerParams(vmem_limit_bytes=56 * 2**20),
        cost_estimate=pl.CostEstimate(
            flops=112 * 10**9, bytes_accessed=0, transcendentals=0
        ),
    )(q, k, v, start, *when)


def attend_back_kernel(
    heads, keys, block, q_ref, k_ref, v_ref, grad_ref, lse_ref, start_ref, cos_ref, sin_ref, *refs
):
    out_ref, bias_ref, dk_ref, dv_ref = refs[-4:]
    total = q_ref.shape[0]
    group = heads // keys
    scale = HEAD_SIZE**-0.5
    factor = scale * log2e
    low = jnp.bfloat16
    dk_ref[...] = jnp.zeros_like(dk_ref)
    dv_ref[...] = jnp.zeros_like(dv_ref)
    inside = lax.broadcasted_iota(jnp.int32, (block, LANES), 1) < HEAD_SIZE
    half = HEAD_SIZE // 2

    def turned_back(w, rows):
        w = w.astype(low).astype(jnp.float32)
        scaled = w * sin_ref[rows, :]
        lane = lax.broadcasted_iota(jnp.int32, w.shape, 1)
        moved = jnp.where(lane < half, pltpu.roll(scaled, LANES - half, 1), pltpu.roll(scaled, half, 1))
        return (w * cos_ref[rows, :] + moved).astype(low)

    for i in range(total // block):
        first, stop = i * block, (i + 1) * block
        rows = slice(first, stop)
        key_place = lax.broadcasted_iota(jnp.int32, (stop, block), 0)
        place = lax.broadcasted_iota(jnp.int32, (stop, block), 1) + first
        good = (key_place >= start_ref[:, rows]) & (key_place <= place)
        bias_ref[:stop, :] = jnp.where(good, 0.0, -1e30)
        grads = grad_ref[rows, :].astype(jnp.float32)
        for head in range(heads):
            lanes = slice(head * LANES, (head + 1) * LANES)
            key = slice(head // group * LANES, (head // group + 1) * LANES)
            query = q_ref[rows, lanes]
            grad = jnp.where(inside, head_of(grads, head), 0.0).astype(low)
            scores = dot_cols(k_ref[:stop, key], query) * factor + bias_ref[:stop, :]
            probs = jnp.exp2(scores - lse_ref[head : head + 1, rows])
            dv_ref[:stop, key] += jnp.dot(probs.astype(low), grad, preferred_element_type=jnp.float32)
            d_probs = dot_cols(v_ref[:stop, key], grad)
            delta = jnp.sum(probs * d_probs, axis=0, keepdims=True)
            d_scores = (probs * (d_probs - delta)).astype(low)
            dk_ref[:stop, key] += jnp.dot(d_scores, query, preferred_element_type=jnp.float32)
            d_query = dot_rows(d_scores, k_ref[:stop, key]) * scale
            out_ref[rows, head * HEAD_SIZE : (head + 1) * HEAD_SIZE] = turned_back(d_query, rows)[:, :HEAD_SIZE]
    for i in range(total // block):
        rows = slice(i * block, (i + 1) * block)
        for j in range(keys):
            lanes = slice(j * LANES, (j + 1) * LANES)
            at = (heads + j) * HEAD_SIZE
            out_ref[rows, at : at + HEAD_SIZE] = turned_back(dk_ref[rows, lanes] * scale, rows)[:, :HEAD_SIZE]
            at = (heads + keys + j) * HEAD_SIZE
            out_ref[rows, at : at + HEAD_SIZE] = dv_ref[rows, lanes][:, :HEAD_SIZE].astype(low)


def attend_back_call(q, k, v, grad, lse_rows, start_row, cosine, sine_back, *when):
    block = 256
    total = q.shape[0]
    heads, keys = q.shape[1] // LANES, k.shape[1] // LANES
    return pl.pallas_call(
        functools.partial(attend_back_kernel, heads, keys, block),
        in_specs=[pl.BlockSpec(memory_space=pltpu.VMEM)] * 8
        + [pl.BlockSpec(memory_space=pl.ANY)] * len(when),
        out_shape=jax.ShapeDtypeStruct((total, (heads + 2 * keys) * HEAD_SIZE), jnp.bfloat16),
        scratch_shapes=[
            pltpu.VMEM((total, block), jnp.float32),
            pltpu.VMEM((total, keys * LANES), jnp.float32),
            pltpu.VMEM((total, keys * LANES), jnp.float32),
        ],
        compiler_params=pltpu.CompilerParams(vmem_limit_bytes=56 * 2**20),
        cost_estimate=pl.CostEstimate(
            flops=100 * 10**9, bytes_accessed=0, transcendentals=0
        ),
    )(q, k, v, grad, lse_rows, start_row, cosine, sine_back, *when)

def gate_up_kernel(x_ref, gate_weight_ref, up_weight_ref, active_ref, gate_ref, up_ref):
    x = x_ref[...]
    gate = jnp.dot(x, gate_weight_ref[...], preferred_element_type=jnp.float32)
    upward = jnp.dot(x, up_weight_ref[...], preferred_element_type=jnp.float32)
    active_ref[...] = (gate / (1.0 + jnp.exp(-gate)) * upward).astype(jnp.bfloat16)
    gate_ref[...] = gate.astype(jnp.bfloat16)
    up_ref[...] = upward.astype(jnp.bfloat16)


def unit_block(units):
    return 256 if units % 256 == 0 else 128


def gate_up_call(x, weights):
    total, width = x.shape
    units = weights.shape[1] // 2
    block = unit_block(units)
    count = units // block
    out = pl.BlockSpec((total, block), lambda j: (0, j))
    return pl.pallas_call(
        gate_up_kernel,
        grid=(count,),
        in_specs=[
            pl.BlockSpec((total, width), lambda j: (0, 0)),
            pl.BlockSpec((width, block), lambda j: (0, j)),
            pl.BlockSpec((width, block), lambda j: (0, j + count)),
        ],
        out_specs=[out] * 3,
        out_shape=[jax.ShapeDtypeStruct((total, units), jnp.bfloat16)] * 3,
        compiler_params=pltpu.CompilerParams(vmem_limit_bytes=56 * 2**20),
        cost_estimate=pl.CostEstimate(
            flops=148 * 10**9, bytes_accessed=0, transcendentals=0
        ),
    )(x, weights, weights)


def unit_back_kernel(incoming_ref, down_ref, gate_ref, up_ref, *refs):
    d_gate_ref, d_up_ref = refs[-2:]
    d_active = dot_cols(incoming_ref[...], down_ref[...])
    gate = gate_ref[...].astype(jnp.float32)
    upward = up_ref[...].astype(jnp.float32)
    logistic = 1.0 / (1.0 + jnp.exp(-gate))
    d_gate_ref[...] = (d_active * upward * logistic * (1.0 + gate * (1.0 - logistic))).astype(jnp.bfloat16)
    d_up_ref[...] = (d_active * gate * logistic).astype(jnp.bfloat16)


def unit_back_call(incoming, down, gate, up, *when):
    total, width = incoming.shape
    units = down.shape[0]
    block = unit_block(units)
    column = pl.BlockSpec((total, block), lambda j: (0, j))
    return pl.pallas_call(
        unit_back_kernel,
        grid=(units // block,),
        in_specs=[
            pl.BlockSpec((total, width), lambda j: (0, 0)),
            pl.BlockSpec((block, width), lambda j: (j, 0)),
            column,
            column,
        ]
        + [pl.BlockSpec(memory_space=pl.ANY)] * len(when),
        out_specs=[column] * 2,
        out_shape=[jax.ShapeDtypeStruct((total, units), jnp.bfloat16)] * 2,
        compiler_params=pltpu.CompilerParams(vmem_limit_bytes=56 * 2**20),
        cost_estimate=pl.CostEstimate(
            flops=104 * 10**9, bytes_accessed=0, transcendentals=0
        ),
    )(incoming, down, gate, up, *when)


def norm_back(d_normed, x, gain):
    scale = lax.rsqrt(jnp.mean(x * x, axis=1, keepdims=True) + eps)
    grad_gain = jnp.sum(d_normed * (x * scale), axis=0, keepdims=True)
    scaled = d_normed * gain
    inner = jnp.mean(scaled * x, axis=1, keepdims=True)
    return scale * scaled - x * (scale * scale * scale * inner), grad_gain


def add_up(ref, value):
    @pl.when(pl.program_id(0) == 0)
    def _():
        ref[...] = jnp.zeros_like(ref)

    ref[...] += value


def mlp_back_kernel(d_gate_ref, d_up_ref, weight_ref, x_ref, gain_ref, *refs):
    out_ref, grad_ref = refs[-2:]
    units = d_gate_ref.shape[1]
    d_normed = dot_cols(d_gate_ref[...], weight_ref[:, :units]) + dot_cols(
        d_up_ref[...], weight_ref[:, units:]
    )
    back, grad_gain = norm_back(d_normed, x_ref[...].astype(jnp.float32), gain_ref[...])
    parts, _, share = out_ref.shape
    for i in range(parts):
        out_ref[i] = back[:, i * share : (i + 1) * share].astype(jnp.bfloat16)
    add_up(grad_ref, grad_gain)


def mlp_back_call(d_gate, d_up, weights, x, gain, parts, *when):
    total, units = d_gate.shape
    width = x.shape[1]
    share = width // parts
    block = 512
    row = lambda n: pl.BlockSpec((block, n), lambda i: (i, 0))
    whole = lambda a: pl.BlockSpec(a.shape, lambda i: (0, 0), pipeline_mode=pl.Buffered(1))
    return pl.pallas_call(
        mlp_back_kernel,
        grid=(total // block,),
        in_specs=[row(units), row(units), whole(weights), row(width), whole(gain)]
        + [pl.BlockSpec(memory_space=pl.ANY)] * len(when),
        out_specs=[
            pl.BlockSpec((parts, block, share), lambda i: (0, i, 0)),
            pl.BlockSpec((1, width), lambda i: (0, 0)),
        ],
        out_shape=[
            jax.ShapeDtypeStruct((parts, total, share), jnp.bfloat16),
            jax.ShapeDtypeStruct((1, width), jnp.float32),
        ],
        compiler_params=pltpu.CompilerParams(vmem_limit_bytes=60 * 2**20),
        cost_estimate=pl.CostEstimate(
            flops=176 * 10**9, bytes_accessed=0, transcendentals=0
        ),
    )(d_gate, d_up, weights, x, gain, *when)


def attend_norm_kernel(parts, place_ref, d_qkv_ref, weight_ref, x_ref, gain_ref, own_ref, *refs):
    out_ref, grad_ref = refs[-2:]
    d_normed = dot_cols(d_qkv_ref[...], weight_ref[:, : d_qkv_ref.shape[1]])
    back, grad_gain = norm_back(d_normed, x_ref[...].astype(jnp.float32), gain_ref[...])
    out_ref[...] = back.astype(jnp.bfloat16)
    share = own_ref.shape[1]
    for place in range(parts):

        @pl.when(place_ref[0] == place)
        def _():
            lanes = slice(place * share, (place + 1) * share)
            out_ref[:, lanes] = (back[:, lanes] + own_ref[...]).astype(jnp.bfloat16)

    add_up(grad_ref, grad_gain)


def attend_norm_call(place, d_qkv, weights, x, gain, own, parts, *when):
    total, width = x.shape
    block = 256
    row = lambda n: pl.BlockSpec((block, n), lambda i: (i, 0))
    whole = lambda a: pl.BlockSpec(a.shape, lambda i: (0, 0), pipeline_mode=pl.Buffered(1))
    return pl.pallas_call(
        functools.partial(attend_norm_kernel, parts),
        grid=(total // block,),
        in_specs=[
            pl.BlockSpec(memory_space=pltpu.SMEM),
            row(d_qkv.shape[1]),
            whole(weights),
            row(width),
            whole(gain),
            row(own.shape[1]),
        ]
        + [pl.BlockSpec(memory_space=pl.ANY)] * len(when),
        out_specs=[row(width), pl.BlockSpec((1, width), lambda i: (0, 0))],
        out_shape=[
            jax.ShapeDtypeStruct((total, width), jnp.bfloat16),
            jax.ShapeDtypeStruct((1, width), jnp.float32),
        ],
        compiler_params=pltpu.CompilerParams(vmem_limit_bytes=56 * 2**20),
        cost_estimate=pl.CostEstimate(
            flops=80 * 10**9, bytes_accessed=0, transcendentals=0
        ),
    )(place, d_qkv, weights, x, gain, own, *when)


def out_back_kernel(d_ref, weight_ref, *refs):
    refs[-1][0] = dot_cols(d_ref[...], weight_ref[...]).astype(jnp.bfloat16)


def out_back_call(d_branch, weights, parts, *when):
    total, share = d_branch.shape
    rows = weights.shape[0] // parts
    return pl.pallas_call(
        out_back_kernel,
        grid=(parts,),
        in_specs=[
            pl.BlockSpec((total, share), lambda i: (0, 0)),
            pl.BlockSpec((rows, share), lambda i: (i, 0)),
        ]
        + [pl.BlockSpec(memory_space=pl.ANY)] * len(when),
        out_specs=pl.BlockSpec((1, total, rows), lambda i: (i, 0, 0)),
        out_shape=jax.ShapeDtypeStruct((parts, total, rows), jnp.bfloat16),
        compiler_params=pltpu.CompilerParams(vmem_limit_bytes=32 * 2**20),
        cost_estimate=pl.CostEstimate(
            flops=32 * 10**9, bytes_accessed=0, transcendentals=0
        ),
    )(d_branch, weights, *when)


def norm_kernel(stack_ref, gain_ref, x_ref, normed_ref):
    parts, _, share = stack_ref.shape
    squares = 0.0
    for i in range(parts):
        piece = stack_ref[i].astype(jnp.float32)
        squares = squares + jnp.sum(piece * piece, axis=1, keepdims=True)
    scale = lax.rsqrt(squares / (parts * share) + eps)
    for i in range(parts):
        lanes = slice(i * share, (i + 1) * share)
        x_ref[:, lanes] = stack_ref[i]
        normed = stack_ref[i].astype(jnp.float32) * scale * gain_ref[:, lanes]
        normed_ref[:, lanes] = normed.astype(jnp.bfloat16)


def norm_call(stack, gain):
    parts, total, share = stack.shape
    block = 256
    row = pl.BlockSpec((block, parts * share), lambda i: (i, 0))
    return pl.pallas_call(
        norm_kernel,
        grid=(total // block,),
        in_specs=[
            pl.BlockSpec((parts, block, share), lambda i: (0, i, 0)),
            pl.BlockSpec((1, parts * share), lambda i: (0, 0)),
        ],
        out_specs=[row, row],
        out_shape=[jax.ShapeDtypeStruct((total, parts * share), jnp.bfloat16)] * 2,
        compiler_params=pltpu.CompilerParams(vmem_limit_bytes=32 * 2**20),
        cost_estimate=pl.CostEstimate(flops=32 * 10**9, bytes_accessed=0, transcendentals=0),
    )(stack, gain)


def out_kernel(stack_ref, weight_ref, x_ref, out_ref):
    parts, _, depth = stack_ref.shape
    total = x_ref[...].astype(jnp.float32)
    for i in range(parts):
        total = total + jnp.dot(
            stack_ref[i], weight_ref[i * depth : (i + 1) * depth, :], preferred_element_type=jnp.float32
        )
    out_ref[...] = total.astype(jnp.bfloat16)


def out_call(stack, weight, x):
    parts, total, depth = stack.shape
    columns = weight.shape[1]
    block = 512
    row = pl.BlockSpec((block, columns), lambda i: (i, 0))
    return pl.pallas_call(
        out_kernel,
        grid=(total // block,),
        in_specs=[
            pl.BlockSpec((parts, block, depth), lambda i: (0, i, 0)),
            pl.BlockSpec(weight.shape, lambda i: (0, 0)),
            row,
        ],
        out_specs=row,
        out_shape=jax.ShapeDtypeStruct((total, columns), jnp.bfloat16),
        compiler_params=pltpu.CompilerParams(vmem_limit_bytes=40 * 2**20),
        cost_estimate=pl.CostEstimate(flops=36 * 10**9, bytes_accessed=0, transcendentals=0),
    )(stack, weight, x)


def stack_rows_kernel(left_ref, right_ref, *refs):
    refs[-1][...] = dot_rows(left_ref[0], right_ref[...]).astype(jnp.bfloat16)


def stack_rows_call(stack, right, *when):
    parts, total, rows = stack.shape
    columns = right.shape[1]
    return pl.pallas_call(
        stack_rows_kernel,
        grid=(parts,),
        in_specs=[
            pl.BlockSpec((1, total, rows), lambda i: (i, 0, 0)),
            pl.BlockSpec((total, columns), lambda i: (0, 0)),
        ]
        + [pl.BlockSpec(memory_space=pl.ANY)] * len(when),
        out_specs=pl.BlockSpec((rows, columns), lambda i: (i, 0)),
        out_shape=jax.ShapeDtypeStruct((parts * rows, columns), jnp.bfloat16),
        compiler_params=pltpu.CompilerParams(vmem_limit_bytes=40 * 2**20),
        cost_estimate=pl.CostEstimate(flops=0 * 10**9, bytes_accessed=0, transcendentals=0),
    )(stack, right, *when)


def rows_kernel(left_ref, right_ref, *refs):
    refs[-1][...] = dot_rows(left_ref[...], right_ref[...]).astype(jnp.bfloat16)


def rows_call(left, right, *when):
    total, rows = left.shape
    columns = right.shape[1]
    block = 256 if columns % 256 == 0 else 128
    return pl.pallas_call(
        rows_kernel,
        grid=(columns // block,),
        in_specs=[
            pl.BlockSpec((total, rows), lambda j: (0, 0)),
            pl.BlockSpec((total, block), lambda j: (0, j)),
        ]
        + [pl.BlockSpec(memory_space=pl.ANY)] * len(when),
        out_specs=pl.BlockSpec((rows, block), lambda j: (0, j)),
        out_shape=jax.ShapeDtypeStruct((rows, columns), jnp.bfloat16),
        compiler_params=pltpu.CompilerParams(vmem_limit_bytes=56 * 2**20),
        cost_estimate=pl.CostEstimate(flops=0 if when else 80 * 10**9, bytes_accessed=0, transcendentals=0),
    )(left, right, *when)


def product_kernel(left_ref, right_ref, *refs):
    refs[-1][...] = jnp.dot(left_ref[...], right_ref[...], preferred_element_type=jnp.float32).astype(
        jnp.bfloat16
    )


def product_call(left, right, *when):
    total, depth = left.shape
    columns = right.shape[1]
    block = 256 if columns % 256 == 0 else 128
    return pl.pallas_call(
        product_kernel,
        grid=(columns // block,),
        in_specs=[
            pl.BlockSpec((total, depth), lambda j: (0, 0)),
            pl.BlockSpec((depth, block), lambda j: (0, j)),
        ]
        + [pl.BlockSpec(memory_space=pl.ANY)] * len(when),
        out_specs=pl.BlockSpec((total, block), lambda j: (0, j)),
        out_shape=jax.ShapeDtypeStruct((total, columns), jnp.bfloat16),
        compiler_params=pltpu.CompilerParams(vmem_limit_bytes=56 * 2**20),
        cost_estimate=pl.CostEstimate(flops=80 * 10**9, bytes_accessed=0, transcendentals=0),
    )(left, right, *when)


def qkv_grad_kernel(normed_ref, d_qkv_ref, gain_ref, *refs):
    out_ref = refs[-1]
    columns = d_qkv_ref.shape[1]
    out_ref[:, :columns] = dot_rows(normed_ref[...], d_qkv_ref[...]).astype(jnp.bfloat16)
    rest = jnp.transpose(gain_ref[...])
    fill = out_ref.shape[1] - columns - rest.shape[1]
    if fill:
        rest = jnp.concatenate([rest, jnp.zeros((rest.shape[0], fill), rest.dtype)], axis=1)
    out_ref[:, columns:] = rest.astype(jnp.bfloat16)


def qkv_grad_call(normed, d_qkv, gain_grads, columns, *when):
    total, width = normed.shape
    block = 512
    return pl.pallas_call(
        qkv_grad_kernel,
        grid=(width // block,),
        in_specs=[
            pl.BlockSpec((total, block), lambda i: (0, i)),
            pl.BlockSpec(d_qkv.shape, lambda i: (0, 0)),
            pl.BlockSpec((gain_grads.shape[0], block), lambda i: (0, i)),
        ]
        + [pl.BlockSpec(memory_space=pl.ANY)] * len(when),
        out_specs=pl.BlockSpec((block, columns), lambda i: (i, 0)),
        out_shape=jax.ShapeDtypeStruct((width, columns), jnp.bfloat16),
        compiler_params=pltpu.CompilerParams(vmem_limit_bytes=48 * 2**20),
        cost_estimate=pl.CostEstimate(flops=48 * 10**9, bytes_accessed=0, transcendentals=0),
    )(normed, d_qkv, gain_grads, *when)


def pieces_sp(value, split, *hold):
    size = lax.axis_size("sp")
    columns = value.shape[1]
    if not split or size != 4 or columns % (2 * LANES):
        others = [(swap(value, turn),) for turn in range(1, size)]
        return [(value,)] + others, [piece for (piece,) in others], []
    half = columns // 2
    left, right = value[:, :half], value[:, half:]
    x_left, y_right = swap(left, 1), swap(right, 2)
    x_right, y_left = swap(right, 1), swap(left, 2)
    far_left, far_right = (after(v, *hold) if hold else v for v in (x_left, y_right))
    far_left, far_right = swap(far_left, 2), swap(far_right, 1)
    return (
        [(left, right), (x_left, x_right), (y_left, y_right), (far_left, far_right)],
        [x_left, y_right, x_right, y_left],
        [far_left, far_right],
    )


def spread_kernel(layout, count, chunks, outputs, place_ref, *refs):
    pieces, outs = refs[: count * chunks], refs[-outputs:]
    size = pieces[0].shape[1]
    for place in range(count):

        @pl.when(place_ref[0] == place)
        def _():
            for part in range(count):
                for first, width, out, at, step in layout:
                    goal = at + part * step
                    while width:
                        chunk, begin = divmod(first, size)
                        some = min(width, size - begin)
                        piece = pieces[(place ^ part) * chunks + chunk]
                        outs[out][:, goal : goal + some] = piece[:, begin : begin + some].astype(jnp.float32)
                        first, goal, width = first + some, goal + some, width - some


def spread_call(place, pieces, layout, widths, *when):
    count, chunks = len(pieces), len(pieces[0])
    rows, columns = pieces[0][0].shape
    block = rows // 5 if rows % 80 == 0 else rows
    return pl.pallas_call(
        functools.partial(spread_kernel, layout, count, chunks, len(widths)),
        grid=(rows // block,),
        in_specs=[pl.BlockSpec(memory_space=pltpu.SMEM)]
        + [pl.BlockSpec((block, columns), lambda i: (i, 0))] * (count * chunks)
        + [pl.BlockSpec(memory_space=pl.ANY)] * len(when),
        out_specs=[pl.BlockSpec((block, w), lambda i: (i, 0)) for w in widths],
        out_shape=[jax.ShapeDtypeStruct((rows, w), jnp.float32) for w in widths],
        compiler_params=pltpu.CompilerParams(vmem_limit_bytes=40 * 2**20),
        cost_estimate=pl.CostEstimate(
            flops=0, bytes_accessed=6 * count * chunks * rows * columns, transcendentals=0
        ),
    )(place, *[chunk for piece in pieces for chunk in piece], *when)


def stack_kernel(count, chunks, place_ref, *refs):
    out_ref = refs[-1]
    size = refs[0].shape[1]
    for turn in range(count):
        for chunk in range(chunks):
            value = refs[turn * chunks + chunk][...].astype(jnp.float32)
            out_ref[place_ref[0] ^ turn, :, chunk * size : (chunk + 1) * size] = value


def stack_call(place, pieces, *when):
    count, chunks = len(pieces), len(pieces[0])
    rows, columns = pieces[0][0].shape
    block = 32 if rows % 32 == 0 else rows
    return pl.pallas_call(
        functools.partial(stack_kernel, count, chunks),
        grid=(rows // block,),
        in_specs=[pl.BlockSpec(memory_space=pltpu.SMEM)]
        + [pl.BlockSpec((block, columns), lambda i: (i, 0))] * (count * chunks)
        + [pl.BlockSpec(memory_space=pl.ANY)] * len(when),
        out_specs=pl.BlockSpec((count, block, chunks * columns), lambda i: (0, i, 0)),
        out_shape=jax.ShapeDtypeStruct((count, rows, chunks * columns), jnp.float32),
        compiler_params=pltpu.CompilerParams(vmem_limit_bytes=40 * 2**20),
        cost_estimate=pl.CostEstimate(
            flops=0, bytes_accessed=6 * count * chunks * rows * columns, transcendentals=0
        ),
    )(place, *[chunk for piece in pieces for chunk in piece], *when).reshape(count * rows, chunks * columns)


def pass_kernel(*refs):
    pass


def after(value, *others):
    here = pl.BlockSpec(memory_space=pl.ANY)
    return pl.pallas_call(
        pass_kernel,
        in_specs=[here] * (1 + len(others)),
        out_specs=here,
        out_shape=jax.ShapeDtypeStruct(value.shape, value.dtype),
        input_output_aliases={0: 0},
        cost_estimate=pl.CostEstimate(flops=0, bytes_accessed=0, transcendentals=0),
    )(value, *others)


def pack_kernel(groups, parts, place_ref, gate_ref, up_ref, _, out_ref):
    rows, columns = gate_ref.shape
    share = columns // (groups * parts)
    for place in range(parts):

        @pl.when(place_ref[0] == place)
        def _():
            for i, ref in enumerate((gate_ref, up_ref)):
                for j in range(groups):
                    at = (i * groups + j) * share
                    begin = (j * parts + place) * share
                    out_ref[:, at : at + share] = ref[:, begin : begin + share]


def pack_call(place, gate, up, when, groups, parts):
    rows, columns = gate.shape
    block = rows // 5 if rows % 80 == 0 else rows
    spec = pl.BlockSpec((block, columns), lambda i: (i, 0))
    return pl.pallas_call(
        functools.partial(pack_kernel, groups, parts),
        grid=(rows // block,),
        in_specs=[
            pl.BlockSpec(memory_space=pltpu.SMEM),
            spec,
            spec,
            pl.BlockSpec(memory_space=pl.ANY),
        ],
        out_specs=pl.BlockSpec((block, 2 * columns // parts), lambda i: (i, 0)),
        out_shape=jax.ShapeDtypeStruct((rows, 2 * columns // parts), gate.dtype),
        compiler_params=pltpu.CompilerParams(vmem_limit_bytes=32 * 2**20),
        cost_estimate=pl.CostEstimate(flops=0, bytes_accessed=5 * rows * columns, transcendentals=0),
    )(place, gate, up, when)


def local(
    tokens,
    cotangent,
    attn_gain,
    w_query,
    key_weight,
    value_weight,
    w_out,
    mlp_gain,
    w_gate,
    w_up,
    w_down,
    positions,
    lengths,
    deal_slots,
):
    groups = lax.axis_size("fsdp")
    parts = lax.axis_size("sp")
    width = tokens.shape[-1]
    rows = tokens.shape[1]
    fsdp_place = lax.axis_index("fsdp")
    sp_place = lax.axis_index("sp")
    low = jnp.bfloat16
    wide = jnp.float32

    lanes = jnp.arange(groups, dtype=jnp.int32)
    own_row = deal_slots[fsdp_place, sp_place]
    target = own_row // groups
    pick_send = jnp.sum(jnp.where(target[None, :] == lanes[:, None], lanes[None, :], 0), axis=1)
    column = deal_slots[:, sp_place, :]
    arrived_slot = jnp.sum(jnp.where(column // groups == fsdp_place, column % groups, 0), axis=1)
    pick_place = jnp.sum(
        jnp.where(arrived_slot[None, :] == lanes[:, None], lanes[None, :], 0), axis=1
    )

    def picked(given):
        return rows_of(given.reshape(groups, -1, width), pick_send)

    def deal(blocks):
        return lax.all_to_all(blocks, "fsdp", split_axis=0, concat_axis=0, tiled=True)

    def in_place(came):
        return rows_of(came, pick_place).reshape(rows, width)

    def blocks_back(owned):
        return rows_of(owned.reshape(groups, -1, width), arrived_slot)

    def scatter_fsdp(matrix):
        return lax.psum_scatter(matrix, "fsdp", scatter_dimension=0, tiled=True)

    def column_share(weight):
        share = weight.shape[1] // parts
        return lax.dynamic_slice_in_dim(weight, sp_place * share, share, axis=1)

    def gather_fsdp(shard):
        return lax.all_gather(shard, "fsdp", axis=0, tiled=True)

    ff_rows = w_down.shape[0]
    ff_share = ff_rows // parts

    query_cols = w_query.shape[1] // parts
    key_cols = key_weight.shape[1] // parts
    qkv_cols = query_cols + 2 * key_cols
    extra = -qkv_cols % 128
    extra = extra if extra else 128
    gains = jnp.pad(jnp.stack([attn_gain, mlp_gain], axis=1), ((0, 0), (0, extra - 2)))
    place = sp_place.reshape(1)
    came_tokens = deal(picked(tokens))
    gate_up_shard = pack_call(place, w_gate, w_up, came_tokens, groups, parts)
    qkv_shard = jnp.concatenate(
        [column_share(w_query), column_share(key_weight), column_share(value_weight), gains], axis=1
    )
    came_incoming = deal(after(picked(cotangent), came_tokens))
    qkv_width = qkv_shard.shape[1]
    qkv_shard = jnp.concatenate([qkv_shard, column_share(w_out)], axis=1)
    qkv_all = gather_fsdp(after(qkv_shard, came_tokens))
    out_all = qkv_all[:, qkv_width:]
    gate_up_all = gather_fsdp(gate_up_shard)
    down_all = gather_fsdp(lax.dynamic_slice_in_dim(w_down, sp_place * ff_share, ff_share, axis=0))
    gain_one = qkv_all[:, qkv_cols].astype(wide)[None, :]
    gain_two = qkv_all[:, qkv_cols + 1].astype(wide)[None, :]

    group_inputs, passed = gather_sp(in_place(came_tokens))
    group_inputs = group_inputs.reshape(-1, width)
    group_positions = gather_small(after(positions.reshape(-1), passed[0])).reshape(-1)
    total = group_inputs.shape[0]

    cosine, sine = rotary_tables(group_positions)
    heads, keys = query_cols // HEAD_SIZE, key_cols // HEAD_SIZE
    normed, query_low, key_low, value_low = qkv_call(
        group_inputs, gain_one, qkv_all, cosine, sine, heads, keys, qkv_width
    )
    sizes = lengths.reshape(-1)
    ends = jnp.cumsum(sizes)
    places = jnp.arange(total, dtype=jnp.int32)
    start = jnp.sum(jnp.where(places[:, None] >= ends[None, :], sizes[None, :], 0), axis=1)
    own_mixed, logs = attend_call(query_low, key_low, value_low, start[:, None])

    share = width // parts

    def own_columns(matrix):
        return lax.dynamic_slice_in_dim(matrix, sp_place * share, share, axis=1)

    mixed, _ = gather_sp(own_mixed)
    own_hidden = out_call(mixed, out_all, own_columns(group_inputs))
    hidden_low, normed_two = norm_call(gather_sp(own_hidden)[0], gain_two)

    active_low, gate, upward = gate_up_call(normed_two, gate_up_all)
    own_incoming = after(in_place(after(came_incoming, own_hidden)), normed_two)
    group_incoming = gather_sp(own_incoming, active_low)[0].reshape(-1, width)
    grad_down = rows_call(active_low, group_incoming)
    result_part = product_call(active_low, down_all, grad_down)
    d_gate, d_up = unit_back_call(group_incoming, down_all, gate, upward, result_part)
    grad_gate = rows_call(normed_two, d_gate)
    result_sum, sums_result, last_result, _ = scatter_sp(
        result_part.reshape(parts, rows, width), lambda first: (grad_gate,)
    )
    own_hidden_rows = lax.dynamic_slice_in_dim(hidden_low, sp_place * rows, rows, axis=0)
    blocks_result = blocks_back((own_hidden_rows.astype(wide) + result_sum).astype(low))

    back_two, grad_gain_two = mlp_back_call(
        d_gate, d_up, gate_up_all, hidden_low, gain_two, parts, grad_gate, *sums_result
    )
    from_others, _, _, (grad_up,) = scatter_sp(
        after(back_two, *last_result), lambda first: (rows_call(normed_two, d_up, *first),)
    )
    gone_result = deal(blocks_result)
    own_d_hidden = own_columns(group_incoming).astype(wide) + from_others
    d_branch = own_d_hidden.astype(low)
    d_mixed, _, _, (grad_out,) = scatter_sp(
        out_back_call(d_branch, out_all, parts), lambda first: (stack_rows_call(mixed, d_branch, *first),)
    )
    d_mixed = d_mixed.astype(low)

    down_sum = after(scatter_fsdp(grad_down), d_mixed)
    down_pieces, down_first, _ = pieces_sp(down_sum, False)
    gate_sum = after(scatter_fsdp(grad_gate), d_mixed, down_sum)
    gate_pieces, gate_first, _ = pieces_sp(gate_sum, False)
    d_qkv = attend_back_call(
        query_low, key_low, value_low, d_mixed, logs.T, start[None, :], cosine, sine
    )
    back_one, grad_gain_one = attend_norm_call(
        place, d_qkv, qkv_all, group_inputs, gain_one, own_d_hidden, parts, *down_first, *gate_first[:2]
    )
    gain_grads = jnp.concatenate(
        [grad_gain_one, grad_gain_two, jnp.zeros((6, width), wide)], axis=0
    )
    layer_out = rows_of(gone_result, target).reshape(tokens.shape)

    grad_qkv = qkv_grad_call(normed, d_qkv, gain_grads, qkv_width, *gate_first[2:])
    hidden_layout = [
        (j * ff_share, ff_share, 0, j * parts * ff_share, ff_share) for j in range(groups)
    ]

    def beside(first):
        gate_shard = spread_call(place, gate_pieces, hidden_layout, [w_gate.shape[1]], *first)[0]
        return stack_call(place, down_pieces, *first), gate_shard, layer_out

    d_inputs, _, _, (down_shard, gate_shard, layer_out) = scatter_sp(
        back_one.reshape(parts, rows, width), beside
    )
    gone_grad = deal(blocks_back(d_inputs.astype(low)))
    input_grad = rows_of(gone_grad, target).reshape(tokens.shape)

    up_pieces, up_first, _ = pieces_sp(scatter_fsdp(after(grad_up, d_branch)), True)
    out_sum = after(scatter_fsdp(after(grad_out, d_mixed)), *up_first[:2])
    out_pieces = pieces_sp(out_sum, False)[0]
    qkv_pieces = pieces_sp(after(scatter_fsdp(grad_qkv), out_sum), True)[0]
    (up_shard,) = spread_call(place, up_pieces, hidden_layout, [w_up.shape[1]])
    (out_shard,) = spread_call(place, out_pieces, [(0, share, 0, 0, share)], [width])
    qkv_layout = [
        (0, query_cols, 0, 0, query_cols),
        (query_cols, key_cols, 1, 0, key_cols),
        (query_cols + key_cols, key_cols, 2, 0, key_cols),
        (qkv_cols, 2, 3, 0, 2),
    ]
    query_shard, key_shard, value_shard, gain_parts = spread_call(
        place,
        qkv_pieces,
        qkv_layout,
        [w_query.shape[1], key_weight.shape[1], value_weight.shape[1], 2 * parts],
    )
    gain_shards = jnp.sum(gain_parts.reshape(-1, parts, 2), axis=1)
    return (
        layer_out,
        input_grad,
        gain_shards[:, 0],
        query_shard,
        key_shard,
        value_shard,
        out_shard,
        gain_shards[:, 1],
        gate_shard,
        up_shard,
        down_shard,
    )


def solution(mesh):
    placed = (
        P("fsdp", "sp", None),
        P("fsdp", "sp", None),
        P("fsdp"),
        P("fsdp", None),
        P("fsdp", None),
        P("fsdp", None),
        P("fsdp", None),
        P("fsdp"),
        P("fsdp", None),
        P("fsdp", None),
        P("fsdp", None),
        P("fsdp", "sp"),
        P("fsdp", None),
        P(),
    )
    return jax.shard_map(
        local,
        mesh=mesh,
        in_specs=placed,
        out_specs=(
            P("fsdp", "sp", None),
            P("fsdp", "sp", None),
            P("fsdp"),
            P("fsdp", None),
            P("fsdp", None),
            P("fsdp", None),
            P("fsdp", None),
            P("fsdp"),
            P("fsdp", None),
            P("fsdp", None),
            P("fsdp", None),
        ),
        check_vma=False,
    )
```

```python
import functools
import jax
import jax.numpy as jnp
from jax import lax
from jax.experimental import pallas as pl
from jax.experimental.pallas import tpu as pltpu
from jax.experimental.layout import Layout, with_layout_constraint
from jax.sharding import PartitionSpec as P

QUERY_HEADS = 32
KEY_VALUE_HEADS = 8
HEAD_SIZE = 80
LANES = 128


eps = 1e-05
theta = 1000000.0
log2e = 1.4426950408889634


def swap(value, bit):
    size = lax.axis_size("sp")
    return lax.ppermute(value, "sp", [(i, i ^ bit) for i in range(size)])


def row_major(value):
    return with_layout_constraint(value, Layout(major_to_minor=tuple(range(value.ndim))))


def gather_sp(value, *hold):
    size = lax.axis_size("sp")
    if size != 4:
        whole = lax.all_gather(value, "sp", axis=0, tiled=False)
        return whole, (whole,)
    place = lax.axis_index("sp")
    half = value.shape[0] // 2
    first, second = value[:half], value[half:]
    x_first, y_second = swap(first, 1), swap(second, 2)
    x_second, y_first = swap(second, 1), swap(first, 2)
    far_first, far_second = (after(v, *hold) if hold else v for v in (x_first, y_second))
    far_first, far_second = swap(far_first, 2), swap(far_second, 1)
    out = jnp.zeros((size,) + value.shape, value.dtype)
    if hold:
        out = after(out, *hold)
    zeros = (0,) * (value.ndim - 1)
    for turn, low, high in (
        (0, first, second),
        (1, x_first, x_second),
        (2, y_first, y_second),
        (3, far_first, far_second),
    ):
        out = lax.dynamic_update_slice(out, low[None], (place ^ turn, 0) + zeros)
        out = lax.dynamic_update_slice(out, high[None], (place ^ turn, half) + zeros)
    return row_major(out), (x_first, y_second)


def rows_of(blocks, picks):
    return blocks.at[picks].get(mode="promise_in_bounds")


def gather_small(value):
    size = lax.axis_size("sp")
    if size != 4:
        return lax.all_gather(value, "sp", axis=0, tiled=False)
    place = lax.axis_index("sp")
    pieces = [value] + [swap(value, turn) for turn in range(1, size)]
    here = [
        sum(jnp.where(place ^ turn == i, pieces[turn], 0) for turn in range(size)) for i in range(size)
    ]
    return jnp.stack(here, axis=0)


def scatter_sp(parts, hook=None, apart=True):
    size = lax.axis_size("sp")
    if size != 4:
        summed = lax.psum_scatter(parts, "sp", scatter_dimension=0, tiled=False)
        given = hook((summed,)) if hook else ()
        return summed.astype(jnp.float32), (summed,), (summed,), given
    place = lax.axis_index("sp")
    half = parts.shape[1] // 2
    parts = row_major(parts)

    def block(parts, turn, lower):
        start = (place ^ turn, 0 if lower else half) + (0,) * (parts.ndim - 2)
        return lax.dynamic_slice(parts, start, (1, half) + parts.shape[2:])[0]

    wide = jnp.float32
    low = parts.dtype

    def added(*values):
        values = lax.optimization_barrier(values)
        total = values[0].astype(wide)
        for value in values[1:]:
            total = total + value.astype(wide)
        return total

    far = block(parts, 3, True), block(parts, 3, False)
    from_x, from_y = swap(far[0], 1), swap(far[1], 2)
    parts = after(parts, *far) if apart else parts
    given = hook((from_x, from_y)) if hook else ()
    if given:
        from_x, from_y = after(from_x, *given), after(from_y, *given)
    x_first, y_second = swap(block(parts, 1, True), 1), swap(block(parts, 2, False), 2)
    y_sent = added(block(parts, 2, True), from_x).astype(low)
    x_sent = added(block(parts, 1, False), from_y).astype(low)
    y_first, x_second = swap(y_sent, 2), swap(x_sent, 1)
    first = added(block(parts, 0, True), x_first, y_first)
    second = added(block(parts, 0, False), y_second, x_second)
    stage = (y_sent, x_sent, x_first, y_second)
    return jnp.concatenate([first, second], axis=0), stage, (y_first, x_second), given


def rotary_tables(positions):
    halves = HEAD_SIZE // 2
    frequency = theta ** (-(2.0 * jnp.arange(halves, dtype=jnp.float32)) / HEAD_SIZE)
    angles = positions.astype(jnp.float32)[:, None] * frequency[None, :]
    cosine, sine = jnp.cos(angles), jnp.sin(angles)
    rest = jnp.zeros((positions.shape[0], LANES - HEAD_SIZE), jnp.float32)
    return (
        jnp.concatenate([cosine, cosine, rest], axis=1),
        jnp.concatenate([-sine, sine, rest], axis=1),
    )


def dot(left, right):
    return jnp.dot(left, right, preferred_element_type=jnp.float32)


def dot_rows(left, right):
    return lax.dot_general(left, right, (((0,), (0,)), ((), ())), preferred_element_type=jnp.float32)


def dot_cols(left, right):
    return lax.dot_general(left, right, (((1,), (1,)), ((), ())), preferred_element_type=jnp.float32)


def head_of(matrix, head):
    first = head * HEAD_SIZE
    if first + LANES <= matrix.shape[1]:
        return matrix[:, first : first + LANES]
    kept = matrix[:, first : first + HEAD_SIZE]
    return jnp.concatenate([kept, jnp.zeros((kept.shape[0], LANES - HEAD_SIZE), kept.dtype)], axis=1)


def half_turn(padded):
    lane = lax.broadcasted_iota(jnp.int32, padded.shape, 1)
    half = HEAD_SIZE // 2
    return jnp.where(lane < half, pltpu.roll(padded, LANES - half, 1), pltpu.roll(padded, half, 1))


def qkv_kernel(heads, keys, width, x_ref, gain_ref, weight_ref, cos_ref, sin_ref, normed_ref, q_ref, k_ref, v_ref):
    x = x_ref[...].astype(jnp.float32)
    scale = lax.rsqrt(jnp.mean(x * x, axis=1, keepdims=True) + eps)
    normed = (x * scale * gain_ref[...]).astype(jnp.bfloat16)
    normed_ref[...] = normed
    rows = jnp.dot(normed, weight_ref[:, :width], preferred_element_type=jnp.float32)
    cosine, sine = cos_ref[...], sin_ref[...]
    inside = lax.broadcasted_iota(jnp.int32, cosine.shape, 1) < HEAD_SIZE
    for i in range(heads + keys):
        v = head_of(rows, i)
        turned = (v * cosine + half_turn(v) * sine).astype(jnp.bfloat16)
        if i < heads:
            q_ref[:, i * LANES : (i + 1) * LANES] = turned
        else:
            k_ref[:, (i - heads) * LANES : (i - heads + 1) * LANES] = turned
    for i in range(keys):
        v = head_of(rows, heads + keys + i)
        v_ref[:, i * LANES : (i + 1) * LANES] = jnp.where(inside, v, 0.0).astype(jnp.bfloat16)


def qkv_call(x, gain, weight, cosine, sine, heads, keys, used):
    total, width = x.shape
    block = 256
    bf = jnp.bfloat16
    row = lambda n: pl.BlockSpec((block, n), lambda i: (i, 0))
    whole = lambda a: pl.BlockSpec(a.shape, lambda i: (0, 0))
    return pl.pallas_call(
        functools.partial(qkv_kernel, heads, keys, used),
        grid=(total // block,),
        in_specs=[row(width), whole(gain), whole(weight), row(LANES), row(LANES)],
        out_specs=[row(width), row(heads * LANES), row(keys * LANES), row(keys * LANES)],
        out_shape=[
            jax.ShapeDtypeStruct((total, width), bf),
            jax.ShapeDtypeStruct((total, heads * LANES), bf),
            jax.ShapeDtypeStruct((total, keys * LANES), bf),
            jax.ShapeDtypeStruct((total, keys * LANES), bf),
        ],
        compiler_params=pltpu.CompilerParams(vmem_limit_bytes=48 * 2**20),
        cost_estimate=pl.CostEstimate(
            flops=96 * 10**9, bytes_accessed=0, transcendentals=0
        ),
    )(x, gain, weight, cosine, sine)


def attend_kernel(heads, keys, block, q_ref, k_ref, v_ref, start_ref, *refs):
    mixed_ref, lse_ref, bias_ref = refs[-3:]
    total = q_ref.shape[0]
    group = heads // keys
    factor = HEAD_SIZE**-0.5 * log2e
    for i in range(total // block):
        first, stop = i * block, (i + 1) * block
        column = lax.broadcasted_iota(jnp.int32, (block, stop), 1)
        row = lax.broadcasted_iota(jnp.int32, (block, stop), 0) + first
        good = (column >= start_ref[first:stop, :]) & (column <= row)
        bias_ref[:, :stop] = jnp.where(good, 0.0, -1e30)
        for head in range(heads):
            lanes = slice(head * LANES, (head + 1) * LANES)
            key = slice(head // group * LANES, (head // group + 1) * LANES)
            scores = dot_cols(q_ref[first:stop, lanes], k_ref[:stop, key]) * factor + bias_ref[:, :stop]
            top = jnp.max(scores, axis=1, keepdims=True)
            weights = jnp.exp2(scores - top)
            summed = jnp.sum(weights, axis=1, keepdims=True)
            mixed = jnp.dot(
                weights.astype(jnp.bfloat16), v_ref[:stop, key], preferred_element_type=jnp.float32
            ) / summed
            mixed_ref[first:stop, head * HEAD_SIZE : (head + 1) * HEAD_SIZE] = mixed[:, :HEAD_SIZE].astype(
                jnp.bfloat16
            )
            lse_ref[first:stop, head : head + 1] = top + jnp.log2(summed)


def attend_call(q, k, v, start, *when):
    block = 256
    total = q.shape[0]
    heads, keys = q.shape[1] // LANES, k.shape[1] // LANES
    return pl.pallas_call(
        functools.partial(attend_kernel, heads, keys, block),
        in_specs=[pl.BlockSpec(memory_space=pltpu.VMEM)] * 4
        + [pl.BlockSpec(memory_space=pl.ANY)] * len(when),
        out_shape=[
            jax.ShapeDtypeStruct((total, heads * HEAD_SIZE), jnp.bfloat16),
            jax.ShapeDtypeStruct((total, heads), jnp.float32),
        ],
        scratch_shapes=[pltpu.VMEM((block, total), jnp.float32)],
        compiler_params=pltpu.CompilerParams(vmem_limit_bytes=56 * 2**20),
        cost_estimate=pl.CostEstimate(
            flops=112 * 10**9, bytes_accessed=0, transcendentals=0
        ),
    )(q, k, v, start, *when)


def attend_back_kernel(
    heads, keys, block, q_ref, k_ref, v_ref, grad_ref, lse_ref, start_ref, cos_ref, sin_ref, *refs
):
    out_ref, bias_ref, dk_ref, dv_ref = refs[-4:]
    total = q_ref.shape[0]
    group = heads // keys
    scale = HEAD_SIZE**-0.5
    factor = scale * log2e
    low = jnp.bfloat16
    dk_ref[...] = jnp.zeros_like(dk_ref)
    dv_ref[...] = jnp.zeros_like(dv_ref)
    inside = lax.broadcasted_iota(jnp.int32, (block, LANES), 1) < HEAD_SIZE
    half = HEAD_SIZE // 2

    def turned_back(w, rows):
        w = w.astype(low).astype(jnp.float32)
        scaled = w * sin_ref[rows, :]
        lane = lax.broadcasted_iota(jnp.int32, w.shape, 1)
        moved = jnp.where(lane < half, pltpu.roll(scaled, LANES - half, 1), pltpu.roll(scaled, half, 1))
        return (w * cos_ref[rows, :] + moved).astype(low)

    for i in range(total // block):
        first, stop = i * block, (i + 1) * block
        rows = slice(first, stop)
        key_place = lax.broadcasted_iota(jnp.int32, (stop, block), 0)
        place = lax.broadcasted_iota(jnp.int32, (stop, block), 1) + first
        good = (key_place >= start_ref[:, rows]) & (key_place <= place)
        bias_ref[:stop, :] = jnp.where(good, 0.0, -1e30)
        grads = grad_ref[rows, :].astype(jnp.float32)
        for head in range(heads):
            lanes = slice(head * LANES, (head + 1) * LANES)
            key = slice(head // group * LANES, (head // group + 1) * LANES)
            query = q_ref[rows, lanes]
            grad = jnp.where(inside, head_of(grads, head), 0.0).astype(low)
            scores = dot_cols(k_ref[:stop, key], query) * factor + bias_ref[:stop, :]
            probs = jnp.exp2(scores - lse_ref[head : head + 1, rows])
            dv_ref[:stop, key] += jnp.dot(probs.astype(low), grad, preferred_element_type=jnp.float32)
            d_probs = dot_cols(v_ref[:stop, key], grad)
            delta = jnp.sum(probs * d_probs, axis=0, keepdims=True)
            d_scores = (probs * (d_probs - delta)).astype(low)
            dk_ref[:stop, key] += jnp.dot(d_scores, query, preferred_element_type=jnp.float32)
            d_query = dot_rows(d_scores, k_ref[:stop, key]) * scale
            out_ref[rows, head * HEAD_SIZE : (head + 1) * HEAD_SIZE] = turned_back(d_query, rows)[:, :HEAD_SIZE]
    for i in range(total // block):
        rows = slice(i * block, (i + 1) * block)
        for j in range(keys):
            lanes = slice(j * LANES, (j + 1) * LANES)
            at = (heads + j) * HEAD_SIZE
            out_ref[rows, at : at + HEAD_SIZE] = turned_back(dk_ref[rows, lanes] * scale, rows)[:, :HEAD_SIZE]
            at = (heads + keys + j) * HEAD_SIZE
            out_ref[rows, at : at + HEAD_SIZE] = dv_ref[rows, lanes][:, :HEAD_SIZE].astype(low)


def attend_back_call(q, k, v, grad, lse_rows, start_row, cosine, sine_back, *when):
    block = 256
    total = q.shape[0]
    heads, keys = q.shape[1] // LANES, k.shape[1] // LANES
    return pl.pallas_call(
        functools.partial(attend_back_kernel, heads, keys, block),
        in_specs=[pl.BlockSpec(memory_space=pltpu.VMEM)] * 8
        + [pl.BlockSpec(memory_space=pl.ANY)] * len(when),
        out_shape=jax.ShapeDtypeStruct((total, (heads + 2 * keys) * HEAD_SIZE), jnp.bfloat16),
        scratch_shapes=[
            pltpu.VMEM((total, block), jnp.float32),
            pltpu.VMEM((total, keys * LANES), jnp.float32),
            pltpu.VMEM((total, keys * LANES), jnp.float32),
        ],
        compiler_params=pltpu.CompilerParams(vmem_limit_bytes=56 * 2**20),
        cost_estimate=pl.CostEstimate(
            flops=100 * 10**9, bytes_accessed=0, transcendentals=0
        ),
    )(q, k, v, grad, lse_rows, start_row, cosine, sine_back, *when)

def gate_up_kernel(x_ref, gate_weight_ref, up_weight_ref, active_ref, gate_ref, up_ref):
    x = x_ref[...]
    gate = jnp.dot(x, gate_weight_ref[...], preferred_element_type=jnp.float32)
    upward = jnp.dot(x, up_weight_ref[...], preferred_element_type=jnp.float32)
    active_ref[...] = (gate / (1.0 + jnp.exp(-gate)) * upward).astype(jnp.bfloat16)
    gate_ref[...] = gate.astype(jnp.bfloat16)
    up_ref[...] = upward.astype(jnp.bfloat16)


def unit_block(units):
    return 256 if units % 256 == 0 else 128


def gate_up_call(x, weights):
    total, width = x.shape
    units = weights.shape[1] // 2
    block = unit_block(units)
    count = units // block
    out = pl.BlockSpec((total, block), lambda j: (0, j))
    return pl.pallas_call(
        gate_up_kernel,
        grid=(count,),
        in_specs=[
            pl.BlockSpec((total, width), lambda j: (0, 0)),
            pl.BlockSpec((width, block), lambda j: (0, j)),
            pl.BlockSpec((width, block), lambda j: (0, j + count)),
        ],
        out_specs=[out] * 3,
        out_shape=[jax.ShapeDtypeStruct((total, units), jnp.bfloat16)] * 3,
        compiler_params=pltpu.CompilerParams(vmem_limit_bytes=56 * 2**20),
        cost_estimate=pl.CostEstimate(
            flops=148 * 10**9, bytes_accessed=0, transcendentals=0
        ),
    )(x, weights, weights)


def unit_back_kernel(incoming_ref, down_ref, gate_ref, up_ref, *refs):
    d_gate_ref, d_up_ref = refs[-2:]
    d_active = dot_cols(incoming_ref[...], down_ref[...])
    gate = gate_ref[...].astype(jnp.float32)
    upward = up_ref[...].astype(jnp.float32)
    logistic = 1.0 / (1.0 + jnp.exp(-gate))
    d_gate_ref[...] = (d_active * upward * logistic * (1.0 + gate * (1.0 - logistic))).astype(jnp.bfloat16)
    d_up_ref[...] = (d_active * gate * logistic).astype(jnp.bfloat16)


def unit_back_call(incoming, down, gate, up, *when):
    total, width = incoming.shape
    units = down.shape[0]
    block = unit_block(units)
    column = pl.BlockSpec((total, block), lambda j: (0, j))
    return pl.pallas_call(
        unit_back_kernel,
        grid=(units // block,),
        in_specs=[
            pl.BlockSpec((total, width), lambda j: (0, 0)),
            pl.BlockSpec((block, width), lambda j: (j, 0)),
            column,
            column,
        ]
        + [pl.BlockSpec(memory_space=pl.ANY)] * len(when),
        out_specs=[column] * 2,
        out_shape=[jax.ShapeDtypeStruct((total, units), jnp.bfloat16)] * 2,
        compiler_params=pltpu.CompilerParams(vmem_limit_bytes=56 * 2**20),
        cost_estimate=pl.CostEstimate(
            flops=104 * 10**9, bytes_accessed=0, transcendentals=0
        ),
    )(incoming, down, gate, up, *when)


def norm_back(d_normed, x, gain):
    scale = lax.rsqrt(jnp.mean(x * x, axis=1, keepdims=True) + eps)
    grad_gain = jnp.sum(d_normed * (x * scale), axis=0, keepdims=True)
    scaled = d_normed * gain
    inner = jnp.mean(scaled * x, axis=1, keepdims=True)
    return scale * scaled - x * (scale * scale * scale * inner), grad_gain


def add_up(ref, value):
    @pl.when(pl.program_id(0) == 0)
    def _():
        ref[...] = jnp.zeros_like(ref)

    ref[...] += value


def mlp_back_kernel(d_gate_ref, d_up_ref, weight_ref, x_ref, gain_ref, *refs):
    out_ref, grad_ref = refs[-2:]
    units = d_gate_ref.shape[1]
    d_normed = dot_cols(d_gate_ref[...], weight_ref[:, :units]) + dot_cols(
        d_up_ref[...], weight_ref[:, units:]
    )
    back, grad_gain = norm_back(d_normed, x_ref[...].astype(jnp.float32), gain_ref[...])
    parts, _, share = out_ref.shape
    for i in range(parts):
        out_ref[i] = back[:, i * share : (i + 1) * share].astype(jnp.bfloat16)
    add_up(grad_ref, grad_gain)


def mlp_back_call(d_gate, d_up, weights, x, gain, parts, *when):
    total, units = d_gate.shape
    width = x.shape[1]
    share = width // parts
    block = 512
    row = lambda n: pl.BlockSpec((block, n), lambda i: (i, 0))
    whole = lambda a: pl.BlockSpec(a.shape, lambda i: (0, 0), pipeline_mode=pl.Buffered(1))
    return pl.pallas_call(
        mlp_back_kernel,
        grid=(total // block,),
        in_specs=[row(units), row(units), whole(weights), row(width), whole(gain)]
        + [pl.BlockSpec(memory_space=pl.ANY)] * len(when),
        out_specs=[
            pl.BlockSpec((parts, block, share), lambda i: (0, i, 0)),
            pl.BlockSpec((1, width), lambda i: (0, 0)),
        ],
        out_shape=[
            jax.ShapeDtypeStruct((parts, total, share), jnp.bfloat16),
            jax.ShapeDtypeStruct((1, width), jnp.float32),
        ],
        compiler_params=pltpu.CompilerParams(vmem_limit_bytes=60 * 2**20),
        cost_estimate=pl.CostEstimate(
            flops=176 * 10**9, bytes_accessed=0, transcendentals=0
        ),
    )(d_gate, d_up, weights, x, gain, *when)


def attend_norm_kernel(parts, place_ref, d_qkv_ref, weight_ref, x_ref, gain_ref, own_ref, *refs):
    out_ref, grad_ref = refs[-2:]
    d_normed = dot_cols(d_qkv_ref[...], weight_ref[:, : d_qkv_ref.shape[1]])
    back, grad_gain = norm_back(d_normed, x_ref[...].astype(jnp.float32), gain_ref[...])
    out_ref[...] = back.astype(jnp.bfloat16)
    share = own_ref.shape[1]
    for place in range(parts):

        @pl.when(place_ref[0] == place)
        def _():
            lanes = slice(place * share, (place + 1) * share)
            out_ref[:, lanes] = (back[:, lanes] + own_ref[...]).astype(jnp.bfloat16)

    add_up(grad_ref, grad_gain)


def attend_norm_call(place, d_qkv, weights, x, gain, own, parts, *when):
    total, width = x.shape
    block = 256
    row = lambda n: pl.BlockSpec((block, n), lambda i: (i, 0))
    whole = lambda a: pl.BlockSpec(a.shape, lambda i: (0, 0), pipeline_mode=pl.Buffered(1))
    return pl.pallas_call(
        functools.partial(attend_norm_kernel, parts),
        grid=(total // block,),
        in_specs=[
            pl.BlockSpec(memory_space=pltpu.SMEM),
            row(d_qkv.shape[1]),
            whole(weights),
            row(width),
            whole(gain),
            row(own.shape[1]),
        ]
        + [pl.BlockSpec(memory_space=pl.ANY)] * len(when),
        out_specs=[row(width), pl.BlockSpec((1, width), lambda i: (0, 0))],
        out_shape=[
            jax.ShapeDtypeStruct((total, width), jnp.bfloat16),
            jax.ShapeDtypeStruct((1, width), jnp.float32),
        ],
        compiler_params=pltpu.CompilerParams(vmem_limit_bytes=56 * 2**20),
        cost_estimate=pl.CostEstimate(
            flops=80 * 10**9, bytes_accessed=0, transcendentals=0
        ),
    )(place, d_qkv, weights, x, gain, own, *when)


def out_back_kernel(d_ref, weight_ref, *refs):
    refs[-1][0] = dot_cols(d_ref[...], weight_ref[...]).astype(jnp.bfloat16)


def out_back_call(d_branch, weights, parts, *when):
    total, share = d_branch.shape
    rows = weights.shape[0] // parts
    return pl.pallas_call(
        out_back_kernel,
        grid=(parts,),
        in_specs=[
            pl.BlockSpec((total, share), lambda i: (0, 0)),
            pl.BlockSpec((rows, share), lambda i: (i, 0)),
        ]
        + [pl.BlockSpec(memory_space=pl.ANY)] * len(when),
        out_specs=pl.BlockSpec((1, total, rows), lambda i: (i, 0, 0)),
        out_shape=jax.ShapeDtypeStruct((parts, total, rows), jnp.bfloat16),
        compiler_params=pltpu.CompilerParams(vmem_limit_bytes=32 * 2**20),
        cost_estimate=pl.CostEstimate(
            flops=32 * 10**9, bytes_accessed=0, transcendentals=0
        ),
    )(d_branch, weights, *when)


def norm_kernel(stack_ref, gain_ref, x_ref, normed_ref):
    parts, _, share = stack_ref.shape
    squares = 0.0
    for i in range(parts):
        piece = stack_ref[i].astype(jnp.float32)
        squares = squares + jnp.sum(piece * piece, axis=1, keepdims=True)
    scale = lax.rsqrt(squares / (parts * share) + eps)
    for i in range(parts):
        lanes = slice(i * share, (i + 1) * share)
        x_ref[:, lanes] = stack_ref[i]
        normed = stack_ref[i].astype(jnp.float32) * scale * gain_ref[:, lanes]
        normed_ref[:, lanes] = normed.astype(jnp.bfloat16)


def norm_call(stack, gain):
    parts, total, share = stack.shape
    block = 256
    row = pl.BlockSpec((block, parts * share), lambda i: (i, 0))
    return pl.pallas_call(
        norm_kernel,
        grid=(total // block,),
        in_specs=[
            pl.BlockSpec((parts, block, share), lambda i: (0, i, 0)),
            pl.BlockSpec((1, parts * share), lambda i: (0, 0)),
        ],
        out_specs=[row, row],
        out_shape=[jax.ShapeDtypeStruct((total, parts * share), jnp.bfloat16)] * 2,
        compiler_params=pltpu.CompilerParams(vmem_limit_bytes=32 * 2**20),
        cost_estimate=pl.CostEstimate(flops=32 * 10**9, bytes_accessed=0, transcendentals=0),
    )(stack, gain)


def out_kernel(stack_ref, weight_ref, x_ref, out_ref):
    parts, _, depth = stack_ref.shape
    total = x_ref[...].astype(jnp.float32)
    for i in range(parts):
        total = total + jnp.dot(
            stack_ref[i], weight_ref[i * depth : (i + 1) * depth, :], preferred_element_type=jnp.float32
        )
    out_ref[...] = total.astype(jnp.bfloat16)


def out_call(stack, weight, x):
    parts, total, depth = stack.shape
    columns = weight.shape[1]
    block = 512
    row = pl.BlockSpec((block, columns), lambda i: (i, 0))
    return pl.pallas_call(
        out_kernel,
        grid=(total // block,),
        in_specs=[
            pl.BlockSpec((parts, block, depth), lambda i: (0, i, 0)),
            pl.BlockSpec(weight.shape, lambda i: (0, 0)),
            row,
        ],
        out_specs=row,
        out_shape=jax.ShapeDtypeStruct((total, columns), jnp.bfloat16),
        compiler_params=pltpu.CompilerParams(vmem_limit_bytes=40 * 2**20),
        cost_estimate=pl.CostEstimate(flops=36 * 10**9, bytes_accessed=0, transcendentals=0),
    )(stack, weight, x)


def stack_rows_kernel(left_ref, right_ref, *refs):
    refs[-1][...] = dot_rows(left_ref[0], right_ref[...]).astype(jnp.bfloat16)


def stack_rows_call(stack, right, *when):
    parts, total, rows = stack.shape
    columns = right.shape[1]
    return pl.pallas_call(
        stack_rows_kernel,
        grid=(parts,),
        in_specs=[
            pl.BlockSpec((1, total, rows), lambda i: (i, 0, 0)),
            pl.BlockSpec((total, columns), lambda i: (0, 0)),
        ]
        + [pl.BlockSpec(memory_space=pl.ANY)] * len(when),
        out_specs=pl.BlockSpec((rows, columns), lambda i: (i, 0)),
        out_shape=jax.ShapeDtypeStruct((parts * rows, columns), jnp.bfloat16),
        compiler_params=pltpu.CompilerParams(vmem_limit_bytes=40 * 2**20),
        cost_estimate=pl.CostEstimate(flops=0 * 10**9, bytes_accessed=0, transcendentals=0),
    )(stack, right, *when)


def rows_kernel(left_ref, right_ref, *refs):
    refs[-1][...] = dot_rows(left_ref[...], right_ref[...]).astype(jnp.bfloat16)


def rows_call(left, right, *when):
    total, rows = left.shape
    columns = right.shape[1]
    block = 256 if columns % 256 == 0 else 128
    return pl.pallas_call(
        rows_kernel,
        grid=(columns // block,),
        in_specs=[
            pl.BlockSpec((total, rows), lambda j: (0, 0)),
            pl.BlockSpec((total, block), lambda j: (0, j)),
        ]
        + [pl.BlockSpec(memory_space=pl.ANY)] * len(when),
        out_specs=pl.BlockSpec((rows, block), lambda j: (0, j)),
        out_shape=jax.ShapeDtypeStruct((rows, columns), jnp.bfloat16),
        compiler_params=pltpu.CompilerParams(vmem_limit_bytes=56 * 2**20),
        cost_estimate=pl.CostEstimate(flops=0 if len(when) > 1 else 80 * 10**9, bytes_accessed=0, transcendentals=0),
    )(left, right, *when)


def product_kernel(left_ref, right_ref, *refs):
    refs[-1][...] = jnp.dot(left_ref[...], right_ref[...], preferred_element_type=jnp.float32).astype(
        jnp.bfloat16
    )


def product_call(left, right, *when):
    total, depth = left.shape
    columns = right.shape[1]
    block = 256 if columns % 256 == 0 else 128
    return pl.pallas_call(
        product_kernel,
        grid=(columns // block,),
        in_specs=[
            pl.BlockSpec((total, depth), lambda j: (0, 0)),
            pl.BlockSpec((depth, block), lambda j: (0, j)),
        ]
        + [pl.BlockSpec(memory_space=pl.ANY)] * len(when),
        out_specs=pl.BlockSpec((total, block), lambda j: (0, j)),
        out_shape=jax.ShapeDtypeStruct((total, columns), jnp.bfloat16),
        compiler_params=pltpu.CompilerParams(vmem_limit_bytes=56 * 2**20),
        cost_estimate=pl.CostEstimate(flops=80 * 10**9, bytes_accessed=0, transcendentals=0),
    )(left, right, *when)


def qkv_grad_kernel(normed_ref, d_qkv_ref, gain_ref, *refs):
    out_ref = refs[-1]
    columns = d_qkv_ref.shape[1]
    out_ref[:, :columns] = dot_rows(normed_ref[...], d_qkv_ref[...]).astype(jnp.bfloat16)
    rest = jnp.transpose(gain_ref[...])
    fill = out_ref.shape[1] - columns - rest.shape[1]
    if fill:
        rest = jnp.concatenate([rest, jnp.zeros((rest.shape[0], fill), rest.dtype)], axis=1)
    out_ref[:, columns:] = rest.astype(jnp.bfloat16)


def qkv_grad_call(normed, d_qkv, gain_grads, columns, *when):
    total, width = normed.shape
    block = 512
    return pl.pallas_call(
        qkv_grad_kernel,
        grid=(width // block,),
        in_specs=[
            pl.BlockSpec((total, block), lambda i: (0, i)),
            pl.BlockSpec(d_qkv.shape, lambda i: (0, 0)),
            pl.BlockSpec((gain_grads.shape[0], block), lambda i: (0, i)),
        ]
        + [pl.BlockSpec(memory_space=pl.ANY)] * len(when),
        out_specs=pl.BlockSpec((block, columns), lambda i: (i, 0)),
        out_shape=jax.ShapeDtypeStruct((width, columns), jnp.bfloat16),
        compiler_params=pltpu.CompilerParams(vmem_limit_bytes=48 * 2**20),
        cost_estimate=pl.CostEstimate(flops=48 * 10**9, bytes_accessed=0, transcendentals=0),
    )(normed, d_qkv, gain_grads, *when)


def pieces_sp(value, split, *hold):
    size = lax.axis_size("sp")
    columns = value.shape[1]
    if not split or size != 4 or columns % (2 * LANES):
        others = [(swap(value, turn),) for turn in range(1, size)]
        return [(value,)] + others, [piece for (piece,) in others], []
    half = columns // 2
    left, right = value[:, :half], value[:, half:]
    x_left, y_right = swap(left, 1), swap(right, 2)
    x_right, y_left = swap(right, 1), swap(left, 2)
    far_left, far_right = (after(v, *hold) if hold else v for v in (x_left, y_right))
    far_left, far_right = swap(far_left, 2), swap(far_right, 1)
    return (
        [(left, right), (x_left, x_right), (y_left, y_right), (far_left, far_right)],
        [x_left, y_right, x_right, y_left],
        [far_left, far_right],
    )


def spread_kernel(layout, count, chunks, outputs, place_ref, *refs):
    pieces, outs = refs[: count * chunks], refs[-outputs:]
    size = pieces[0].shape[1]
    for place in range(count):

        @pl.when(place_ref[0] == place)
        def _():
            for part in range(count):
                for first, width, out, at, step in layout:
                    goal = at + part * step
                    while width:
                        chunk, begin = divmod(first, size)
                        some = min(width, size - begin)
                        piece = pieces[(place ^ part) * chunks + chunk]
                        outs[out][:, goal : goal + some] = piece[:, begin : begin + some].astype(jnp.float32)
                        first, goal, width = first + some, goal + some, width - some


def spread_call(place, pieces, layout, widths, *when):
    count, chunks = len(pieces), len(pieces[0])
    rows, columns = pieces[0][0].shape
    block = rows // 5 if rows % 80 == 0 else rows
    return pl.pallas_call(
        functools.partial(spread_kernel, layout, count, chunks, len(widths)),
        grid=(rows // block,),
        in_specs=[pl.BlockSpec(memory_space=pltpu.SMEM)]
        + [pl.BlockSpec((block, columns), lambda i: (i, 0))] * (count * chunks)
        + [pl.BlockSpec(memory_space=pl.ANY)] * len(when),
        out_specs=[pl.BlockSpec((block, w), lambda i: (i, 0)) for w in widths],
        out_shape=[jax.ShapeDtypeStruct((rows, w), jnp.float32) for w in widths],
        compiler_params=pltpu.CompilerParams(vmem_limit_bytes=40 * 2**20),
        cost_estimate=pl.CostEstimate(
            flops=0, bytes_accessed=6 * count * chunks * rows * columns, transcendentals=0
        ),
    )(place, *[chunk for piece in pieces for chunk in piece], *when)


def stack_kernel(count, chunks, place_ref, *refs):
    out_ref = refs[-1]
    size = refs[0].shape[1]
    for turn in range(count):
        for chunk in range(chunks):
            value = refs[turn * chunks + chunk][...].astype(jnp.float32)
            out_ref[place_ref[0] ^ turn, :, chunk * size : (chunk + 1) * size] = value


def stack_call(place, pieces, *when):
    count, chunks = len(pieces), len(pieces[0])
    rows, columns = pieces[0][0].shape
    block = 32 if rows % 32 == 0 else rows
    return pl.pallas_call(
        functools.partial(stack_kernel, count, chunks),
        grid=(rows // block,),
        in_specs=[pl.BlockSpec(memory_space=pltpu.SMEM)]
        + [pl.BlockSpec((block, columns), lambda i: (i, 0))] * (count * chunks)
        + [pl.BlockSpec(memory_space=pl.ANY)] * len(when),
        out_specs=pl.BlockSpec((count, block, chunks * columns), lambda i: (0, i, 0)),
        out_shape=jax.ShapeDtypeStruct((count, rows, chunks * columns), jnp.float32),
        compiler_params=pltpu.CompilerParams(vmem_limit_bytes=40 * 2**20),
        cost_estimate=pl.CostEstimate(
            flops=0, bytes_accessed=6 * count * chunks * rows * columns, transcendentals=0
        ),
    )(place, *[chunk for piece in pieces for chunk in piece], *when).reshape(count * rows, chunks * columns)


def pass_kernel(*refs):
    pass


def after(value, *others):
    here = pl.BlockSpec(memory_space=pl.ANY)
    return pl.pallas_call(
        pass_kernel,
        in_specs=[here] * (1 + len(others)),
        out_specs=here,
        out_shape=jax.ShapeDtypeStruct(value.shape, value.dtype),
        input_output_aliases={0: 0},
        cost_estimate=pl.CostEstimate(flops=0, bytes_accessed=0, transcendentals=0),
    )(value, *others)


def pack_kernel(groups, parts, place_ref, gate_ref, up_ref, _, out_ref):
    rows, columns = gate_ref.shape
    share = columns // (groups * parts)
    for place in range(parts):

        @pl.when(place_ref[0] == place)
        def _():
            for i, ref in enumerate((gate_ref, up_ref)):
                for j in range(groups):
                    at = (i * groups + j) * share
                    begin = (j * parts + place) * share
                    out_ref[:, at : at + share] = ref[:, begin : begin + share]


def pack_call(place, gate, up, when, groups, parts):
    rows, columns = gate.shape
    block = rows // 5 if rows % 80 == 0 else rows
    spec = pl.BlockSpec((block, columns), lambda i: (i, 0))
    return pl.pallas_call(
        functools.partial(pack_kernel, groups, parts),
        grid=(rows // block,),
        in_specs=[
            pl.BlockSpec(memory_space=pltpu.SMEM),
            spec,
            spec,
            pl.BlockSpec(memory_space=pl.ANY),
        ],
        out_specs=pl.BlockSpec((block, 2 * columns // parts), lambda i: (i, 0)),
        out_shape=jax.ShapeDtypeStruct((rows, 2 * columns // parts), gate.dtype),
        compiler_params=pltpu.CompilerParams(vmem_limit_bytes=32 * 2**20),
        cost_estimate=pl.CostEstimate(flops=0, bytes_accessed=5 * rows * columns, transcendentals=0),
    )(place, gate, up, when)


def local(
    tokens,
    cotangent,
    attn_gain,
    w_query,
    key_weight,
    value_weight,
    w_out,
    mlp_gain,
    w_gate,
    w_up,
    w_down,
    positions,
    lengths,
    deal_slots,
):
    groups = lax.axis_size("fsdp")
    parts = lax.axis_size("sp")
    width = tokens.shape[-1]
    rows = tokens.shape[1]
    fsdp_place = lax.axis_index("fsdp")
    sp_place = lax.axis_index("sp")
    low = jnp.bfloat16
    wide = jnp.float32

    lanes = jnp.arange(groups, dtype=jnp.int32)
    own_row = deal_slots[fsdp_place, sp_place]
    target = own_row // groups
    pick_send = jnp.sum(jnp.where(target[None, :] == lanes[:, None], lanes[None, :], 0), axis=1)
    column = deal_slots[:, sp_place, :]
    arrived_slot = jnp.sum(jnp.where(column // groups == fsdp_place, column % groups, 0), axis=1)
    pick_place = jnp.sum(
        jnp.where(arrived_slot[None, :] == lanes[:, None], lanes[None, :], 0), axis=1
    )

    def picked(given):
        return rows_of(given.reshape(groups, -1, width), pick_send)

    def deal(blocks):
        return lax.all_to_all(blocks, "fsdp", split_axis=0, concat_axis=0, tiled=True)

    def in_place(came):
        return rows_of(came, pick_place).reshape(rows, width)

    def blocks_back(owned):
        return rows_of(owned.reshape(groups, -1, width), arrived_slot)

    def scatter_fsdp(matrix):
        return lax.psum_scatter(matrix, "fsdp", scatter_dimension=0, tiled=True)

    def column_share(weight):
        share = weight.shape[1] // parts
        return lax.dynamic_slice_in_dim(weight, sp_place * share, share, axis=1)

    def gather_fsdp(shard):
        return lax.all_gather(shard, "fsdp", axis=0, tiled=True)

    ff_rows = w_down.shape[0]
    ff_share = ff_rows // parts

    query_cols = w_query.shape[1] // parts
    key_cols = key_weight.shape[1] // parts
    qkv_cols = query_cols + 2 * key_cols
    extra = -qkv_cols % 128
    extra = extra if extra else 128
    gains = jnp.pad(jnp.stack([attn_gain, mlp_gain], axis=1), ((0, 0), (0, extra - 2)))
    place = sp_place.reshape(1)
    came_tokens = deal(picked(tokens))
    gate_up_shard = pack_call(place, w_gate, w_up, came_tokens, groups, parts)
    qkv_shard = jnp.concatenate(
        [column_share(w_query), column_share(key_weight), column_share(value_weight), gains], axis=1
    )
    came_incoming = deal(after(picked(cotangent), came_tokens))
    qkv_width = qkv_shard.shape[1]
    qkv_shard = jnp.concatenate([qkv_shard, column_share(w_out)], axis=1)
    qkv_all = gather_fsdp(after(qkv_shard, came_tokens))
    out_all = qkv_all[:, qkv_width:]
    gate_up_all = gather_fsdp(gate_up_shard)
    down_all = gather_fsdp(lax.dynamic_slice_in_dim(w_down, sp_place * ff_share, ff_share, axis=0))
    gain_one = qkv_all[:, qkv_cols].astype(wide)[None, :]
    gain_two = qkv_all[:, qkv_cols + 1].astype(wide)[None, :]

    group_inputs, passed = gather_sp(in_place(came_tokens))
    group_inputs = group_inputs.reshape(-1, width)
    group_positions = gather_small(after(positions.reshape(-1), passed[0])).reshape(-1)
    total = group_inputs.shape[0]

    cosine, sine = rotary_tables(group_positions)
    heads, keys = query_cols // HEAD_SIZE, key_cols // HEAD_SIZE
    normed, query_low, key_low, value_low = qkv_call(
        group_inputs, gain_one, qkv_all, cosine, sine, heads, keys, qkv_width
    )
    sizes = lengths.reshape(-1)
    ends = jnp.cumsum(sizes)
    places = jnp.arange(total, dtype=jnp.int32)
    start = jnp.sum(jnp.where(places[:, None] >= ends[None, :], sizes[None, :], 0), axis=1)
    own_mixed, logs = attend_call(query_low, key_low, value_low, start[:, None])

    share = width // parts

    def own_columns(matrix):
        return lax.dynamic_slice_in_dim(matrix, sp_place * share, share, axis=1)

    mixed, _ = gather_sp(own_mixed)
    own_hidden = out_call(mixed, out_all, own_columns(group_inputs))
    hidden_low, normed_two = norm_call(gather_sp(own_hidden)[0], gain_two)

    active_low, gate, upward = gate_up_call(normed_two, gate_up_all)
    own_incoming = after(in_place(after(came_incoming, own_hidden)), normed_two)
    group_incoming = gather_sp(own_incoming, active_low)[0].reshape(-1, width)
    result_part = product_call(active_low, down_all)
    grad_down = rows_call(active_low, group_incoming, result_part)
    d_gate, d_up = unit_back_call(group_incoming, down_all, gate, upward, grad_down)
    grad_gate = rows_call(normed_two, d_gate)
    result_sum, sums_result, last_result, _ = scatter_sp(
        result_part.reshape(parts, rows, width), lambda first: (grad_gate,), False
    )
    own_hidden_rows = lax.dynamic_slice_in_dim(hidden_low, sp_place * rows, rows, axis=0)
    blocks_result = blocks_back((own_hidden_rows.astype(wide) + result_sum).astype(low))

    back_two, grad_gain_two = mlp_back_call(
        d_gate, d_up, gate_up_all, hidden_low, gain_two, parts, grad_gate, *sums_result
    )
    from_others, _, _, (grad_up,) = scatter_sp(
        after(back_two, *last_result), lambda first: (rows_call(normed_two, d_up, *first),)
    )
    gone_result = deal(blocks_result)
    own_d_hidden = own_columns(group_incoming).astype(wide) + from_others
    d_branch = own_d_hidden.astype(low)
    d_mixed, _, _, (grad_out,) = scatter_sp(
        out_back_call(d_branch, out_all, parts), lambda first: (stack_rows_call(mixed, d_branch, *first),)
    )
    d_mixed = d_mixed.astype(low)

    down_sum = after(scatter_fsdp(grad_down), d_mixed)
    down_pieces, down_first, _ = pieces_sp(down_sum, False)
    gate_sum = after(scatter_fsdp(grad_gate), d_mixed, down_sum)
    gate_pieces, gate_first, _ = pieces_sp(gate_sum, False)
    d_qkv = attend_back_call(
        query_low, key_low, value_low, d_mixed, logs.T, start[None, :], cosine, sine
    )
    back_one, grad_gain_one = attend_norm_call(
        place, d_qkv, qkv_all, group_inputs, gain_one, own_d_hidden, parts, *down_first, *gate_first[:2]
    )
    gain_grads = jnp.concatenate(
        [grad_gain_one, grad_gain_two, jnp.zeros((6, width), wide)], axis=0
    )
    layer_out = rows_of(gone_result, target).reshape(tokens.shape)

    grad_qkv = qkv_grad_call(normed, d_qkv, gain_grads, qkv_width, *gate_first[2:])
    hidden_layout = [
        (j * ff_share, ff_share, 0, j * parts * ff_share, ff_share) for j in range(groups)
    ]

    def beside(first):
        gate_shard = spread_call(place, gate_pieces, hidden_layout, [w_gate.shape[1]], *first)[0]
        return stack_call(place, down_pieces, *first), gate_shard, layer_out

    d_inputs, _, _, (down_shard, gate_shard, layer_out) = scatter_sp(
        back_one.reshape(parts, rows, width), beside
    )
    gone_grad = deal(blocks_back(d_inputs.astype(low)))
    input_grad = rows_of(gone_grad, target).reshape(tokens.shape)

    up_pieces, up_first, _ = pieces_sp(scatter_fsdp(after(grad_up, d_branch)), True)
    out_sum = after(scatter_fsdp(after(grad_out, d_mixed)), *up_first[:2])
    out_pieces = pieces_sp(out_sum, False)[0]
    qkv_pieces = pieces_sp(after(scatter_fsdp(grad_qkv), out_sum), True)[0]
    (up_shard,) = spread_call(place, up_pieces, hidden_layout, [w_up.shape[1]])
    (out_shard,) = spread_call(place, out_pieces, [(0, share, 0, 0, share)], [width])
    qkv_layout = [
        (0, query_cols, 0, 0, query_cols),
        (query_cols, key_cols, 1, 0, key_cols),
        (query_cols + key_cols, key_cols, 2, 0, key_cols),
        (qkv_cols, 2, 3, 0, 2),
    ]
    query_shard, key_shard, value_shard, gain_parts = spread_call(
        place,
        qkv_pieces,
        qkv_layout,
        [w_query.shape[1], key_weight.shape[1], value_weight.shape[1], 2 * parts],
    )
    gain_shards = jnp.sum(gain_parts.reshape(-1, parts, 2), axis=1)
    return (
        layer_out,
        input_grad,
        gain_shards[:, 0],
        query_shard,
        key_shard,
        value_shard,
        out_shard,
        gain_shards[:, 1],
        gate_shard,
        up_shard,
        down_shard,
    )


def solution(mesh):
    placed = (
        P("fsdp", "sp", None),
        P("fsdp", "sp", None),
        P("fsdp"),
        P("fsdp", None),
        P("fsdp", None),
        P("fsdp", None),
        P("fsdp", None),
        P("fsdp"),
        P("fsdp", None),
        P("fsdp", None),
        P("fsdp", None),
        P("fsdp", "sp"),
        P("fsdp", None),
        P(),
    )
    return jax.shard_map(
        local,
        mesh=mesh,
        in_specs=placed,
        out_specs=(
            P("fsdp", "sp", None),
            P("fsdp", "sp", None),
            P("fsdp"),
            P("fsdp", None),
            P("fsdp", None),
            P("fsdp", None),
            P("fsdp", None),
            P("fsdp"),
            P("fsdp", None),
            P("fsdp", None),
            P("fsdp", None),
        ),
        check_vma=False,
    )
```
